256 devices in a mesh: dp: 32 (over y_lo, z, core), fsdp: 8 (over x, y_hi).
Axes of the slice: x: 4, y: 4 (y_hi: 2, y_lo: 2; y = y_hi * 2 + y_lo), z: 8, core: 2. Of those that a mesh axis runs over, the one named last changes fastest.
Arguments:
- features: bfloat16 [1024, 8, 8, 3072], P(('dp', 'fsdp')), may hold values from -8 to 8
- text_embed: bfloat16 [1024, 1152], P(('dp', 'fsdp')), may hold values from -1 to 1
- img_ids: int32 [1024], P(('dp', 'fsdp')), may hold values from 0 to 63
- txt_ids: int32 [1024], P(('dp', 'fsdp')), may hold values from 0 to 63
- kernel: float32 [7, 7, 3072], replicated, may hold values from -0.875 to 0.875
- norm_gain: float32 [3072], replicated, may hold values from 0.1 to 1.9
- head_gain: float32 [3072], replicated, may hold values from 0.1 to 1.9
- projection: bfloat16 [3072, 1152], P('fsdp'), may hold values from -0.109375 to 0.109375
- logit_scale: float32 [1], replicated, may hold values from 3 to 6
- logit_bias: float32 [1], replicated, may hold values from -4 to -1
Outputs:
- grad_features: bfloat16 [1024, 8, 8, 3072], P(('dp', 'fsdp'))
- grad_text: float32 [1024, 1152], P(('dp', 'fsdp'))
- grad_proj: float32 [3072, 1152], P('fsdp')
The draws below stay inside these ranges and needn't reach their ends.
All inputs are finite; a program needn't handle non-finite values.
Results may differ from the reference program's by a relative error of at most 0.007.
Values may be sent and summed in bfloat16 or wider, within the bound.
No kernel may reach another device: no remote copies, remote signals or barrier semaphores. Data moves between devices by JAX's collectives and lax.ppermute only.
A program may use at most 128 MiB of HBM per device.

```python
import jax
import jax.numpy as jnp
from jax import lax

C = 3072
E = 1152
KER = 7
GRID = 8
B_DEV = 4
TOTAL = 1024


def draw_features(key, part):
    base_key, chan_key, cell_key = jax.random.split(key, 3)
    values_drawn = jax.random.normal(base_key, (TOTAL, GRID, GRID, C), jnp.float32)
    channel = jnp.exp(jax.random.uniform(chan_key, (C,), jnp.float32, jnp.log(0.3), jnp.log(3.0)))
    cell_scale = jnp.exp(jax.random.uniform(cell_key, (TOTAL, GRID, GRID, 1), jnp.float32, jnp.log(0.3), jnp.log(3.0)))
    return jnp.clip(values_drawn * channel * cell_scale, -8.0, 8.0).astype(jnp.bfloat16)


def draw_text_embed(key, part):
    base_key, row_key, col_key = jax.random.split(key, 3)
    values_drawn = jax.random.normal(base_key, (TOTAL, E), jnp.float32)
    row_scale = jnp.exp(jax.random.uniform(row_key, (TOTAL, 1), jnp.float32, 0.0, jnp.log(10.0)))
    col_scale = jnp.exp(jax.random.uniform(col_key, (E,), jnp.float32, jnp.log(0.3), jnp.log(3.0)))
    return jnp.clip(0.01 * values_drawn * row_scale * col_scale, -1.0, 1.0).astype(jnp.bfloat16)


def touch_ends(array, own_key, smallest, top_value):
    shape = array.shape
    spot = [jax.random.randint(jax.random.fold_in(own_key, axis), (), 0, shape[axis]) for axis in range(len(shape))]
    array = array.at[tuple(spot)].set(smallest)
    longest = shape.index(max(shape))
    spot[longest] = (spot[longest] + 1) % shape[longest]
    return array.at[tuple(spot)].set(top_value)


def steps_of(key, shape, shards, low, largest):
    gain = 1.0
    for axis_at, parts in shards:
        draws = jax.random.uniform(jax.random.fold_in(jax.random.fold_in(key, 6), axis_at), (parts,), jnp.float32, low / len(shards), largest / len(shards))
        gain = gain * jnp.repeat(jnp.exp(draws), shape[axis_at] // parts).reshape((-1,) + (1,) * (len(shape) - 1 - axis_at))
    return gain


def noise(key, shape, scale, most, cuts=(), dtype=jnp.bfloat16):
    drawn = scale * jax.random.normal(key, shape, jnp.float32)
    if cuts:
        drawn = drawn * steps_of(key, shape, cuts, -0.22, 0.18)
    return jnp.clip(drawn, -most, most).astype(dtype)


def setup_inputs(seed: int = 0) -> dict:
    seeds = jax.random.split(jax.random.key(seed), 11)
    return {
        "features": draw_features(jax.random.fold_in(seeds[10], 71), 0),
        "text_embed": draw_text_embed(jax.random.fold_in(seeds[10], 71), 0),
        "img_ids": touch_ends(jax.random.randint(seeds[2], (TOTAL,), 0, TOTAL // 16), jax.random.fold_in(seeds[2], 1), 0, (TOTAL // 16) - 1).astype(jnp.int32),
        "txt_ids": touch_ends(jax.random.randint(seeds[3], (TOTAL,), 0, TOTAL // 16), jax.random.fold_in(seeds[3], 1), 0, (TOTAL // 16) - 1).astype(jnp.int32),
        "kernel": noise(seeds[4], (KER, KER, C), (KER * KER) ** -0.5, 0.875, (), jnp.float32),
        "norm_gain": jnp.clip(1.0 + 0.18 * jax.random.normal(seeds[5], (C,), jnp.float32), 0.1, 1.9),
        "head_gain": jnp.clip(1.0 + 0.18 * jax.random.normal(seeds[6], (C,), jnp.float32), 0.1, 1.9),
        "projection": noise(seeds[7], (C, E), C ** -0.5, 0.109375, ((0, 8),)),
        "logit_scale": jnp.clip(jax.random.uniform(seeds[8], (1,), jnp.float32, 3.0, 6.0), 3.0, 6.0),
        "logit_bias": jnp.clip(jax.random.uniform(seeds[9], (1,), jnp.float32, -4.0, -1.0), -4.0, -1.0),
    }


EPSILON = 1e-06

def depthwise(widened, kernel):
    margin = kernel.shape[0] // 2
    extent = widened.shape[1]
    padded = jnp.pad(widened, ((0, 0), (margin, margin), (margin, margin), (0, 0)))
    filtered = jnp.zeros_like(widened)
    for row_tap in range(kernel.shape[0]):
        for col_tap in range(kernel.shape[1]):
            filtered = filtered + padded[:, row_tap:row_tap + extent, col_tap:col_tap + extent, :] * kernel[row_tap, col_tap]
    return filtered

def block_pool(widened, kernel, norm_gain):
    filtered = depthwise(widened, kernel)
    average = lax.optimization_barrier(jnp.mean(filtered, axis=-1, keepdims=True))
    centred = filtered - average
    spread = lax.optimization_barrier(jnp.mean(centred * centred, axis=-1, keepdims=True))
    normed = centred * lax.rsqrt(spread + EPSILON) * norm_gain
    return lax.optimization_barrier(jnp.mean(widened + normed, axis=(1, 2)))

def head_norm(pooled):
    average = lax.optimization_barrier(jnp.mean(pooled, axis=-1, keepdims=True))
    centred = pooled - average
    spread = lax.optimization_barrier(jnp.mean(centred * centred, axis=-1, keepdims=True))
    return centred * lax.rsqrt(spread + EPSILON)

def unit_rows(values):
    return values * lax.rsqrt(lax.optimization_barrier(jnp.sum(values * values, axis=-1, keepdims=True)) + EPSILON)

def reference(features, text_embed, img_ids, txt_ids, kernel, norm_gain, head_gain, projection, logit_scale, logit_bias):
    blocks = features.reshape(TOTAL // B_DEV, B_DEV, GRID, GRID, C)

    def forward_block(block):
        return block_pool(block.astype(jnp.float32), kernel, norm_gain)
    pooled = lax.map(forward_block, blocks).reshape(TOTAL, C)
    normalized, head_back = jax.vjp(head_norm, pooled)
    head_input = (normalized * head_gain).astype(jnp.bfloat16)
    embedded = jnp.dot(head_input, projection, preferred_element_type=jnp.float32)
    image_unit, image_back = jax.vjp(unit_rows, embedded)
    text_unit, text_back = jax.vjp(unit_rows, text_embed.astype(jnp.float32))
    image_low = image_unit.astype(jnp.bfloat16)
    text_low = text_unit.astype(jnp.bfloat16)
    logits = logit_scale[0] * jnp.dot(image_low, text_low.T, preferred_element_type=jnp.float32) + logit_bias[0]
    signs = jnp.where(img_ids[:, None] == txt_ids[None, :], 1.0, -1.0).astype(jnp.float32)
    pair_grad = (-signs * jax.nn.sigmoid(-signs * logits)).astype(jnp.bfloat16)
    image_grad = logit_scale[0] * jnp.dot(pair_grad, text_low, preferred_element_type=jnp.float32)
    text_grad = logit_scale[0] * jnp.dot(pair_grad.T, image_low, preferred_element_type=jnp.float32)
    embed_grad = image_back(image_grad)[0]
    embed_low = embed_grad.astype(jnp.bfloat16)
    grad_text = text_back(text_grad)[0]
    head_grad = jnp.dot(embed_low, projection.T, preferred_element_type=jnp.float32)
    grad_proj = jnp.dot(head_input.T, embed_low, preferred_element_type=jnp.float32)
    pooled_grad = head_back(head_grad * head_gain)[0]

    def backward_block(block_pair):
        block, cotangent = block_pair

        def local_pool(widened):
            return block_pool(widened, kernel, norm_gain)
        unused, block_back = jax.vjp(local_pool, block.astype(jnp.float32))
        return block_back(cotangent)[0].astype(jnp.bfloat16)
    grad_blocks = lax.map(backward_block, (blocks, pooled_grad.reshape(TOTAL // B_DEV, B_DEV, C)))
    grad_features = grad_blocks.reshape(TOTAL, GRID, GRID, C)
    return (grad_features, grad_text, grad_proj)
```

```python
import jax
import jax.numpy as jnp
from jax import lax
from jax.sharding import Mesh, PartitionSpec as P

EPSILON = 1e-06
AXES = ("y_lo", "z", "core", "x", "y_hi")
SIZES = (2, 8, 2, 4, 2)
ALL = AXES
GROUP = ("x", "y_hi")
LINE = ("y_lo", "z")
IDS = 128
HALF = 640


def block_pool(widened, kernel, norm_gain):
    margin = kernel.shape[0] // 2
    filtered = lax.conv_general_dilated(
        widened,
        kernel[:, :, None, :],
        (1, 1),
        ((margin, margin), (margin, margin)),
        dimension_numbers=("NHWC", "HWIO", "NHWC"),
        feature_group_count=widened.shape[3],
        precision=lax.Precision.HIGHEST,
    )
    average = jnp.mean(filtered, axis=-1, keepdims=True)
    centred = filtered - average
    spread = jnp.mean(centred * centred, axis=-1, keepdims=True)
    normed = centred * lax.rsqrt(spread + EPSILON) * norm_gain
    return jnp.mean(widened + normed, axis=(1, 2))


def head_norm(pooled):
    average = jnp.mean(pooled, axis=-1, keepdims=True)
    centred = pooled - average
    spread = jnp.mean(centred * centred, axis=-1, keepdims=True)
    return centred * lax.rsqrt(spread + EPSILON)


def inverse_length(values):
    return lax.rsqrt(jnp.sum(values * values, axis=-1, keepdims=True) + EPSILON)


def length_back(unit, inverse, cotangent):
    return inverse * (cotangent - unit * jnp.sum(unit * cotangent, axis=-1, keepdims=True))


def exchange(blocks, axes):
    return lax.all_to_all(blocks, axes, 0, 0, tiled=True)


def spread_out(block, axes, count):
    return exchange(jnp.broadcast_to(block[None], (count,) + block.shape), axes)


def swap_core(block):
    return lax.ppermute(block, "core", ((0, 1), (1, 0)))


def one_hot(ids):
    return (ids[:, None] == lax.broadcasted_iota(jnp.int32, (1, IDS), 1)).astype(jnp.bfloat16)


def dot(left, right, left_dim, right_dim):
    return lax.dot_general(
        left, right, (((left_dim,), (right_dim,)), ((), ())), preferred_element_type=jnp.float32
    )


def pair_weights(image_low, image_hot, text_low, text_hot, scale, shift):
    logits = scale * dot(image_low, text_low, 1, 1) + shift
    signs = 2.0 * dot(image_hot, text_hot, 1, 1) - 1.0
    return (-signs * jax.nn.sigmoid(-signs * logits)).astype(jnp.bfloat16)


def local(
    features,
    text_embed,
    img_ids,
    txt_ids,
    kernel,
    norm_gain,
    head_gain,
    projection,
    logit_scale,
    logit_bias,
):
    scale = logit_scale[0]
    shift = logit_bias[0]
    core = lax.axis_index("core")
    rows = text_embed.shape[0]
    width = text_embed.shape[1]
    share = projection.shape[0]
    group = lax.axis_size(GROUP)
    line = lax.axis_size(LINE)
    mine = lax.axis_index(GROUP)

    text_wide = text_embed.astype(jnp.float32)
    text_inverse = inverse_length(text_wide)
    text_unit = text_wide * text_inverse
    packed = jnp.concatenate([text_unit.astype(jnp.bfloat16), one_hot(txt_ids)], axis=1)
    group_texts = spread_out(packed, GROUP, group).reshape(group * rows, width + IDS)
    near_texts = spread_out(group_texts, LINE, line)
    far_texts = swap_core(near_texts)

    widened = features.astype(jnp.float32)

    def local_pool(field):
        return block_pool(field, kernel, norm_gain)

    pooled, block_back = jax.vjp(local_pool, widened)
    normalized, head_back = jax.vjp(head_norm, pooled)
    head_input = (normalized * head_gain).astype(jnp.bfloat16)

    split_input = head_input.reshape(rows, group, share).transpose(1, 0, 2)
    hot = jnp.broadcast_to(one_hot(img_ids)[None], (group, rows, IDS))
    received = exchange(jnp.concatenate([split_input, hot], axis=2), GROUP)
    received = received.reshape(group * rows, share + IDS)
    own_columns = received[:, :share]
    image_hot = received[:, share:]
    partial = dot(own_columns, projection, 1, 0).astype(jnp.bfloat16)
    embedded = jnp.sum(spread_out(partial, GROUP, group).astype(jnp.float32), axis=0)
    image_inverse = inverse_length(embedded)
    image_unit = embedded * image_inverse
    image_low = image_unit.astype(jnp.bfloat16)

    near_flat = near_texts.reshape(line * group * rows, width + IDS)
    far_flat = far_texts.reshape(line * group * rows, width + IDS)
    near_weights = pair_weights(
        image_low, image_hot, near_flat[:, :width], near_flat[:, width:], scale, shift
    )
    far_weights = pair_weights(
        image_low, image_hot, far_flat[:, :width], far_flat[:, width:], scale, shift
    )
    image_grad = scale * (
        dot(near_weights, near_flat[:, :width], 1, 0) + dot(far_weights, far_flat[:, :width], 1, 0)
    )
    embed_low = length_back(image_unit, image_inverse, image_grad).astype(jnp.bfloat16)

    head_part = dot(embed_low, projection, 1, 1)
    head_blocks = exchange(head_part.reshape(group, rows, share), GROUP)
    head_grad = head_blocks.transpose(1, 0, 2).reshape(rows, group * share)

    keep_at = core * (width - HALF)
    give_at = (1 - core) * (width - HALF)
    give = dot(own_columns, lax.dynamic_slice_in_dim(embed_low, give_at, HALF, 1), 0, 0)
    keep = dot(own_columns, lax.dynamic_slice_in_dim(embed_low, keep_at, HALF, 1), 0, 0)
    pair_sum = keep + swap_core(give.astype(jnp.bfloat16)).astype(jnp.float32)
    strips = exchange(pair_sum.astype(jnp.bfloat16).reshape(line, share // line, HALF), LINE)
    strip = jnp.sum(strips.astype(jnp.float32), axis=0).astype(jnp.bfloat16)
    near_half = spread_out(strip, LINE, line).reshape(share, HALF)
    far_half = swap_core(near_half)
    low_half = jnp.where(core == 0, near_half, far_half)
    high_half = jnp.where(core == 0, far_half, near_half)
    grad_proj = jnp.concatenate([low_half, high_half[:, 2 * HALF - width :]], axis=1).astype(
        jnp.float32
    )

    def own_texts(weights):
        blocks = weights.reshape(group * rows, line, group, rows)
        picked = lax.dynamic_slice_in_dim(blocks, mine, 1, 2)
        return picked.reshape(group * rows, line * rows)

    text_near = dot(own_texts(near_weights), image_low, 0, 0)
    text_far = dot(own_texts(far_weights), image_low, 0, 0)
    text_pair = text_near + swap_core(text_far.astype(jnp.bfloat16)).astype(jnp.float32)
    text_blocks = exchange(text_pair.astype(jnp.bfloat16).reshape(line, rows, width), LINE)
    text_grad = scale * jnp.sum(text_blocks.astype(jnp.float32), axis=0)
    grad_text = length_back(text_unit, text_inverse, text_grad)

    pooled_grad = head_back(head_grad * head_gain)[0]
    grad_features = block_back(pooled_grad)[0].astype(jnp.bfloat16)
    return (grad_features, grad_text, grad_proj)


def solution(mesh):
    fine = Mesh(mesh.devices.reshape(SIZES), AXES)
    placed = (
        P(ALL, None, None, None),
        P(ALL, None),
        P(ALL),
        P(ALL),
        P(),
        P(),
        P(),
        P(GROUP, None),
        P(),
        P(),
    )
    return jax.shard_map(
        local,
        mesh=fine,
        in_specs=placed,
        out_specs=(P(ALL, None, None, None), P(ALL, None), P(GROUP, None)),
        check_vma=False,
    )
```

```python
import jax
import jax.numpy as jnp
from jax import lax
from jax.experimental import pallas as pl
from jax.experimental.pallas import tpu as pltpu
from jax.sharding import Mesh, PartitionSpec as P

EPSILON = 1e-06
AXES = ("y_lo", "z", "core", "x", "y_hi")
SIZES = (2, 8, 2, 4, 2)
ALL = AXES
GROUP = ("x", "y_hi")
LINE = ("y_lo", "z")
PLANE = ("y_lo", "z", "y_hi")
MIB = 1024 * 1024
BIG = 60
IDS = 128
HALF = 640
LANES = 128
SIDE = 8
CELLS = 64
TAPS = 7
VMEM = pl.BlockSpec(memory_space=pltpu.VMEM)
SMEM = pl.BlockSpec(memory_space=pltpu.SMEM)
HBM = pl.BlockSpec(memory_space=pltpu.HBM)
STEPS = 4
PEERS = tuple((step_x, step_y) for step_x in range(4) for step_y in range(2))
BF16 = jnp.bfloat16
F32 = jnp.float32


def shape_of(dims, dtype):
    return jax.ShapeDtypeStruct(dims, dtype)


def call(body, outs, operands, name, micros, scratch=(), grant=40):
    specs = tuple(spec for _, spec in outs)
    shapes = tuple(shape for shape, _ in outs)
    single = len(outs) == 1
    return pl.pallas_call(
        body,
        out_shape=shapes[0] if single else shapes,
        in_specs=[spec for _, spec in operands],
        out_specs=specs[0] if single else specs,
        scratch_shapes=list(scratch),
        compiler_params=pltpu.CompilerParams(vmem_limit_bytes=grant * MIB),
        cost_estimate=pl.CostEstimate(
            flops=0, bytes_accessed=int(micros * 3e6), transcendentals=0
        ),
        name=name,
    )(*[operand for operand, _ in operands])


def group_peer(x, y_hi, step_x, step_y):
    return lax.rem(x + step_x, 4) * 2 + lax.rem(y_hi + step_y, 2)


def tap_weights(kernel_ref, at, column, flip):
    place = lax.broadcasted_iota(jnp.int32, (SIDE, LANES), 0) + (column - TAPS // 2)
    valid = (place >= 0) & (place < SIDE)
    weights = []
    for row in range(TAPS):
        if flip:
            line = kernel_ref[TAPS - 1 - row, pl.ds(TAPS - 1 - column, 1), at]
        else:
            line = kernel_ref[row, pl.ds(column, 1), at]
        weights.append(jnp.where(valid, jnp.broadcast_to(line, (SIDE, LANES)), 0.0))
    return weights


def filter_rows(fields, sums, kernel_ref, at, flip):
    for column in range(TAPS):
        weights = tap_weights(kernel_ref, at, column, flip)
        shift = (TAPS // 2 - column) % SIDE
        for field, total in zip(fields, sums):
            for source in range(SIDE):
                moved = field[source] if shift == 0 else pltpu.roll(field[source], shift, 0)
                for row in range(TAPS):
                    target = source - row + TAPS // 2
                    if 0 <= target < SIDE:
                        term = moved * weights[row]
                        total[target] = term if total[target] is None else total[target] + term
    return sums


def forward_kernel(
    field_hbm, kernel_hbm, gain_hbm, head_gain_hbm, ids_hbm,
    filtered_hbm, mean_ref, inverse_ref, normal_ref, send_ref,
    field_ref, kernel_ref, gain_ref, head_gain_ref, ids_ref, filtered_ref, pooled_ref, total_ref,
    field_sems, kernel_sems, small_sems, out_sems,
):
    images = field_ref.shape[0] // CELLS
    channels = field_ref.shape[1]
    chunks = channels // LANES
    part = 1.0 / channels
    block = channels // STEPS
    per_block = chunks // STEPS

    def block_at(step):
        return pl.ds(pl.multiple_of(step * block, LANES), block)

    def field_copy(step):
        at = block_at(step)
        return pltpu.make_async_copy(field_hbm.at[:, at], field_ref.at[:, at], field_sems.at[step])

    def kernel_copy(step):
        at = block_at(step)
        return pltpu.make_async_copy(
            kernel_hbm.at[:, :, at], kernel_ref.at[:, :, at], kernel_sems.at[step]
        )

    def filtered_copy(step):
        at = block_at(step)
        return pltpu.make_async_copy(filtered_ref.at[:, at], filtered_hbm.at[:, at], out_sems.at[step])

    small_copies = [
        pltpu.make_async_copy(gain_hbm, gain_ref, small_sems.at[0]),
        pltpu.make_async_copy(head_gain_hbm, head_gain_ref, small_sems.at[1]),
        pltpu.make_async_copy(ids_hbm, ids_ref, small_sems.at[2]),
    ]
    for step in range(STEPS):
        field_copy(step).start()
        kernel_copy(step).start()
    for copy in small_copies:
        copy.start()

    total_ref[...] = jnp.zeros_like(total_ref)

    def filter_chunk(chunk, carry):
        step = chunk // per_block

        @pl.when(chunk == step * per_block)
        def _():
            field_copy(step).wait()
            kernel_copy(step).wait()

        at = pl.ds(pl.multiple_of(chunk * LANES, LANES), LANES)
        for first in range(0, images, 2):
            fields = []
            for image in range(first, first + 2):
                rows = []
                for pair in range(SIDE // 2):
                    both = field_ref[pl.ds(image * CELLS + pair * 2 * SIDE, 2 * SIDE), at]
                    both = both.astype(jnp.float32)
                    rows += [both[:SIDE], both[SIDE:]]
                fields.append(rows)
            sums = [[None] * SIDE for _ in fields]
            filter_rows(fields, sums, kernel_ref, at, False)
            for offset, total in enumerate(sums):
                for row in range(SIDE):
                    cells = pl.ds((first + offset) * CELLS + row * SIDE, SIDE)
                    filtered_ref[cells, at] = total[row]
                    total_ref[cells, :] += total[row]
        return carry

    lax.fori_loop(0, chunks, filter_chunk, 0)
    for step in range(STEPS):
        filtered_copy(step).start()
    for copy in small_copies:
        copy.wait()
    mean_ref[...] = jnp.broadcast_to(
        jnp.sum(total_ref[...], axis=1, keepdims=True) * part, mean_ref.shape
    )

    for image in range(images):
        cells = pl.ds(image * CELLS, CELLS)
        average = mean_ref[cells, :]

        def spread_chunk(chunk, squares):
            at = pl.ds(pl.multiple_of(chunk * LANES, LANES), LANES)
            centred = filtered_ref[cells, at] - average
            return squares + centred * centred

        squares = lax.fori_loop(
            0, chunks, spread_chunk, jnp.zeros((CELLS, LANES), jnp.float32), unroll=4
        )
        spread = jnp.sum(squares, axis=1, keepdims=True) * part
        inverse_ref[cells, :] = jnp.broadcast_to(lax.rsqrt(spread + EPSILON), (CELLS, LANES))

    for image in range(images):
        cells = pl.ds(image * CELLS, CELLS)
        average = mean_ref[cells, :]
        inverse = inverse_ref[cells, :]

        def pool_chunk(chunk, carry):
            at = pl.ds(pl.multiple_of(chunk * LANES, LANES), LANES)
            normal = (filtered_ref[cells, at] - average) * inverse
            mixed = field_ref[cells, at].astype(jnp.float32) + normal * gain_ref[:, at]
            pooled_ref[pl.ds(image, 1), at] = jnp.sum(mixed, axis=0, keepdims=True) * (1.0 / CELLS)
            return carry

        lax.fori_loop(0, chunks, pool_chunk, 0, unroll=2)

    pooled = pooled_ref[...]
    centred = pooled - jnp.sum(pooled, axis=1, keepdims=True) * part
    spread = jnp.sum(centred * centred, axis=1, keepdims=True) * part
    head_inverse = lax.rsqrt(spread + EPSILON)
    normal = centred * head_inverse
    normal_ref[:, :channels] = normal
    normal_ref[:, channels:] = jnp.broadcast_to(head_inverse, (images, LANES))
    head_input = (normal * head_gain_ref[...]).astype(jnp.bfloat16)
    hot = hot_rows(ids_ref, images)
    group = send_ref.shape[0]
    share = channels // group
    for owner in range(group):
        send_ref[owner, :, :share] = head_input[:, owner * share : (owner + 1) * share]
        send_ref[owner, :, share:] = hot
    for step in range(STEPS):
        filtered_copy(step).wait()


def block_forward(features, kernel, norm_gain, head_gain, img_ids, group):
    images, channels = features.shape[0], features.shape[3]
    cells = images * CELLS
    dma = pltpu.SemaphoreType.DMA
    return call(
        forward_kernel,
        (
            (shape_of((cells, channels), F32), HBM),
            (shape_of((cells, LANES), F32), VMEM),
            (shape_of((cells, LANES), F32), VMEM),
            (shape_of((images, channels + LANES), F32), VMEM),
            (shape_of((group, images, channels // group + IDS), BF16), VMEM),
        ),
        (
            (features.reshape(cells, channels), HBM),
            (kernel, HBM),
            (norm_gain.reshape(1, channels), HBM),
            (head_gain.reshape(1, channels), HBM),
            (img_ids, HBM),
        ),
        "block_forward",
        14,
        scratch=(
            pltpu.VMEM((cells, channels), BF16),
            pltpu.VMEM(kernel.shape, F32),
            pltpu.VMEM((1, channels), F32),
            pltpu.VMEM((1, channels), F32),
            pltpu.SMEM(img_ids.shape, jnp.int32),
            pltpu.VMEM((cells, channels), F32),
            pltpu.VMEM((images, channels), F32),
            pltpu.VMEM((cells, LANES), F32),
            dma((STEPS,)),
            dma((STEPS,)),
            dma((3,)),
            dma((STEPS,)),
        ),
        grant=BIG,
    )


def backward_kernel(
    b0, b1, b2, b3, b4, b5, b6, b7, normal_hbm, gain_hbm, head_gain_hbm,
    filtered_hbm, mean_hbm, inverse_hbm, kernel_hbm, after_hbm,
    out_hbm,
    blocks_ref, normal_ref, gain_ref, head_gain_ref, filtered_ref, mean_ref, inverse_ref, kernel_ref,
    out_ref, even_ref, lean_ref, pull_ref, tilt_ref,
    block_sems, small_sems, filtered_sems, out_sems,
):
    del after_hbm
    images, channels = even_ref.shape
    blocks = (b0, b1, b2, b3, b4, b5, b6, b7)
    share = channels // len(blocks)
    wide = channels // STEPS

    def block_at(step):
        return pl.ds(pl.multiple_of(step * wide, LANES), wide)

    def out_copy(step):
        at = block_at(step)
        return pltpu.make_async_copy(out_ref.at[:, at], out_hbm.at[:, at], out_sems.at[step])

    head_copies = [
        pltpu.make_async_copy(block, blocks_ref.at[index], block_sems.at[index])
        for index, block in enumerate(blocks)
    ]
    small_copies = [
        pltpu.make_async_copy(source, target, small_sems.at[index])
        for index, (source, target) in enumerate((
            (head_gain_hbm, head_gain_ref), (gain_hbm, gain_ref), (normal_hbm, normal_ref),
            (mean_hbm, mean_ref), (inverse_hbm, inverse_ref),
        ))
    ]
    filtered_copies = [
        pltpu.make_async_copy(
            filtered_hbm.at[:, block_at(step)], filtered_ref.at[:, block_at(step)],
            filtered_sems.at[step],
        )
        for step in range(STEPS)
    ]
    kernel_copy = pltpu.make_async_copy(kernel_hbm, kernel_ref, small_sems.at[5])
    for copy in (*head_copies, *small_copies, *filtered_copies, kernel_copy):
        copy.start()
    chunks = channels // LANES
    per_block = chunks // STEPS
    part = 1.0 / channels

    for copy in (*head_copies, *small_copies):
        copy.wait()
    x, y_hi = lax.axis_index("x"), lax.axis_index("y_hi")
    for index, (step_x, step_y) in enumerate(PEERS):
        owner = group_peer(x, y_hi, 4 - step_x, step_y)
        at = pl.ds(pl.multiple_of(owner * share, LANES), share)
        tilt_ref[:, at] = blocks_ref[index] * head_gain_ref[:, at]
    cotangent = tilt_ref[...]
    normal = normal_ref[:, :channels]
    level = jnp.sum(cotangent, axis=1, keepdims=True) * part
    lean = jnp.sum(cotangent * normal, axis=1, keepdims=True) * part
    pooled_grad = normal_ref[:, channels : channels + 1] * (cotangent - level - normal * lean)
    even = pooled_grad * (1.0 / CELLS)
    even_ref[...] = even
    pull = even * gain_ref[...]
    pull_ref[...] = pull
    tilt_ref[...] = pull - jnp.sum(pull, axis=1, keepdims=True) * part

    for step in range(STEPS):
        filtered_copies[step].wait()
        for image in range(images):
            cells = pl.ds(image * CELLS, CELLS)
            average = mean_ref[cells, :]

            def lean_chunk(chunk, total):
                at = pl.ds(pl.multiple_of(chunk * LANES, LANES), LANES)
                return total + (filtered_ref[cells, at] - average) * pull_ref[pl.ds(image, 1), at]

            total = jnp.zeros((CELLS, LANES), F32) if step == 0 else lean_ref[cells, :]
            lean_ref[cells, :] = lax.fori_loop(
                step * per_block, (step + 1) * per_block, lean_chunk, total, unroll=True
            )
    inverse = inverse_ref[...]
    mean_lean = jnp.sum(lean_ref[...], axis=1, keepdims=True) * part
    lean_ref[...] = inverse * (inverse * (inverse * mean_lean))
    kernel_copy.wait()

    def filter_chunk(chunk, carry):
        at = pl.ds(pl.multiple_of(chunk * LANES, LANES), LANES)
        for first in range(0, images, 2):
            fields = []
            sums = []
            for image in range(first, first + 2):
                tilt = jnp.broadcast_to(tilt_ref[pl.ds(image, 1), at], (SIDE, LANES))
                even = jnp.broadcast_to(even_ref[pl.ds(image, 1), at], (SIDE, LANES))
                rows = []
                for row in range(SIDE):
                    cells = pl.ds(image * CELLS + row * SIDE, SIDE)
                    rows.append(
                        inverse_ref[cells, :] * tilt
                        - lean_ref[cells, :] * (filtered_ref[cells, at] - mean_ref[cells, :])
                    )
                fields.append(rows)
                sums.append([even] * SIDE)
            filter_rows(fields, sums, kernel_ref, at, True)
            for offset, total in enumerate(sums):
                for pair in range(SIDE // 2):
                    both = jnp.concatenate(total[2 * pair : 2 * pair + 2], axis=0)
                    cells = pl.ds((first + offset) * CELLS + pair * 2 * SIDE, 2 * SIDE)
                    out_ref[cells, at] = both.astype(jnp.bfloat16)
        step = chunk // per_block

        @pl.when(chunk == step * per_block + per_block - 1)
        def _():
            out_copy(step).start()

        return carry

    lax.fori_loop(0, chunks, filter_chunk, 0)
    for step in range(STEPS):
        out_copy(step).wait()


def block_backward(blocks, normal, norm_gain, head_gain, filtered, mean, inverse, kernel, after):
    cells, channels = filtered.shape
    images = cells // CELLS
    dma = pltpu.SemaphoreType.DMA
    out = call(
        backward_kernel,
        ((shape_of((cells, channels), BF16), HBM),),
        tuple(
            (array, HBM)
            for array in (
                *blocks, normal, norm_gain.reshape(1, channels), head_gain.reshape(1, channels),
                filtered, mean, inverse, kernel, after,
            )
        ),
        "block_backward",
        14,
        scratch=(
            pltpu.VMEM((len(blocks),) + blocks[0].shape, F32),
            pltpu.VMEM(normal.shape, F32),
            pltpu.VMEM((1, channels), F32),
            pltpu.VMEM((1, channels), F32),
            pltpu.VMEM((cells, channels), F32),
            pltpu.VMEM((cells, LANES), F32),
            pltpu.VMEM((cells, LANES), F32),
            pltpu.VMEM(kernel.shape, F32),
            pltpu.VMEM((cells, channels), BF16),
            pltpu.VMEM((images, channels), F32),
            pltpu.VMEM((cells, LANES), F32),
            pltpu.VMEM((images, channels), F32),
            pltpu.VMEM((images, channels), F32),
            dma((len(blocks),)),
            dma((6,)),
            dma((STEPS,)),
            dma((STEPS,)),
        ),
        grant=BIG,
    )
    return out.reshape(images, SIDE, SIDE, channels)


def dot(left, right, left_dim, right_dim):
    return lax.dot_general(
        left, right, (((left_dim,), (right_dim,)), ((), ())), preferred_element_type=F32
    )


def inverse_length(values):
    return lax.rsqrt(jnp.sum(values * values, axis=-1, keepdims=True) + EPSILON)


def length_back(unit, inverse, cotangent):
    return inverse * (cotangent - unit * jnp.sum(unit * cotangent, axis=-1, keepdims=True))


def hot_rows(ids_ref, rows):
    row = lax.broadcasted_iota(jnp.int32, (rows, IDS), 0)
    ids = jnp.zeros((rows, IDS), jnp.int32)
    for index in range(rows):
        ids = jnp.where(row == index, ids_ref[index], ids)
    lane = lax.broadcasted_iota(jnp.int32, (rows, IDS), 1)
    return jnp.where(ids == lane, 1.0, 0.0).astype(BF16)


def pack_kernel(text_hbm, ids_hbm, out_ref, text_ref, ids_ref, sems):
    copies = [
        pltpu.make_async_copy(text_hbm, text_ref, sems.at[0]),
        pltpu.make_async_copy(ids_hbm, ids_ref, sems.at[1]),
    ]
    for copy in copies:
        copy.start()
    for copy in copies:
        copy.wait()
    rows, width = text_ref.shape
    text = text_ref[...].astype(F32)
    unit = (text * inverse_length(text)).astype(BF16)
    hot = hot_rows(ids_ref, rows)
    for target in range(out_ref.shape[0]):
        out_ref[target, :, :width] = unit
        out_ref[target, :, width:] = hot


def line_kernel(plane_ref, after_ref, out_ref):
    del after_ref
    plane, rows, _ = plane_ref.shape
    line = plane // 2
    y_hi = lax.axis_index("y_hi")
    for side in range(2):
        part = lax.rem(y_hi + side, 2)
        for first in range(0, line, 4):
            four = [plane_ref[(first + offset) * 2 + part].astype(F32) for offset in range(4)]
            at = (side * line + first) * rows
            out_ref[at : at + 4 * rows, :] = jnp.concatenate(four, axis=0).astype(BF16)


def partial_kernel(received_ref, projection_ref, out_ref, columns_ref, hot_ref):
    group = received_ref.shape[0]
    share = projection_ref.shape[0]
    rows = jnp.concatenate([received_ref[owner].astype(F32) for owner in range(group)], axis=0)
    columns = rows[:, :share].astype(BF16)
    columns_ref[...] = columns
    hot_ref[...] = rows[:, share:].astype(BF16)
    partial = dot(columns, projection_ref[...], 1, 0).astype(BF16)
    for target in range(group):
        out_ref[target] = partial


def pair_kernel(
    partials_ref, columns_ref, hot_ref, projection_ref, t0, t1, t2, t3, t4, t5, t6, t7,
    scale_ref, shift_ref,
    h0, h1, h2, h3, h4, h5, h6, h7, keep_ref, give_ref,
    low_ref, embed_ref, rows_ref, near_ref, far_ref, head_ref,
):
    group, images, width = partials_ref.shape
    blocks = (t0, t1, t2, t3, t4, t5, t6, t7)
    scale, shift, core = scale_ref[0], shift_ref[0], lax.axis_index("core")
    embedded = partials_ref[0].astype(F32)
    for owner in range(1, group):
        embedded += partials_ref[owner].astype(F32)
    inverse = inverse_length(embedded)
    unit = embedded * inverse
    low = unit.astype(BF16)
    low_ref[...] = low
    hot = hot_ref[...]
    weights = []
    for block in blocks:
        logits = scale * dot(low, block[:, :width], 1, 1) + shift
        signs = 2.0 * dot(hot, block[:, width:], 1, 1) - 1.0
        weights.append((-signs * jax.nn.sigmoid(-signs * logits)).astype(BF16))
    image_grad = dot(weights[0], t0[:, :width], 1, 0)
    for weight, block in zip(weights[1:], blocks[1:]):
        image_grad += dot(weight, block[:, :width], 1, 0)
    embed = length_back(unit, inverse, scale * image_grad).astype(BF16)
    embed_ref[...] = embed
    head = dot(embed, projection_ref[...], 1, 1)
    rows = images // group
    for owner in range(group):
        head_ref[owner] = head[owner * rows : (owner + 1) * rows]
    x, y_hi = lax.axis_index("x"), lax.axis_index("y_hi")
    for (step_x, step_y), out_ref in zip(PEERS, (h0, h1, h2, h3, h4, h5, h6, h7)):
        out_ref[...] = head_ref[group_peer(x, y_hi, step_x, step_y)]
    columns = columns_ref[...]
    line = keep_ref.shape[0]
    own = weights[0][:, : line * rows]
    other = weights[4][:, : line * rows]
    strip = columns.shape[1] // line
    for out_ref, side, first, second in (
        (give_ref, 1 - core, other, own),
        (keep_ref, core, own, other),
    ):
        at = pl.ds(pl.multiple_of(side * (width - HALF), LANES), HALF)
        rows_ref[...] = dot(columns, embed_ref[:, at], 0, 0)
        low_half = low_ref[:, at]
        near_ref[...] = dot(first, low_half, 0, 0)
        far_ref[...] = dot(second, low_half, 0, 0)
        for target in range(line):
            texts = slice(target * rows, (target + 1) * rows)
            stacked = jnp.concatenate(
                [rows_ref[target * strip : (target + 1) * strip], near_ref[texts], far_ref[texts]],
                axis=0,
            )
            out_ref[target] = stacked.astype(out_ref.dtype)


def add_kernel(keep_ref, got_ref, out_ref):
    out_ref[...] = (keep_ref[...] + got_ref[...].astype(F32)).astype(BF16)


def strip_kernel(strips_ref, out_ref, mine_ref, theirs_ref):
    line, rows, half = strips_ref.shape
    texts = mine_ref.shape[0]
    strip = rows - 2 * texts
    total = strips_ref[0].astype(F32)
    for source in range(1, line):
        total += strips_ref[source].astype(F32)
    low = total[:strip].astype(BF16)
    for target in range(line):
        out_ref[target] = low
    mine_ref[...] = total[strip : strip + texts]
    theirs_ref[...] = total[strip + texts :]


def text_kernel(text_ref, mine_ref, got_ref, scale_ref, out_ref):
    width = text_ref.shape[1]
    text = text_ref[...].astype(F32)
    inverse = inverse_length(text)
    first = lax.axis_index("core") == 0
    mine, got = mine_ref[...], got_ref[...]
    left = jnp.where(first, mine, got)
    right = jnp.where(first, got, mine)
    grad = jnp.concatenate([left, right[:, 2 * HALF - width :]], axis=1)
    out_ref[...] = length_back(text * inverse, inverse, scale_ref[0] * grad)


def join_kernel(near_ref, far_ref, out_ref):
    core = lax.axis_index("core")
    width = out_ref.shape[1]

    def put(left, right):
        out_ref[:, :HALF] = left[...].astype(F32)
        out_ref[:, HALF:] = right[:, 2 * HALF - width :].astype(F32)

    pl.when(core == 0)(lambda: put(near_ref, far_ref))
    pl.when(core != 0)(lambda: put(far_ref, near_ref))


def exchange(blocks, axes):
    return lax.all_to_all(blocks, axes, 0, 0, tiled=True)


def swap_core(block):
    return lax.ppermute(block, "core", ((0, 1), (1, 0)))


def along_x(block, step):
    return lax.ppermute(block, "x", tuple((i, (i + step) % 4) for i in range(4)))


def local(
    features,
    text_embed,
    img_ids,
    txt_ids,
    kernel,
    norm_gain,
    head_gain,
    projection,
    logit_scale,
    logit_bias,
):
    rows, width = text_embed.shape
    share = projection.shape[0]
    group = lax.axis_size(GROUP)
    line = lax.axis_size(LINE)
    images = group * rows
    texts = line * rows
    strip = share // line
    dma = pltpu.SemaphoreType.DMA

    packed = call(
        pack_kernel,
        ((shape_of((2 * line, rows, width + IDS), BF16), VMEM),),
        ((text_embed, HBM), (txt_ids, HBM)),
        "text_pack", 1,
        scratch=(
            pltpu.VMEM((rows, width), BF16), pltpu.SMEM((rows,), jnp.int32), dma((2,)),
        ),
        grant=BIG,
    )
    gathered = exchange(packed, PLANE)
    filtered, mean, inverse, normal, send = block_forward(
        features, kernel, norm_gain, head_gain, img_ids, group
    )
    gathered, send = lax.optimization_barrier((gathered, send))
    received = exchange(send, GROUP)
    partials, columns, hot = call(
        partial_kernel,
        (
            (shape_of((group, images, width), BF16), VMEM),
            (shape_of((images, share), BF16), VMEM),
            (shape_of((images, IDS), BF16), VMEM),
        ),
        ((received, VMEM), (projection, VMEM)),
        "partial_embed", 2,
    )
    near = [
        call(
            line_kernel,
            ((shape_of((2 * texts, width + IDS), BF16), VMEM),),
            ((gathered, VMEM), (columns, VMEM)),
            "line_rows", 1,
        )
    ]
    near += [along_x(near[0], step) for step in (1, 3, 2)]
    far = [swap_core(block) for block in near]
    partials = exchange(partials, GROUP)
    results = call(
        pair_kernel,
        ((shape_of((rows, share), F32), VMEM),) * group
        + (
            (shape_of((line, strip + 2 * rows, HALF), F32), VMEM),
            (shape_of((line, strip + 2 * rows, HALF), BF16), VMEM),
        ),
        tuple((array, VMEM) for array in (partials, columns, hot, projection, *near, *far))
        + ((logit_scale, SMEM), (logit_bias, SMEM)),
        "pairs", 6,
        scratch=(
            pltpu.VMEM((images, width), BF16),
            pltpu.VMEM((images, width), BF16),
            pltpu.VMEM((share, HALF), F32),
            pltpu.VMEM((texts, HALF), F32),
            pltpu.VMEM((texts, HALF), F32),
            pltpu.VMEM((group, rows, share), F32),
        ),
    )
    head_parts, (keep, give) = results[:group], results[group:]
    strips = call(
        add_kernel, ((shape_of(keep.shape, BF16), VMEM),), ((keep, VMEM), (swap_core(give), VMEM)),
        "strip_add", 1,
        grant=BIG,
    )
    strips = exchange(strips, LINE)
    head_blocks = [head_parts[0]]
    for (step_x, step_y), part in zip(PEERS[1:], head_parts[1:]):
        pairs = tuple(
            (at, (at // 2 + step_x) % 4 * 2 + (at % 2 + step_y) % 2) for at in range(group)
        )
        head_blocks.append(lax.ppermute(part, GROUP, pairs))
    strips, *head_blocks = lax.optimization_barrier((strips, *head_blocks))
    sums, mine, theirs = call(
        strip_kernel,
        (
            (shape_of((line, strip, HALF), BF16), VMEM),
            (shape_of((rows, HALF), F32), VMEM),
            (shape_of((rows, HALF), F32), VMEM),
        ),
        ((strips, VMEM),),
        "strip_sum", 1,
        grant=BIG,
    )
    near_half = exchange(sums, LINE).reshape(share, HALF)
    grad_features = block_backward(
        head_blocks, normal, norm_gain, head_gain, filtered, mean, inverse, kernel, mine
    )
    near_half, theirs, grad_features = lax.optimization_barrier((near_half, theirs, grad_features))
    grad_text = call(
        text_kernel,
        ((shape_of((rows, width), F32), VMEM),),
        ((text_embed, VMEM), (mine, VMEM), (swap_core(theirs), VMEM), (logit_scale, SMEM)),
        "text_grad", 1,
    )
    grad_proj = call(
        join_kernel,
        ((shape_of((share, width), F32), VMEM),),
        ((near_half, VMEM), (swap_core(near_half), VMEM)),
        "proj_join", 2,
    )
    return (grad_features, grad_text, grad_proj)


def solution(mesh):
    fine = Mesh(mesh.devices.reshape(SIZES), AXES)
    placed = (
        P(ALL, None, None, None),
        P(ALL, None),
        P(ALL),
        P(ALL),
        P(),
        P(),
        P(),
        P(GROUP, None),
        P(),
        P(),
    )
    return jax.shard_map(
        local,
        mesh=fine,
        in_specs=placed,
        out_specs=(P(ALL, None, None, None), P(ALL, None), P(GROUP, None)),
        check_vma=False,
    )
```

```python
import functools

import jax
import jax.numpy as jnp
from jax import lax
from jax.experimental import pallas as pl
from jax.experimental.pallas import tpu as pltpu
from jax.sharding import Mesh, PartitionSpec as P

EPSILON = 1e-06
AXES = ("y_lo", "z", "core", "x", "y_hi")
SIZES = (2, 8, 2, 4, 2)
ALL = AXES
GROUP = ("x", "y_hi")
LINE = ("y_lo", "z")
MIB = 1024 * 1024
BIG = 60
IDS = 128
HALF = 640
LANES = 128
SIDE = 8
CELLS = 64
TAPS = 7
VMEM = pl.BlockSpec(memory_space=pltpu.VMEM)
SMEM = pl.BlockSpec(memory_space=pltpu.SMEM)
HBM = pl.BlockSpec(memory_space=pltpu.HBM)
STEPS = 4
PEERS = tuple((step_x, step_y) for step_x in range(4) for step_y in range(2))
BF16 = jnp.bfloat16
F32 = jnp.float32


def shape_of(dims, dtype):
    return jax.ShapeDtypeStruct(dims, dtype)


def call(body, outs, operands, name, micros, scratch=(), grant=40, aliases=None):
    specs = tuple(spec for _, spec in outs)
    shapes = tuple(shape for shape, _ in outs)
    single = len(outs) == 1
    return pl.pallas_call(
        body,
        out_shape=shapes[0] if single else shapes,
        in_specs=[spec for _, spec in operands],
        out_specs=specs[0] if single else specs,
        scratch_shapes=list(scratch),
        compiler_params=pltpu.CompilerParams(vmem_limit_bytes=grant * MIB),
        cost_estimate=pl.CostEstimate(
            flops=0, bytes_accessed=int(micros * 3e6), transcendentals=0
        ),
        input_output_aliases=aliases or {},
        name=name,
    )(*[operand for operand, _ in operands])


def group_peer(x, y_hi, step_x, step_y):
    return lax.rem(x + step_x, 4) * 2 + lax.rem(y_hi + step_y, 2)


def tap_weights(kernel_ref, at, column, flip):
    place = lax.broadcasted_iota(jnp.int32, (SIDE, LANES), 0) + (column - TAPS // 2)
    valid = (place >= 0) & (place < SIDE)
    weights = []
    for row in range(TAPS):
        if flip:
            line = kernel_ref[TAPS - 1 - row, pl.ds(TAPS - 1 - column, 1), at]
        else:
            line = kernel_ref[row, pl.ds(column, 1), at]
        weights.append(jnp.where(valid, jnp.broadcast_to(line, (SIDE, LANES)), 0.0))
    return weights


def filter_rows(fields, sums, kernel_ref, at, flip):
    for column in range(TAPS):
        weights = tap_weights(kernel_ref, at, column, flip)
        shift = (TAPS // 2 - column) % SIDE
        for field, total in zip(fields, sums):
            for source in range(SIDE):
                moved = field[source] if shift == 0 else pltpu.roll(field[source], shift, 0)
                for row in range(TAPS):
                    target = source - row + TAPS // 2
                    if 0 <= target < SIDE:
                        term = moved * weights[row]
                        total[target] = term if total[target] is None else total[target] + term
    return sums


def forward_kernel(
    field_hbm, kernel_hbm, gain_hbm, head_gain_hbm, ids_hbm,
    filtered_hbm, mean_ref, inverse_ref, normal_ref, send_ref,
    field_ref, kernel_ref, gain_ref, head_gain_ref, ids_ref, filtered_ref, pooled_ref, total_ref,
    field_sems, kernel_sems, small_sems, out_sems,
):
    images = field_ref.shape[0] // CELLS
    channels = field_ref.shape[1]
    chunks = channels // LANES
    part = 1.0 / channels
    block = channels // STEPS
    per_block = chunks // STEPS

    def block_at(step):
        return pl.ds(pl.multiple_of(step * block, LANES), block)

    def field_copy(step):
        at = block_at(step)
        return pltpu.make_async_copy(field_hbm.at[:, at], field_ref.at[:, at], field_sems.at[step])

    def kernel_copy(step):
        at = block_at(step)
        return pltpu.make_async_copy(
            kernel_hbm.at[:, :, at], kernel_ref.at[:, :, at], kernel_sems.at[step]
        )

    def filtered_copy(step):
        at = block_at(step)
        return pltpu.make_async_copy(filtered_ref.at[:, at], filtered_hbm.at[:, at], out_sems.at[step])

    small_copies = [
        pltpu.make_async_copy(gain_hbm, gain_ref, small_sems.at[0]),
        pltpu.make_async_copy(head_gain_hbm, head_gain_ref, small_sems.at[1]),
        pltpu.make_async_copy(ids_hbm, ids_ref, small_sems.at[2]),
    ]
    for step in range(STEPS):
        field_copy(step).start()
        kernel_copy(step).start()
    for copy in small_copies:
        copy.start()

    total_ref[...] = jnp.zeros_like(total_ref)

    def filter_chunk(chunk, carry):
        step = chunk // per_block

        @pl.when(chunk == step * per_block)
        def _():
            field_copy(step).wait()
            kernel_copy(step).wait()

        at = pl.ds(pl.multiple_of(chunk * LANES, LANES), LANES)
        for first in range(0, images, 2):
            fields = []
            for image in range(first, first + 2):
                rows = []
                for pair in range(SIDE // 2):
                    both = field_ref[pl.ds(image * CELLS + pair * 2 * SIDE, 2 * SIDE), at]
                    both = both.astype(jnp.float32)
                    rows += [both[:SIDE], both[SIDE:]]
                fields.append(rows)
            sums = [[None] * SIDE for _ in fields]
            filter_rows(fields, sums, kernel_ref, at, False)
            for offset, total in enumerate(sums):
                for row in range(SIDE):
                    cells = pl.ds((first + offset) * CELLS + row * SIDE, SIDE)
                    filtered_ref[cells, at] = total[row]
                    total_ref[cells, :] += total[row]
        return carry

    lax.fori_loop(0, chunks, filter_chunk, 0)
    for step in range(STEPS):
        filtered_copy(step).start()
    for copy in small_copies:
        copy.wait()
    mean_ref[...] = jnp.broadcast_to(
        jnp.sum(total_ref[...], axis=1, keepdims=True) * part, mean_ref.shape
    )

    for image in range(images):
        cells = pl.ds(image * CELLS, CELLS)
        average = mean_ref[cells, :]

        def spread_chunk(chunk, squares):
            at = pl.ds(pl.multiple_of(chunk * LANES, LANES), LANES)
            centred = filtered_ref[cells, at] - average
            return squares + centred * centred

        squares = lax.fori_loop(
            0, chunks, spread_chunk, jnp.zeros((CELLS, LANES), jnp.float32), unroll=4
        )
        spread = jnp.sum(squares, axis=1, keepdims=True) * part
        inverse_ref[cells, :] = jnp.broadcast_to(lax.rsqrt(spread + EPSILON), (CELLS, LANES))

    for image in range(images):
        cells = pl.ds(image * CELLS, CELLS)
        average = mean_ref[cells, :]
        inverse = inverse_ref[cells, :]

        def pool_chunk(chunk, carry):
            at = pl.ds(pl.multiple_of(chunk * LANES, LANES), LANES)
            normal = (filtered_ref[cells, at] - average) * inverse
            mixed = field_ref[cells, at].astype(jnp.float32) + normal * gain_ref[:, at]
            pooled_ref[pl.ds(image, 1), at] = jnp.sum(mixed, axis=0, keepdims=True) * (1.0 / CELLS)
            return carry

        lax.fori_loop(0, chunks, pool_chunk, 0, unroll=2)

    pooled = pooled_ref[...]
    centred = pooled - jnp.sum(pooled, axis=1, keepdims=True) * part
    spread = jnp.sum(centred * centred, axis=1, keepdims=True) * part
    head_inverse = lax.rsqrt(spread + EPSILON)
    normal = centred * head_inverse
    normal_ref[:, :channels] = normal
    normal_ref[:, channels:] = jnp.broadcast_to(head_inverse, (images, LANES))
    head_input = (normal * head_gain_ref[...]).astype(jnp.bfloat16)
    hot = hot_rows(ids_ref, images)
    group = send_ref.shape[0]
    share = channels // group
    for owner in range(group):
        send_ref[owner, :, :share] = head_input[:, owner * share : (owner + 1) * share]
        send_ref[owner, :, share:] = hot
    for step in range(STEPS):
        filtered_copy(step).wait()


def block_forward(features, kernel, norm_gain, head_gain, img_ids, group):
    images, channels = features.shape[0], features.shape[3]
    cells = images * CELLS
    dma = pltpu.SemaphoreType.DMA
    return call(
        forward_kernel,
        (
            (shape_of((cells, channels), F32), HBM),
            (shape_of((cells, LANES), F32), VMEM),
            (shape_of((cells, LANES), F32), VMEM),
            (shape_of((images, channels + LANES), F32), VMEM),
            (shape_of((group, images, channels // group + IDS), BF16), VMEM),
        ),
        (
            (features.reshape(cells, channels), HBM),
            (kernel, HBM),
            (norm_gain.reshape(1, channels), HBM),
            (head_gain.reshape(1, channels), HBM),
            (img_ids, HBM),
        ),
        "block_forward",
        14,
        scratch=(
            pltpu.VMEM((cells, channels), BF16),
            pltpu.VMEM(kernel.shape, F32),
            pltpu.VMEM((1, channels), F32),
            pltpu.VMEM((1, channels), F32),
            pltpu.SMEM(img_ids.shape, jnp.int32),
            pltpu.VMEM((cells, channels), F32),
            pltpu.VMEM((images, channels), F32),
            pltpu.VMEM((cells, LANES), F32),
            dma((STEPS,)),
            dma((STEPS,)),
            dma((3,)),
            dma((STEPS,)),
        ),
        grant=BIG,
    )


def backward_kernel(
    pair, s0, s1, s2, s3, normal_hbm, gain_hbm, head_gain_hbm,
    filtered_hbm, mean_hbm, inverse_hbm, kernel_hbm, after_hbm,
    out_hbm,
    blocks_ref, normal_ref, gain_ref, head_gain_ref, filtered_ref, mean_ref, inverse_ref, kernel_ref,
    out_ref, even_ref, lean_ref, pull_ref, tilt_ref,
    block_sems, small_sems, filtered_sems, out_sems,
):
    del after_hbm
    images, channels = even_ref.shape
    blocks = (s0, s1, s2, s3)
    share = channels // len(PEERS)
    cells = pl.ds(pair * 2 * CELLS, 2 * CELLS)
    wide = channels // STEPS

    def block_at(step):
        return pl.ds(pl.multiple_of(step * wide, LANES), wide)

    def out_copy(step):
        at = block_at(step)
        return pltpu.make_async_copy(out_ref.at[:, at], out_hbm.at[cells, at], out_sems.at[step])

    head_copies = [
        pltpu.make_async_copy(block, blocks_ref.at[index], block_sems.at[index])
        for index, block in enumerate(blocks)
    ]
    small_copies = [
        pltpu.make_async_copy(source, target, small_sems.at[index])
        for index, (source, target) in enumerate((
            (head_gain_hbm, head_gain_ref), (gain_hbm, gain_ref), (normal_hbm, normal_ref),
            (mean_hbm.at[cells, :], mean_ref), (inverse_hbm.at[cells, :], inverse_ref),
        ))
    ]
    filtered_copies = [
        pltpu.make_async_copy(
            filtered_hbm.at[cells, block_at(step)], filtered_ref.at[:, block_at(step)],
            filtered_sems.at[step],
        )
        for step in range(STEPS)
    ]
    kernel_copy = pltpu.make_async_copy(kernel_hbm, kernel_ref, small_sems.at[5])
    for copy in (*head_copies, *small_copies, *filtered_copies, kernel_copy):
        copy.start()
    chunks = channels // LANES
    per_block = chunks // STEPS
    part = 1.0 / channels

    for copy in (*head_copies, *small_copies):
        copy.wait()
    x, y_hi = lax.axis_index("x"), lax.axis_index("y_hi")
    for step_x, step_y in PEERS:
        owner = group_peer(x, y_hi, 4 - step_x, step_y)
        at = pl.ds(pl.multiple_of(owner * share, LANES), share)
        tilt_ref[:, at] = blocks_ref[step_x, step_y] * head_gain_ref[:, at]
    cotangent = tilt_ref[...]
    normal = normal_ref[:, :channels]
    level = jnp.sum(cotangent, axis=1, keepdims=True) * part
    lean = jnp.sum(cotangent * normal, axis=1, keepdims=True) * part
    pooled_grad = normal_ref[:, channels : channels + 1] * (cotangent - level - normal * lean)
    even = pooled_grad * (1.0 / CELLS)
    even_ref[...] = even
    pull = even * gain_ref[...]
    pull_ref[...] = pull
    tilt_ref[...] = pull - jnp.sum(pull, axis=1, keepdims=True) * part

    for step in range(STEPS):
        filtered_copies[step].wait()
        for image in range(2):
            spot = pl.ds(image * CELLS, CELLS)
            average = mean_ref[spot, :]

            def lean_chunk(chunk, total, spot=spot, average=average, image=image):
                at = pl.ds(pl.multiple_of(chunk * LANES, LANES), LANES)
                return total + (filtered_ref[spot, at] - average) * pull_ref[pl.ds(2 * pair + image, 1), at]

            total = jnp.zeros((CELLS, LANES), F32) if step == 0 else lean_ref[spot, :]
            lean_ref[spot, :] = lax.fori_loop(
                step * per_block, (step + 1) * per_block, lean_chunk, total, unroll=True
            )
    inverse = inverse_ref[...]
    mean_lean = jnp.sum(lean_ref[...], axis=1, keepdims=True) * part
    lean_ref[...] = inverse * (inverse * (inverse * mean_lean))
    kernel_copy.wait()

    def filter_chunk(chunk, carry):
        at = pl.ds(pl.multiple_of(chunk * LANES, LANES), LANES)
        fields = []
        sums = []
        for image in range(2):
            source = pl.ds(2 * pair + image, 1)
            tilt = jnp.broadcast_to(tilt_ref[source, at], (SIDE, LANES))
            even = jnp.broadcast_to(even_ref[source, at], (SIDE, LANES))
            rows = []
            for row in range(SIDE):
                spot = pl.ds(image * CELLS + row * SIDE, SIDE)
                rows.append(
                    inverse_ref[spot, :] * tilt
                    - lean_ref[spot, :] * (filtered_ref[spot, at] - mean_ref[spot, :])
                )
            fields.append(rows)
            sums.append([even] * SIDE)
        filter_rows(fields, sums, kernel_ref, at, True)
        for image, total in enumerate(sums):
            for half in range(SIDE // 2):
                two = jnp.concatenate(total[2 * half : 2 * half + 2], axis=0)
                spot = pl.ds(image * CELLS + half * 2 * SIDE, 2 * SIDE)
                out_ref[spot, at] = two.astype(jnp.bfloat16)
        step = chunk // per_block

        @pl.when(chunk == step * per_block + per_block - 1)
        def _():
            out_copy(step).start()

        return carry

    lax.fori_loop(0, chunks, filter_chunk, 0)
    for step in range(STEPS):
        out_copy(step).wait()


def first_backward(pair, *refs):
    backward_kernel(pair, *refs)


def second_backward(pair, *refs):
    backward_kernel(pair, *refs[:12], *refs[13:])


def block_backward(pair, blocks, normal, norm_gain, head_gain, filtered, mean, inverse, kernel, after, held=None):
    cells, channels = filtered.shape
    images = cells // CELLS
    some = 2 * CELLS
    dma = pltpu.SemaphoreType.DMA
    operands = [
        *blocks, normal, norm_gain.reshape(1, channels), head_gain.reshape(1, channels),
        filtered, mean, inverse, kernel, after,
    ]
    body = first_backward if held is None else second_backward
    if held is not None:
        operands.append(held)
    return call(
        functools.partial(body, pair),
        ((shape_of((cells, channels), BF16), HBM),),
        tuple((array, HBM) for array in operands),
        "block_backward",
        8,
        scratch=(
            pltpu.VMEM((len(blocks),) + blocks[0].shape, F32),
            pltpu.VMEM(normal.shape, F32),
            pltpu.VMEM((1, channels), F32),
            pltpu.VMEM((1, channels), F32),
            pltpu.VMEM((some, channels), F32),
            pltpu.VMEM((some, LANES), F32),
            pltpu.VMEM((some, LANES), F32),
            pltpu.VMEM(kernel.shape, F32),
            pltpu.VMEM((some, channels), BF16),
            pltpu.VMEM((images, channels), F32),
            pltpu.VMEM((some, LANES), F32),
            pltpu.VMEM((images, channels), F32),
            pltpu.VMEM((images, channels), F32),
            dma((len(blocks),)),
            dma((6,)),
            dma((STEPS,)),
            dma((STEPS,)),
        ),
        grant=BIG,
        aliases={} if held is None else {len(operands) - 1: 0},
    )


def dot(left, right, left_dim, right_dim):
    return lax.dot_general(
        left, right, (((left_dim,), (right_dim,)), ((), ())), preferred_element_type=F32
    )


def inverse_length(values):
    return lax.rsqrt(jnp.sum(values * values, axis=-1, keepdims=True) + EPSILON)


def length_back(unit, inverse, cotangent):
    return inverse * (cotangent - unit * jnp.sum(unit * cotangent, axis=-1, keepdims=True))


def hot_rows(ids_ref, rows):
    row = lax.broadcasted_iota(jnp.int32, (rows, IDS), 0)
    ids = jnp.zeros((rows, IDS), jnp.int32)
    for index in range(rows):
        ids = jnp.where(row == index, ids_ref[index], ids)
    lane = lax.broadcasted_iota(jnp.int32, (rows, IDS), 1)
    return jnp.where(ids == lane, 1.0, 0.0).astype(BF16)


def pack_kernel(text_hbm, ids_hbm, out_ref, text_ref, ids_ref, sems):
    copies = [
        pltpu.make_async_copy(text_hbm, text_ref, sems.at[0]),
        pltpu.make_async_copy(ids_hbm, ids_ref, sems.at[1]),
    ]
    for copy in copies:
        copy.start()
    for copy in copies:
        copy.wait()
    rows, width = text_ref.shape
    text = text_ref[...].astype(F32)
    unit = (text * inverse_length(text)).astype(BF16)
    hot = hot_rows(ids_ref, rows)
    for target in range(out_ref.shape[0]):
        out_ref[target, :, :width] = unit
        out_ref[target, :, width:] = hot


def line_kernel(line_ref, out_ref):
    line, rows, _ = line_ref.shape
    for first in range(0, line, 4):
        four = [line_ref[first + offset].astype(F32) for offset in range(4)]
        at = slice(first * rows, (first + 4) * rows)
        out_ref[at, :] = jnp.concatenate(four, axis=0).astype(BF16)


def join_texts_kernel(own_ref, next_ref, after_ref, out_ref):
    del after_ref
    texts = own_ref.shape[0]
    out_ref[:texts, :] = own_ref[...]
    out_ref[texts:, :] = next_ref[...]


def partial_kernel(received_ref, projection_ref, out_ref, columns_ref, hot_ref):
    group = received_ref.shape[0]
    share = projection_ref.shape[0]
    rows = jnp.concatenate([received_ref[owner].astype(F32) for owner in range(group)], axis=0)
    columns = rows[:, :share].astype(BF16)
    columns_ref[...] = columns
    hot_ref[...] = rows[:, share:].astype(BF16)
    partial = dot(columns, projection_ref[...], 1, 0).astype(BF16)
    for target in range(group):
        out_ref[target] = partial


def pair_kernel(
    partials_ref, hot_ref, projection_ref, t0, t1, t2, t3, t4, t5, t6, t7,
    scale_ref, shift_ref,
    stay_ref, send_ref, factors_ref,
    head_ref,
):
    group, images, width = partials_ref.shape
    blocks = (t0, t1, t2, t3, t4, t5, t6, t7)
    scale, shift = scale_ref[0], shift_ref[0]
    embedded = partials_ref[0].astype(F32)
    for owner in range(1, group):
        embedded += partials_ref[owner].astype(F32)
    inverse = inverse_length(embedded)
    unit = embedded * inverse
    low = unit.astype(BF16)
    factors_ref[:, width : 2 * width] = low
    hot = hot_ref[...]
    weights = []
    for block in blocks:
        logits = scale * dot(low, block[:, :width], 1, 1) + shift
        signs = 2.0 * dot(hot, block[:, width:], 1, 1) - 1.0
        weights.append((-signs * jax.nn.sigmoid(-signs * logits)).astype(BF16))
    image_grad = dot(weights[0], t0[:, :width], 1, 0)
    for weight, block in zip(weights[1:], blocks[1:]):
        image_grad += dot(weight, block[:, :width], 1, 0)
    embed = length_back(unit, inverse, scale * image_grad).astype(BF16)
    factors_ref[:, :width] = embed
    factors_ref[:, 2 * width : 2 * width + LANES] = weights[0]
    factors_ref[:, 2 * width + LANES :] = weights[4]
    head = dot(embed, projection_ref[...], 1, 1)
    rows = images // group
    for owner in range(group):
        head_ref[owner] = head[owner * rows : (owner + 1) * rows]
    x, y_hi = lax.axis_index("x"), lax.axis_index("y_hi")
    for step in range(4):
        stay_ref[step] = head_ref[group_peer(x, y_hi, step, 0)]
        send_ref[step] = head_ref[group_peer(x, y_hi, step, 1)]


def merge_kernel(stay_ref, got_ref, s0, s1, s2, s3):
    for step, out_ref in enumerate((s0, s1, s2, s3)):
        out_ref[0] = stay_ref[step]
        out_ref[1] = got_ref[step]


def strip_make_kernel(mine_ref, theirs_ref, columns_ref, far_columns_ref, out_ref, rows_ref, near_ref, far_ref):
    width = (mine_ref.shape[1] - 2 * LANES) // 2
    line, strip_rows, half = out_ref.shape
    strip = columns_ref.shape[1] // line
    rows = (strip_rows - strip) // 2
    texts = line * rows
    start = pl.multiple_of(lax.axis_index("core") * (width - half), LANES)

    def both(at):
        return jnp.concatenate([mine_ref[:, at], theirs_ref[:, at]], axis=0)

    columns = jnp.concatenate([columns_ref[...], far_columns_ref[...]], axis=0)
    rows_ref[...] = dot(columns, both(pl.ds(start, half)), 0, 0)
    low = both(pl.ds(pl.multiple_of(start + width, LANES), half))
    first = slice(2 * width, 2 * width + texts)
    second = slice(2 * width + LANES, 2 * width + LANES + texts)
    own = jnp.concatenate([mine_ref[:, first], theirs_ref[:, second]], axis=0)
    other = jnp.concatenate([mine_ref[:, second], theirs_ref[:, first]], axis=0)
    near_ref[...] = dot(own, low, 0, 0)
    far_ref[...] = dot(other, low, 0, 0)
    for target in range(line):
        at = slice(target * rows, (target + 1) * rows)
        stacked = jnp.concatenate(
            [rows_ref[target * strip : (target + 1) * strip], near_ref[at], far_ref[at]], axis=0
        )
        out_ref[target] = stacked.astype(BF16)


def strip_kernel(strips_ref, out_ref, mine_ref, theirs_ref):
    line, rows, half = strips_ref.shape
    texts = mine_ref.shape[0]
    strip = rows - 2 * texts
    total = strips_ref[0].astype(F32)
    for source in range(1, line):
        total += strips_ref[source].astype(F32)
    low = total[:strip].astype(BF16)
    for target in range(line):
        out_ref[target] = low
    mine_ref[...] = total[strip : strip + texts]
    theirs_ref[...] = total[strip + texts :]


def text_kernel(text_ref, mine_ref, got_ref, scale_ref, out_ref):
    width = text_ref.shape[1]
    text = text_ref[...].astype(F32)
    inverse = inverse_length(text)
    first = lax.axis_index("core") == 0
    mine, got = mine_ref[...], got_ref[...]
    left = jnp.where(first, mine, got)
    right = jnp.where(first, got, mine)
    grad = jnp.concatenate([left, right[:, 2 * HALF - width :]], axis=1)
    out_ref[...] = length_back(text * inverse, inverse, scale_ref[0] * grad)


def join_kernel(near_ref, far_ref, out_ref):
    core = lax.axis_index("core")
    width = out_ref.shape[1]

    def put(left, right):
        out_ref[:, :HALF] = left[...].astype(F32)
        out_ref[:, HALF:] = right[:, 2 * HALF - width :].astype(F32)

    pl.when(core == 0)(lambda: put(near_ref, far_ref))
    pl.when(core != 0)(lambda: put(far_ref, near_ref))


def exchange(blocks, axes):
    return lax.all_to_all(blocks, axes, 0, 0, tiled=True)


def swap_core(block):
    return lax.ppermute(block, "core", ((0, 1), (1, 0)))


def along_x(block, step):
    return lax.ppermute(block, "x", tuple((i, (i + step) % 4) for i in range(4)))


def local(
    features,
    text_embed,
    img_ids,
    txt_ids,
    kernel,
    norm_gain,
    head_gain,
    projection,
    logit_scale,
    logit_bias,
):
    rows, width = text_embed.shape
    share = projection.shape[0]
    group = lax.axis_size(GROUP)
    line = lax.axis_size(LINE)
    images = group * rows
    texts = line * rows
    strip = share // line
    dma = pltpu.SemaphoreType.DMA

    packed = call(
        pack_kernel,
        ((shape_of((line, rows, width + IDS), BF16), VMEM),),
        ((text_embed, HBM), (txt_ids, HBM)),
        "text_pack", 1,
        scratch=(
            pltpu.VMEM((rows, width), BF16), pltpu.SMEM((rows,), jnp.int32), dma((2,)),
        ),
        grant=BIG,
    )
    gathered = exchange(packed, LINE)
    filtered, mean, inverse, normal, send = block_forward(
        features, kernel, norm_gain, head_gain, img_ids, group
    )
    gathered, send = lax.optimization_barrier((gathered, send))
    received = exchange(send, GROUP)
    partials, columns, hot = call(
        partial_kernel,
        (
            (shape_of((group, images, width), BF16), VMEM),
            (shape_of((images, share), BF16), VMEM),
            (shape_of((images, IDS), BF16), VMEM),
        ),
        ((received, VMEM), (projection, VMEM)),
        "partial_embed", 2,
    )
    own_line = call(
        line_kernel, ((shape_of((texts, width + IDS), BF16), VMEM),), ((gathered, VMEM),),
        "line_rows", 1,
    )
    next_line = lax.ppermute(own_line, "y_hi", ((0, 1), (1, 0)))
    near = [
        call(
            join_texts_kernel,
            ((shape_of((2 * texts, width + IDS), BF16), VMEM),),
            ((own_line, VMEM), (next_line, VMEM), (columns, VMEM)),
            "join_texts", 1,
        )
    ]
    near += [along_x(near[0], step) for step in (1, 3, 2)]
    far = [swap_core(block) for block in near]
    far_columns = swap_core(columns)
    partials = exchange(partials, GROUP)
    stay, away, factors = call(
        pair_kernel,
        (
            (shape_of((4, rows, share), F32), VMEM),
            (shape_of((4, rows, share), F32), VMEM),
            (shape_of((images, 2 * width + 2 * LANES), BF16), VMEM),
        ),
        tuple((array, VMEM) for array in (partials, hot, projection, *near, *far))
        + ((logit_scale, SMEM), (logit_bias, SMEM)),
        "pairs", 4,
        scratch=(pltpu.VMEM((group, rows, share), F32),),
    )
    far_factors = swap_core(factors)
    got = lax.ppermute(away, "y_hi", ((0, 1), (1, 0)))
    strips = call(
        strip_make_kernel,
        ((shape_of((line, strip + 2 * rows, HALF), BF16), VMEM),),
        tuple((array, VMEM) for array in (factors, far_factors, columns, far_columns)),
        "strip_make", 2,
        scratch=(
            pltpu.VMEM((share, HALF), F32),
            pltpu.VMEM((texts, HALF), F32),
            pltpu.VMEM((texts, HALF), F32),
        ),
    )
    strips = exchange(strips, LINE)
    merged = call(
        merge_kernel,
        ((shape_of((2, rows, share), F32), VMEM),) * 4,
        ((stay, VMEM), (got, VMEM)),
        "head_merge", 1,
    )
    blocks = [merged[0]] + [along_x(merged[step], step) for step in (1, 2, 3)]
    shared = (normal, norm_gain, head_gain, filtered, mean, inverse, kernel)
    held = block_backward(0, blocks, *shared, mean)
    strips, held = lax.optimization_barrier((strips, held))
    sums, mine, theirs = call(
        strip_kernel,
        (
            (shape_of((line, strip, HALF), BF16), VMEM),
            (shape_of((rows, HALF), F32), VMEM),
            (shape_of((rows, HALF), F32), VMEM),
        ),
        ((strips, VMEM),),
        "strip_sum", 1,
    )
    near_half = exchange(sums, LINE).reshape(share, HALF)
    grad_text = call(
        text_kernel,
        ((shape_of((rows, width), F32), VMEM),),
        ((text_embed, VMEM), (mine, VMEM), (swap_core(theirs), VMEM), (logit_scale, SMEM)),
        "text_grad", 1,
    )
    grad_features = block_backward(1, blocks, *shared, mine, held)
    near_half, grad_features, grad_text = lax.optimization_barrier(
        (near_half, grad_features, grad_text)
    )
    grad_proj = call(
        join_kernel,
        ((shape_of((share, width), F32), VMEM),),
        ((near_half, VMEM), (swap_core(near_half), VMEM)),
        "proj_join", 2,
    )
    grad_features = grad_features.reshape(features.shape)
    return (grad_features, grad_text, grad_proj)


def solution(mesh):
    fine = Mesh(mesh.devices.reshape(SIZES), AXES)
    placed = (
        P(ALL, None, None, None),
        P(ALL, None),
        P(ALL),
        P(ALL),
        P(),
        P(),
        P(),
        P(GROUP, None),
        P(),
        P(),
    )
    return jax.shard_map(
        local,
        mesh=fine,
        in_specs=placed,
        out_specs=(P(ALL, None, None, None), P(ALL, None), P(GROUP, None)),
        check_vma=False,
    )
```

```python
import functools

import jax
import jax.numpy as jnp
from jax import lax
from jax.experimental import pallas as pl
from jax.experimental.pallas import tpu as pltpu
from jax.sharding import Mesh, PartitionSpec as P

EPSILON = 1e-06
AXES = ("y_lo", "z", "core", "x", "y_hi")
SIZES = (2, 8, 2, 4, 2)
ALL = AXES
GROUP = ("x", "y_hi")
LINE = ("y_lo", "z")
MIB = 1024 * 1024
BIG = 60
IDS = 128
HALF = 640
LANES = 128
SIDE = 8
CELLS = 64
TAPS = 7
VMEM = pl.BlockSpec(memory_space=pltpu.VMEM)
SMEM = pl.BlockSpec(memory_space=pltpu.SMEM)
HBM = pl.BlockSpec(memory_space=pltpu.HBM)
STEPS = 4
PEERS = tuple((step_x, step_y) for step_x in range(4) for step_y in range(2))
BF16 = jnp.bfloat16
F32 = jnp.float32


def shape_of(dims, dtype):
    return jax.ShapeDtypeStruct(dims, dtype)


def call(body, outs, operands, name, micros, scratch=(), grant=40, aliases=None):
    specs = tuple(spec for _, spec in outs)
    shapes = tuple(shape for shape, _ in outs)
    single = len(outs) == 1
    return pl.pallas_call(
        body,
        out_shape=shapes[0] if single else shapes,
        in_specs=[spec for _, spec in operands],
        out_specs=specs[0] if single else specs,
        scratch_shapes=list(scratch),
        compiler_params=pltpu.CompilerParams(vmem_limit_bytes=grant * MIB),
        cost_estimate=pl.CostEstimate(
            flops=0, bytes_accessed=int(micros * 3e6), transcendentals=0
        ),
        input_output_aliases=aliases or {},
        name=name,
    )(*[operand for operand, _ in operands])


def group_peer(x, y_hi, step_x, step_y):
    return lax.rem(x + step_x, 4) * 2 + lax.rem(y_hi + step_y, 2)


def tap_weights(kernel_ref, at, column, flip):
    place = lax.broadcasted_iota(jnp.int32, (SIDE, LANES), 0) + (column - TAPS // 2)
    valid = (place >= 0) & (place < SIDE)
    weights = []
    for row in range(TAPS):
        if flip:
            line = kernel_ref[TAPS - 1 - row, pl.ds(TAPS - 1 - column, 1), at]
        else:
            line = kernel_ref[row, pl.ds(column, 1), at]
        weights.append(jnp.where(valid, jnp.broadcast_to(line, (SIDE, LANES)), 0.0))
    return weights


def filter_rows(fields, sums, kernel_ref, at, flip):
    for column in range(TAPS):
        weights = tap_weights(kernel_ref, at, column, flip)
        shift = (TAPS // 2 - column) % SIDE
        for field, total in zip(fields, sums):
            for source in range(SIDE):
                moved = field[source] if shift == 0 else pltpu.roll(field[source], shift, 0)
                for row in range(TAPS):
                    target = source - row + TAPS // 2
                    if 0 <= target < SIDE:
                        term = moved * weights[row]
                        total[target] = term if total[target] is None else total[target] + term
    return sums


def forward_kernel(
    field_hbm, kernel_hbm, gain_hbm, head_gain_hbm, ids_hbm,
    filtered_hbm, mean_ref, inverse_ref, normal_ref, send_ref,
    field_ref, kernel_ref, gain_ref, head_gain_ref, ids_ref, filtered_ref, pooled_ref, total_ref,
    field_sems, kernel_sems, small_sems, out_sems,
):
    images = field_ref.shape[0] // CELLS
    channels = field_ref.shape[1]
    chunks = channels // LANES
    part = 1.0 / channels
    block = channels // STEPS
    per_block = chunks // STEPS

    def block_at(step):
        return pl.ds(pl.multiple_of(step * block, LANES), block)

    def field_copy(step):
        at = block_at(step)
        return pltpu.make_async_copy(field_hbm.at[:, at], field_ref.at[:, at], field_sems.at[step])

    def kernel_copy(step):
        at = block_at(step)
        return pltpu.make_async_copy(
            kernel_hbm.at[:, :, at], kernel_ref.at[:, :, at], kernel_sems.at[step]
        )

    def filtered_copy(step):
        at = block_at(step)
        return pltpu.make_async_copy(filtered_ref.at[:, at], filtered_hbm.at[:, at], out_sems.at[step])

    small_copies = [
        pltpu.make_async_copy(gain_hbm, gain_ref, small_sems.at[0]),
        pltpu.make_async_copy(head_gain_hbm, head_gain_ref, small_sems.at[1]),
        pltpu.make_async_copy(ids_hbm, ids_ref, small_sems.at[2]),
    ]
    for step in range(STEPS):
        field_copy(step).start()
        kernel_copy(step).start()
    for copy in small_copies:
        copy.start()

    total_ref[...] = jnp.zeros_like(total_ref)

    def filter_chunk(chunk, carry):
        step = chunk // per_block

        @pl.when(chunk == step * per_block)
        def _():
            field_copy(step).wait()
            kernel_copy(step).wait()

        at = pl.ds(pl.multiple_of(chunk * LANES, LANES), LANES)
        for first in range(0, images, 2):
            fields = []
            for image in range(first, first + 2):
                rows = []
                for pair in range(SIDE // 2):
                    both = field_ref[pl.ds(image * CELLS + pair * 2 * SIDE, 2 * SIDE), at]
                    both = both.astype(jnp.float32)
                    rows += [both[:SIDE], both[SIDE:]]
                fields.append(rows)
            sums = [[None] * SIDE for _ in fields]
            filter_rows(fields, sums, kernel_ref, at, False)
            for offset, total in enumerate(sums):
                for row in range(SIDE):
                    cells = pl.ds((first + offset) * CELLS + row * SIDE, SIDE)
                    filtered_ref[cells, at] = total[row]
                    total_ref[cells, :] += total[row]
        return carry

    lax.fori_loop(0, chunks, filter_chunk, 0)
    for step in range(STEPS):
        filtered_copy(step).start()
    for copy in small_copies:
        copy.wait()
    mean_ref[...] = jnp.broadcast_to(
        jnp.sum(total_ref[...], axis=1, keepdims=True) * part, mean_ref.shape
    )

    for image in range(images):
        cells = pl.ds(image * CELLS, CELLS)
        average = mean_ref[cells, :]

        def spread_chunk(chunk, squares):
            at = pl.ds(pl.multiple_of(chunk * LANES, LANES), LANES)
            centred = filtered_ref[cells, at] - average
            return squares + centred * centred

        squares = lax.fori_loop(
            0, chunks, spread_chunk, jnp.zeros((CELLS, LANES), jnp.float32), unroll=4
        )
        spread = jnp.sum(squares, axis=1, keepdims=True) * part
        inverse_ref[cells, :] = jnp.broadcast_to(lax.rsqrt(spread + EPSILON), (CELLS, LANES))

    for image in range(images):
        cells = pl.ds(image * CELLS, CELLS)
        average = mean_ref[cells, :]
        inverse = inverse_ref[cells, :]

        def pool_chunk(chunk, carry):
            at = pl.ds(pl.multiple_of(chunk * LANES, LANES), LANES)
            normal = (filtered_ref[cells, at] - average) * inverse
            mixed = field_ref[cells, at].astype(jnp.float32) + normal * gain_ref[:, at]
            pooled_ref[pl.ds(image, 1), at] = jnp.sum(mixed, axis=0, keepdims=True) * (1.0 / CELLS)
            return carry

        lax.fori_loop(0, chunks, pool_chunk, 0, unroll=2)

    pooled = pooled_ref[...]
    centred = pooled - jnp.sum(pooled, axis=1, keepdims=True) * part
    spread = jnp.sum(centred * centred, axis=1, keepdims=True) * part
    head_inverse = lax.rsqrt(spread + EPSILON)
    normal = centred * head_inverse
    normal_ref[:, :channels] = normal
    normal_ref[:, channels:] = jnp.broadcast_to(head_inverse, (images, LANES))
    head_input = (normal * head_gain_ref[...]).astype(jnp.bfloat16)
    hot = hot_rows(ids_ref, images)
    group = send_ref.shape[0]
    share = channels // group
    for owner in range(group):
        send_ref[owner, :, :share] = head_input[:, owner * share : (owner + 1) * share]
        send_ref[owner, :, share:] = hot
    for step in range(STEPS):
        filtered_copy(step).wait()


def block_forward(features, kernel, norm_gain, head_gain, img_ids, group):
    images, channels = features.shape[0], features.shape[3]
    cells = images * CELLS
    dma = pltpu.SemaphoreType.DMA
    return call(
        forward_kernel,
        (
            (shape_of((cells, channels), F32), HBM),
            (shape_of((cells, LANES), F32), VMEM),
            (shape_of((cells, LANES), F32), VMEM),
            (shape_of((images, channels + LANES), F32), VMEM),
            (shape_of((group, images, channels // group + IDS), BF16), VMEM),
        ),
        (
            (features.reshape(cells, channels), HBM),
            (kernel, HBM),
            (norm_gain.reshape(1, channels), HBM),
            (head_gain.reshape(1, channels), HBM),
            (img_ids, HBM),
        ),
        "block_forward",
        14,
        scratch=(
            pltpu.VMEM((cells, channels), BF16),
            pltpu.VMEM(kernel.shape, F32),
            pltpu.VMEM((1, channels), F32),
            pltpu.VMEM((1, channels), F32),
            pltpu.SMEM(img_ids.shape, jnp.int32),
            pltpu.VMEM((cells, channels), F32),
            pltpu.VMEM((images, channels), F32),
            pltpu.VMEM((cells, LANES), F32),
            dma((STEPS,)),
            dma((STEPS,)),
            dma((3,)),
            dma((STEPS,)),
        ),
        grant=BIG,
    )


def backward_kernel(
    pair, s0, s1, s2, s3, normal_hbm, gain_hbm, head_gain_hbm,
    filtered_hbm, mean_hbm, inverse_hbm, kernel_hbm, after_hbm,
    out_hbm,
    blocks_ref, normal_ref, gain_ref, head_gain_ref, filtered_ref, mean_ref, inverse_ref, kernel_ref,
    out_ref, even_ref, lean_ref, pull_ref, tilt_ref,
    block_sems, small_sems, filtered_sems, out_sems,
):
    del after_hbm
    images, channels = even_ref.shape
    blocks = (s0, s1, s2, s3)
    share = channels // len(PEERS)
    cells = pl.ds(pair * 2 * CELLS, 2 * CELLS)
    wide = channels // STEPS

    def block_at(step):
        return pl.ds(pl.multiple_of(step * wide, LANES), wide)

    def out_copy(step):
        at = block_at(step)
        return pltpu.make_async_copy(out_ref.at[:, at], out_hbm.at[cells, at], out_sems.at[step])

    head_copies = [
        pltpu.make_async_copy(block, blocks_ref.at[index], block_sems.at[index])
        for index, block in enumerate(blocks)
    ]
    small_copies = [
        pltpu.make_async_copy(source, target, small_sems.at[index])
        for index, (source, target) in enumerate((
            (head_gain_hbm, head_gain_ref), (gain_hbm, gain_ref), (normal_hbm, normal_ref),
            (mean_hbm.at[cells, :], mean_ref), (inverse_hbm.at[cells, :], inverse_ref),
        ))
    ]
    filtered_copies = [
        pltpu.make_async_copy(
            filtered_hbm.at[cells, block_at(step)], filtered_ref.at[:, block_at(step)],
            filtered_sems.at[step],
        )
        for step in range(STEPS)
    ]
    kernel_copy = pltpu.make_async_copy(kernel_hbm, kernel_ref, small_sems.at[5])
    for copy in (*head_copies, *small_copies, *filtered_copies, kernel_copy):
        copy.start()
    chunks = channels // LANES
    per_block = chunks // STEPS
    part = 1.0 / channels

    for copy in (*head_copies, *small_copies):
        copy.wait()
    x, y_hi = lax.axis_index("x"), lax.axis_index("y_hi")
    for step_x, step_y in PEERS:
        owner = group_peer(x, y_hi, 4 - step_x, step_y)
        at = pl.ds(pl.multiple_of(owner * share, LANES), share)
        tilt_ref[:, at] = blocks_ref[step_x, step_y] * head_gain_ref[:, at]
    cotangent = tilt_ref[...]
    normal = normal_ref[:, :channels]
    level = jnp.sum(cotangent, axis=1, keepdims=True) * part
    lean = jnp.sum(cotangent * normal, axis=1, keepdims=True) * part
    pooled_grad = normal_ref[:, channels : channels + 1] * (cotangent - level - normal * lean)
    even = pooled_grad * (1.0 / CELLS)
    even_ref[...] = even
    pull = even * gain_ref[...]
    pull_ref[...] = pull
    tilt_ref[...] = pull - jnp.sum(pull, axis=1, keepdims=True) * part

    for step in range(STEPS):
        filtered_copies[step].wait()
        for image in range(2):
            spot = pl.ds(image * CELLS, CELLS)
            average = mean_ref[spot, :]

            def lean_chunk(chunk, total, spot=spot, average=average, image=image):
                at = pl.ds(pl.multiple_of(chunk * LANES, LANES), LANES)
                return total + (filtered_ref[spot, at] - average) * pull_ref[pl.ds(2 * pair + image, 1), at]

            total = jnp.zeros((CELLS, LANES), F32) if step == 0 else lean_ref[spot, :]
            lean_ref[spot, :] = lax.fori_loop(
                step * per_block, (step + 1) * per_block, lean_chunk, total, unroll=True
            )
    inverse = inverse_ref[...]
    mean_lean = jnp.sum(lean_ref[...], axis=1, keepdims=True) * part
    lean_ref[...] = inverse * (inverse * (inverse * mean_lean))
    kernel_copy.wait()

    def filter_chunk(chunk, carry):
        at = pl.ds(pl.multiple_of(chunk * LANES, LANES), LANES)
        fields = []
        sums = []
        for image in range(2):
            source = pl.ds(2 * pair + image, 1)
            tilt = jnp.broadcast_to(tilt_ref[source, at], (SIDE, LANES))
            even = jnp.broadcast_to(even_ref[source, at], (SIDE, LANES))
            rows = []
            for row in range(SIDE):
                spot = pl.ds(image * CELLS + row * SIDE, SIDE)
                rows.append(
                    inverse_ref[spot, :] * tilt
                    - lean_ref[spot, :] * (filtered_ref[spot, at] - mean_ref[spot, :])
                )
            fields.append(rows)
            sums.append([even] * SIDE)
        filter_rows(fields, sums, kernel_ref, at, True)
        for image, total in enumerate(sums):
            for half in range(SIDE // 2):
                two = jnp.concatenate(total[2 * half : 2 * half + 2], axis=0)
                spot = pl.ds(image * CELLS + half * 2 * SIDE, 2 * SIDE)
                out_ref[spot, at] = two.astype(jnp.bfloat16)
        step = chunk // per_block

        @pl.when(chunk == step * per_block + per_block - 1)
        def _():
            out_copy(step).start()

        return carry

    lax.fori_loop(0, chunks, filter_chunk, 0)
    for step in range(STEPS):
        out_copy(step).wait()


def first_backward(pair, *refs):
    backward_kernel(pair, *refs)


def second_backward(pair, *refs):
    backward_kernel(pair, *refs[:12], *refs[13:])


def block_backward(pair, blocks, normal, norm_gain, head_gain, filtered, mean, inverse, kernel, after, held=None):
    cells, channels = filtered.shape
    images = cells // CELLS
    some = 2 * CELLS
    dma = pltpu.SemaphoreType.DMA
    operands = [
        *blocks, normal, norm_gain.reshape(1, channels), head_gain.reshape(1, channels),
        filtered, mean, inverse, kernel, after,
    ]
    body = first_backward if held is None else second_backward
    if held is not None:
        operands.append(held)
    return call(
        functools.partial(body, pair),
        ((shape_of((cells, channels), BF16), HBM),),
        tuple((array, HBM) for array in operands),
        "block_backward",
        8,
        scratch=(
            pltpu.VMEM((len(blocks),) + blocks[0].shape, F32),
            pltpu.VMEM(normal.shape, F32),
            pltpu.VMEM((1, channels), F32),
            pltpu.VMEM((1, channels), F32),
            pltpu.VMEM((some, channels), F32),
            pltpu.VMEM((some, LANES), F32),
            pltpu.VMEM((some, LANES), F32),
            pltpu.VMEM(kernel.shape, F32),
            pltpu.VMEM((some, channels), BF16),
            pltpu.VMEM((images, channels), F32),
            pltpu.VMEM((some, LANES), F32),
            pltpu.VMEM((images, channels), F32),
            pltpu.VMEM((images, channels), F32),
            dma((len(blocks),)),
            dma((6,)),
            dma((STEPS,)),
            dma((STEPS,)),
        ),
        grant=BIG,
        aliases={} if held is None else {len(operands) - 1: 0},
    )


def dot(left, right, left_dim, right_dim):
    return lax.dot_general(
        left, right, (((left_dim,), (right_dim,)), ((), ())), preferred_element_type=F32
    )


def inverse_length(values):
    return lax.rsqrt(jnp.sum(values * values, axis=-1, keepdims=True) + EPSILON)


def length_back(unit, inverse, cotangent):
    return inverse * (cotangent - unit * jnp.sum(unit * cotangent, axis=-1, keepdims=True))


def hot_rows(ids_ref, rows):
    row = lax.broadcasted_iota(jnp.int32, (rows, IDS), 0)
    ids = jnp.zeros((rows, IDS), jnp.int32)
    for index in range(rows):
        ids = jnp.where(row == index, ids_ref[index], ids)
    lane = lax.broadcasted_iota(jnp.int32, (rows, IDS), 1)
    return jnp.where(ids == lane, 1.0, 0.0).astype(BF16)


def pack_kernel(text_hbm, ids_hbm, out_ref, text_ref, ids_ref, sems):
    copies = [
        pltpu.make_async_copy(text_hbm, text_ref, sems.at[0]),
        pltpu.make_async_copy(ids_hbm, ids_ref, sems.at[1]),
    ]
    for copy in copies:
        copy.start()
    for copy in copies:
        copy.wait()
    rows, width = text_ref.shape
    text = text_ref[...].astype(F32)
    unit = (text * inverse_length(text)).astype(BF16)
    hot = hot_rows(ids_ref, rows)
    for target in range(out_ref.shape[0]):
        out_ref[target, :, :width] = unit
        out_ref[target, :, width:] = hot


def line_kernel(line_ref, out_ref):
    line, rows, _ = line_ref.shape
    for first in range(0, line, 4):
        four = [line_ref[first + offset].astype(F32) for offset in range(4)]
        at = slice(first * rows, (first + 4) * rows)
        out_ref[at, :] = jnp.concatenate(four, axis=0).astype(BF16)


def join_texts_kernel(own_ref, next_ref, after_ref, out_ref):
    del after_ref
    texts = own_ref.shape[0]
    out_ref[:texts, :] = own_ref[...]
    out_ref[texts:, :] = next_ref[...]


def partial_kernel(received_ref, projection_ref, out_ref, columns_ref, hot_ref):
    group = received_ref.shape[0]
    share = projection_ref.shape[0]
    rows = jnp.concatenate([received_ref[owner].astype(F32) for owner in range(group)], axis=0)
    columns = rows[:, :share].astype(BF16)
    columns_ref[...] = columns
    hot_ref[...] = rows[:, share:].astype(BF16)
    partial = dot(columns, projection_ref[...], 1, 0).astype(BF16)
    for target in range(group):
        out_ref[target] = partial


def pair_kernel(
    partials_ref, columns_ref, hot_ref, projection_ref, t0, t1, t2, t3, t4, t5, t6, t7,
    scale_ref, shift_ref,
    stay_ref, send_ref, factors_ref,
    head_ref,
):
    group, images, width = partials_ref.shape
    blocks = (t0, t1, t2, t3, t4, t5, t6, t7)
    scale, shift = scale_ref[0], shift_ref[0]
    embedded = partials_ref[0].astype(F32)
    for owner in range(1, group):
        embedded += partials_ref[owner].astype(F32)
    inverse = inverse_length(embedded)
    unit = embedded * inverse
    low = unit.astype(BF16)
    factors_ref[:, width : 2 * width] = low
    hot = hot_ref[...]
    weights = []
    for block in blocks:
        logits = scale * dot(low, block[:, :width], 1, 1) + shift
        signs = 2.0 * dot(hot, block[:, width:], 1, 1) - 1.0
        weights.append((-signs * jax.nn.sigmoid(-signs * logits)).astype(BF16))
    image_grad = dot(weights[0], t0[:, :width], 1, 0)
    for weight, block in zip(weights[1:], blocks[1:]):
        image_grad += dot(weight, block[:, :width], 1, 0)
    embed = length_back(unit, inverse, scale * image_grad).astype(BF16)
    factors_ref[:, :width] = embed
    factors_ref[:, 2 * width : 2 * width + LANES] = weights[0]
    factors_ref[:, 2 * width + LANES : 2 * width + 2 * LANES] = weights[4]
    factors_ref[:, 2 * width + 2 * LANES :] = columns_ref[...]
    head = dot(embed, projection_ref[...], 1, 1)
    rows = images // group
    for owner in range(group):
        head_ref[owner] = head[owner * rows : (owner + 1) * rows]
    x, y_hi = lax.axis_index("x"), lax.axis_index("y_hi")
    for step in range(4):
        stay_ref[step] = head_ref[group_peer(x, y_hi, step, 0)]
        send_ref[step] = head_ref[group_peer(x, y_hi, step, 1)]


def merge_kernel(stay_ref, got_ref, s0, s1, s2, s3):
    for step, out_ref in enumerate((s0, s1, s2, s3)):
        out_ref[0] = stay_ref[step]
        out_ref[1] = got_ref[step]


def strip_make_kernel(mine_ref, core_ref, side_ref, both_ref, out_ref, rows_ref, near_ref, far_ref):
    line, strip_rows, half = out_ref.shape
    share = rows_ref.shape[0]
    strip = share // 2 // line
    width = (mine_ref.shape[1] - share - 2 * LANES) // 2
    rows = (strip_rows - strip) // 2
    texts = 2 * line * rows
    start = pl.multiple_of(lax.axis_index("core") * (width - half), LANES)
    y_lo = lax.axis_index("y_lo")
    first = slice(2 * width, 2 * width + texts)
    second = slice(2 * width + LANES, 2 * width + LANES + texts)

    def stack(near_at, far_at):
        return jnp.concatenate(
            [mine_ref[:, near_at], side_ref[:, near_at], core_ref[:, far_at], both_ref[:, far_at]],
            axis=0,
        )

    columns = stack(slice(2 * width + 2 * LANES, None), slice(2 * width + 2 * LANES, None))
    at = pl.ds(start, half)
    rows_ref[...] = dot(columns, stack(at, at), 0, 0)
    at = pl.ds(pl.multiple_of(start + width, LANES), half)
    low = stack(at, at)
    near = dot(stack(first, second), low, 0, 0)
    far = dot(stack(second, first), low, 0, 0)
    for side in range(2):
        at = slice(side * texts // 2, (side + 1) * texts // 2)
        near_ref[side] = near[at]
        far_ref[side] = far[at]
    for target in range(line):
        at = slice(target * rows, (target + 1) * rows)
        stacked = jnp.concatenate(
            [
                rows_ref[pl.ds(pl.multiple_of(y_lo * (share // 2) + target * strip, 8), strip), :],
                near_ref[y_lo, at],
                far_ref[y_lo, at],
            ],
            axis=0,
        )
        out_ref[target] = stacked.astype(BF16)


def strip_kernel(strips_ref, out_ref, mine_ref, theirs_ref):
    line, rows, half = strips_ref.shape
    texts = mine_ref.shape[0]
    strip = rows - 2 * texts
    total = strips_ref[0].astype(F32)
    for source in range(1, line):
        total += strips_ref[source].astype(F32)
    low = total[:strip].astype(BF16)
    for target in range(line):
        out_ref[target] = low
    mine_ref[...] = total[strip : strip + texts]
    theirs_ref[...] = total[strip + texts :]


def text_kernel(text_ref, mine_ref, got_ref, scale_ref, out_ref):
    width = text_ref.shape[1]
    text = text_ref[...].astype(F32)
    inverse = inverse_length(text)
    first = lax.axis_index("core") == 0
    mine, got = mine_ref[...], got_ref[...]
    left = jnp.where(first, mine, got)
    right = jnp.where(first, got, mine)
    grad = jnp.concatenate([left, right[:, 2 * HALF - width :]], axis=1)
    out_ref[...] = length_back(text * inverse, inverse, scale_ref[0] * grad)


def join_kernel(mine_ref, side_ref, core_ref, both_ref, out_ref):
    width = out_ref.shape[1]
    rows = mine_ref.shape[0]
    core = lax.axis_index("core")
    y_lo = lax.axis_index("y_lo")

    def put(row, left, right):
        at = pl.ds(pl.multiple_of(row * rows, 16), rows)
        out_ref[at, :HALF] = left[...].astype(F32)
        out_ref[at, HALF:] = right[:, 2 * HALF - width :].astype(F32)

    @pl.when(core == 0)
    def _():
        put(y_lo, mine_ref, core_ref)
        put(1 - y_lo, side_ref, both_ref)

    @pl.when(core != 0)
    def _():
        put(y_lo, core_ref, mine_ref)
        put(1 - y_lo, both_ref, side_ref)


def exchange(blocks, axes):
    return lax.all_to_all(blocks, axes, 0, 0, tiled=True)


def swap_core(block):
    return lax.ppermute(block, "core", ((0, 1), (1, 0)))


def swap_side(block):
    return lax.ppermute(block, "y_lo", ((0, 1), (1, 0)))


def swap_both(block):
    return lax.ppermute(block, ("y_lo", "core"), tuple((i, 3 - i) for i in range(4)))


def along_x(block, step):
    return lax.ppermute(block, "x", tuple((i, (i + step) % 4) for i in range(4)))


def local(
    features,
    text_embed,
    img_ids,
    txt_ids,
    kernel,
    norm_gain,
    head_gain,
    projection,
    logit_scale,
    logit_bias,
):
    rows, width = text_embed.shape
    share = projection.shape[0]
    group = lax.axis_size(GROUP)
    line = lax.axis_size(LINE)
    images = group * rows
    texts = line * rows
    strip = share // line
    dma = pltpu.SemaphoreType.DMA

    packed = call(
        pack_kernel,
        ((shape_of((line, rows, width + IDS), BF16), VMEM),),
        ((text_embed, HBM), (txt_ids, HBM)),
        "text_pack", 1,
        scratch=(
            pltpu.VMEM((rows, width), BF16), pltpu.SMEM((rows,), jnp.int32), dma((2,)),
        ),
        grant=BIG,
    )
    gathered = exchange(packed, LINE)
    filtered, mean, inverse, normal, send = block_forward(
        features, kernel, norm_gain, head_gain, img_ids, group
    )
    gathered, send = lax.optimization_barrier((gathered, send))
    received = exchange(send, GROUP)
    partials, columns, hot = call(
        partial_kernel,
        (
            (shape_of((group, images, width), BF16), VMEM),
            (shape_of((images, share), BF16), VMEM),
            (shape_of((images, IDS), BF16), VMEM),
        ),
        ((received, VMEM), (projection, VMEM)),
        "partial_embed", 2,
    )
    own_line = call(
        line_kernel, ((shape_of((texts, width + IDS), BF16), VMEM),), ((gathered, VMEM),),
        "line_rows", 1,
    )
    next_line = lax.ppermute(own_line, "y_hi", ((0, 1), (1, 0)))
    near = [
        call(
            join_texts_kernel,
            ((shape_of((2 * texts, width + IDS), BF16), VMEM),),
            ((own_line, VMEM), (next_line, VMEM), (columns, VMEM)),
            "join_texts", 1,
        )
    ]
    near += [along_x(near[0], step) for step in (1, 3, 2)]
    far = [swap_core(block) for block in near]
    partials = exchange(partials, GROUP)
    stay, away, factors = call(
        pair_kernel,
        (
            (shape_of((4, rows, share), F32), VMEM),
            (shape_of((4, rows, share), F32), VMEM),
            (shape_of((images, 2 * width + 2 * LANES + share), BF16), VMEM),
        ),
        tuple((array, VMEM) for array in (partials, columns, hot, projection, *near, *far))
        + ((logit_scale, SMEM), (logit_bias, SMEM)),
        "pairs", 4,
        scratch=(pltpu.VMEM((group, rows, share), F32),),
    )
    factors = (factors, swap_core(factors), swap_side(factors), swap_both(factors))
    got = lax.ppermute(away, "y_hi", ((0, 1), (1, 0)))
    ring = lax.axis_size("z")
    strip = share // 2 // ring
    strips = call(
        strip_make_kernel,
        ((shape_of((ring, strip + 2 * rows, HALF), BF16), VMEM),),
        tuple((array, VMEM) for array in factors),
        "strip_make", 2,
        scratch=(
            pltpu.VMEM((share, HALF), F32),
            pltpu.VMEM((2, texts // 2, HALF), F32),
            pltpu.VMEM((2, texts // 2, HALF), F32),
        ),
    )
    strips = exchange(strips, "z")
    merged = call(
        merge_kernel,
        ((shape_of((2, rows, share), F32), VMEM),) * 4,
        ((stay, VMEM), (got, VMEM)),
        "head_merge", 1,
    )
    blocks = [merged[0]] + [along_x(merged[step], step) for step in (1, 2, 3)]
    shared = (normal, norm_gain, head_gain, filtered, mean, inverse, kernel)
    strips, *blocks = lax.optimization_barrier((strips, *blocks))
    sums, mine, theirs = call(
        strip_kernel,
        (
            (shape_of((ring, strip, HALF), BF16), VMEM),
            (shape_of((rows, HALF), F32), VMEM),
            (shape_of((rows, HALF), F32), VMEM),
        ),
        ((strips, VMEM),),
        "strip_sum", 1,
    )
    quarter = exchange(sums, "z").reshape(share // 2, HALF)
    held = block_backward(0, blocks, *shared, mine)
    grad_text = call(
        text_kernel,
        ((shape_of((rows, width), F32), VMEM),),
        ((text_embed, VMEM), (mine, VMEM), (swap_core(theirs), VMEM), (logit_scale, SMEM)),
        "text_grad", 1,
    )
    quarter, held = lax.optimization_barrier((quarter, held))
    side = swap_side(quarter)
    grad_features = block_backward(1, blocks, *shared, quarter, held)
    side, grad_features, grad_text = lax.optimization_barrier((side, grad_features, grad_text))
    grad_proj = call(
        join_kernel,
        ((shape_of((share, width), F32), VMEM),),
        ((quarter, VMEM), (side, VMEM), (swap_core(quarter), VMEM), (swap_core(side), VMEM)),
        "proj_join", 2,
    )
    grad_features = grad_features.reshape(features.shape)
    return (grad_features, grad_text, grad_proj)


def solution(mesh):
    fine = Mesh(mesh.devices.reshape(SIZES), AXES)
    placed = (
        P(ALL, None, None, None),
        P(ALL, None),
        P(ALL),
        P(ALL),
        P(),
        P(),
        P(),
        P(GROUP, None),
        P(),
        P(),
    )
    return jax.shard_map(
        local,
        mesh=fine,
        in_specs=placed,
        out_specs=(P(ALL, None, None, None), P(ALL, None), P(GROUP, None)),
        check_vma=False,
    )
```

```python
import jax
import jax.numpy as jnp
from jax import lax
from jax.experimental import pallas as pl
from jax.experimental.pallas import tpu as pltpu
from jax.sharding import Mesh, PartitionSpec as P

EPSILON = 1e-06
AXES = ("y_lo", "z", "core", "x", "y_hi")
SIZES = (2, 8, 2, 4, 2)
ALL = AXES
GROUP = ("x", "y_hi")
LINE = ("y_lo", "z")
MIB = 1024 * 1024
BIG = 60
IDS = 128
HALF = 640
LANES = 128
SIDE = 8
CELLS = 64
TAPS = 7
VMEM = pl.BlockSpec(memory_space=pltpu.VMEM)
SMEM = pl.BlockSpec(memory_space=pltpu.SMEM)
HBM = pl.BlockSpec(memory_space=pltpu.HBM)
STEPS = 4
PEERS = tuple((step_x, step_y) for step_x in range(4) for step_y in range(2))
BF16 = jnp.bfloat16
F32 = jnp.float32


def shape_of(dims, dtype):
    return jax.ShapeDtypeStruct(dims, dtype)


def call(body, outs, operands, name, micros, scratch=(), grant=40):
    specs = tuple(spec for _, spec in outs)
    shapes = tuple(shape for shape, _ in outs)
    single = len(outs) == 1
    return pl.pallas_call(
        body,
        out_shape=shapes[0] if single else shapes,
        in_specs=[spec for _, spec in operands],
        out_specs=specs[0] if single else specs,
        scratch_shapes=list(scratch),
        compiler_params=pltpu.CompilerParams(vmem_limit_bytes=grant * MIB),
        cost_estimate=pl.CostEstimate(
            flops=0, bytes_accessed=int(micros * 3e6), transcendentals=0
        ),
        name=name,
    )(*[operand for operand, _ in operands])


def group_peer(x, y_hi, step_x, step_y):
    return lax.rem(x + step_x, 4) * 2 + lax.rem(y_hi + step_y, 2)


def tap_weights(kernel_ref, at, column, flip):
    place = lax.broadcasted_iota(jnp.int32, (SIDE, LANES), 0) + (column - TAPS // 2)
    valid = (place >= 0) & (place < SIDE)
    weights = []
    for row in range(TAPS):
        if flip:
            line = kernel_ref[TAPS - 1 - row, pl.ds(TAPS - 1 - column, 1), at]
        else:
            line = kernel_ref[row, pl.ds(column, 1), at]
        weights.append(jnp.where(valid, jnp.broadcast_to(line, (SIDE, LANES)), 0.0))
    return weights


def filter_rows(fields, sums, kernel_ref, at, flip):
    for column in range(TAPS):
        weights = tap_weights(kernel_ref, at, column, flip)
        shift = (TAPS // 2 - column) % SIDE
        for field, total in zip(fields, sums):
            for source in range(SIDE):
                moved = field[source] if shift == 0 else pltpu.roll(field[source], shift, 0)
                for row in range(TAPS):
                    target = source - row + TAPS // 2
                    if 0 <= target < SIDE:
                        term = moved * weights[row]
                        total[target] = term if total[target] is None else total[target] + term
    return sums


def forward_kernel(
    field_hbm, kernel_hbm, gain_hbm, head_gain_hbm, ids_hbm,
    filtered_hbm, mean_ref, inverse_ref, normal_ref, send_ref,
    field_ref, kernel_ref, gain_ref, head_gain_ref, ids_ref, filtered_ref, pooled_ref, total_ref,
    field_sems, kernel_sems, small_sems, out_sems,
):
    images = field_ref.shape[0] // CELLS
    channels = field_ref.shape[1]
    chunks = channels // LANES
    part = 1.0 / channels
    block = channels // STEPS
    per_block = chunks // STEPS

    def block_at(step):
        return pl.ds(pl.multiple_of(step * block, LANES), block)

    def field_copy(step):
        at = block_at(step)
        return pltpu.make_async_copy(field_hbm.at[:, at], field_ref.at[:, at], field_sems.at[step])

    def kernel_copy(step):
        at = block_at(step)
        return pltpu.make_async_copy(
            kernel_hbm.at[:, :, at], kernel_ref.at[:, :, at], kernel_sems.at[step]
        )

    def filtered_copy(step):
        at = block_at(step)
        return pltpu.make_async_copy(filtered_ref.at[:, at], filtered_hbm.at[:, at], out_sems.at[step])

    small_copies = [
        pltpu.make_async_copy(gain_hbm, gain_ref, small_sems.at[0]),
        pltpu.make_async_copy(head_gain_hbm, head_gain_ref, small_sems.at[1]),
        pltpu.make_async_copy(ids_hbm, ids_ref, small_sems.at[2]),
    ]
    for step in range(STEPS):
        field_copy(step).start()
        kernel_copy(step).start()
    for copy in small_copies:
        copy.start()

    total_ref[...] = jnp.zeros_like(total_ref)

    def filter_chunk(chunk, carry):
        step = chunk // per_block

        @pl.when(chunk == step * per_block)
        def _():
            field_copy(step).wait()
            kernel_copy(step).wait()

        at = pl.ds(pl.multiple_of(chunk * LANES, LANES), LANES)
        for first in range(0, images, 2):
            fields = []
            for image in range(first, first + 2):
                rows = []
                for pair in range(SIDE // 2):
                    both = field_ref[pl.ds(image * CELLS + pair * 2 * SIDE, 2 * SIDE), at]
                    both = both.astype(jnp.float32)
                    rows += [both[:SIDE], both[SIDE:]]
                fields.append(rows)
            sums = [[None] * SIDE for _ in fields]
            filter_rows(fields, sums, kernel_ref, at, False)
            for offset, total in enumerate(sums):
                for row in range(SIDE):
                    cells = pl.ds((first + offset) * CELLS + row * SIDE, SIDE)
                    filtered_ref[cells, at] = total[row]
                    total_ref[cells, :] += total[row]
        return carry

    lax.fori_loop(0, chunks, filter_chunk, 0)
    for step in range(STEPS):
        filtered_copy(step).start()
    for copy in small_copies:
        copy.wait()
    mean_ref[...] = jnp.broadcast_to(
        jnp.sum(total_ref[...], axis=1, keepdims=True) * part, mean_ref.shape
    )

    for image in range(images):
        cells = pl.ds(image * CELLS, CELLS)
        average = mean_ref[cells, :]

        def spread_chunk(chunk, squares):
            at = pl.ds(pl.multiple_of(chunk * LANES, LANES), LANES)
            centred = filtered_ref[cells, at] - average
            return squares + centred * centred

        squares = lax.fori_loop(
            0, chunks, spread_chunk, jnp.zeros((CELLS, LANES), jnp.float32), unroll=4
        )
        spread = jnp.sum(squares, axis=1, keepdims=True) * part
        inverse_ref[cells, :] = jnp.broadcast_to(lax.rsqrt(spread + EPSILON), (CELLS, LANES))

    for image in range(images):
        cells = pl.ds(image * CELLS, CELLS)
        average = mean_ref[cells, :]
        inverse = inverse_ref[cells, :]

        def pool_chunk(chunk, carry):
            at = pl.ds(pl.multiple_of(chunk * LANES, LANES), LANES)
            normal = (filtered_ref[cells, at] - average) * inverse
            mixed = field_ref[cells, at].astype(jnp.float32) + normal * gain_ref[:, at]
            pooled_ref[pl.ds(image, 1), at] = jnp.sum(mixed, axis=0, keepdims=True) * (1.0 / CELLS)
            return carry

        lax.fori_loop(0, chunks, pool_chunk, 0, unroll=2)

    pooled = pooled_ref[...]
    centred = pooled - jnp.sum(pooled, axis=1, keepdims=True) * part
    spread = jnp.sum(centred * centred, axis=1, keepdims=True) * part
    head_inverse = lax.rsqrt(spread + EPSILON)
    normal = centred * head_inverse
    normal_ref[:, :channels] = normal
    normal_ref[:, channels:] = jnp.broadcast_to(head_inverse, (images, LANES))
    head_input = (normal * head_gain_ref[...]).astype(jnp.bfloat16)
    hot = hot_rows(ids_ref, images)
    group = send_ref.shape[0]
    share = channels // group
    for owner in range(group):
        send_ref[owner, :, :share] = head_input[:, owner * share : (owner + 1) * share]
        send_ref[owner, :, share:] = hot
    for step in range(STEPS):
        filtered_copy(step).wait()


def block_forward(features, kernel, norm_gain, head_gain, img_ids, group):
    images, channels = features.shape[0], features.shape[3]
    cells = images * CELLS
    dma = pltpu.SemaphoreType.DMA
    return call(
        forward_kernel,
        (
            (shape_of((cells, channels), F32), HBM),
            (shape_of((cells, LANES), F32), VMEM),
            (shape_of((cells, LANES), F32), VMEM),
            (shape_of((images, channels + LANES), F32), VMEM),
            (shape_of((group, images, channels // group + IDS), BF16), VMEM),
        ),
        (
            (features.reshape(cells, channels), HBM),
            (kernel, HBM),
            (norm_gain.reshape(1, channels), HBM),
            (head_gain.reshape(1, channels), HBM),
            (img_ids, HBM),
        ),
        "block_forward",
        14,
        scratch=(
            pltpu.VMEM((cells, channels), BF16),
            pltpu.VMEM(kernel.shape, F32),
            pltpu.VMEM((1, channels), F32),
            pltpu.VMEM((1, channels), F32),
            pltpu.SMEM(img_ids.shape, jnp.int32),
            pltpu.VMEM((cells, channels), F32),
            pltpu.VMEM((images, channels), F32),
            pltpu.VMEM((cells, LANES), F32),
            dma((STEPS,)),
            dma((STEPS,)),
            dma((3,)),
            dma((STEPS,)),
        ),
        grant=BIG,
    )


def backward_kernel(
    s0, s1, s2, s3, normal_hbm, gain_hbm, head_gain_hbm,
    filtered_hbm, mean_hbm, inverse_hbm, kernel_hbm, after_hbm,
    out_hbm,
    blocks_ref, normal_ref, gain_ref, head_gain_ref, filtered_ref, mean_ref, inverse_ref, kernel_ref,
    out_ref, even_ref, lean_ref, pull_ref, tilt_ref,
    block_sems, small_sems, filtered_sems, out_sems,
):
    del after_hbm
    images, channels = even_ref.shape
    blocks = (s0, s1, s2, s3)
    share = channels // len(PEERS)
    wide = channels // STEPS

    def block_at(step):
        return pl.ds(pl.multiple_of(step * wide, LANES), wide)

    def out_copy(step):
        at = block_at(step)
        return pltpu.make_async_copy(out_ref.at[:, at], out_hbm.at[:, at], out_sems.at[step])

    head_copies = [
        pltpu.make_async_copy(block, blocks_ref.at[index], block_sems.at[index])
        for index, block in enumerate(blocks)
    ]
    small_copies = [
        pltpu.make_async_copy(source, target, small_sems.at[index])
        for index, (source, target) in enumerate((
            (head_gain_hbm, head_gain_ref), (gain_hbm, gain_ref), (normal_hbm, normal_ref),
            (mean_hbm, mean_ref), (inverse_hbm, inverse_ref),
        ))
    ]
    filtered_copies = [
        pltpu.make_async_copy(
            filtered_hbm.at[:, block_at(step)], filtered_ref.at[:, block_at(step)],
            filtered_sems.at[step],
        )
        for step in range(STEPS)
    ]
    kernel_copy = pltpu.make_async_copy(kernel_hbm, kernel_ref, small_sems.at[5])
    for copy in (*head_copies, *small_copies, *filtered_copies, kernel_copy):
        copy.start()
    chunks = channels // LANES
    per_block = chunks // STEPS
    part = 1.0 / channels

    for copy in (*head_copies, *small_copies):
        copy.wait()
    x, y_hi = lax.axis_index("x"), lax.axis_index("y_hi")
    for step_x, step_y in PEERS:
        owner = group_peer(x, y_hi, 4 - step_x, step_y)
        at = pl.ds(pl.multiple_of(owner * share, LANES), share)
        tilt_ref[:, at] = blocks_ref[step_x, step_y] * head_gain_ref[:, at]
    cotangent = tilt_ref[...]
    normal = normal_ref[:, :channels]
    level = jnp.sum(cotangent, axis=1, keepdims=True) * part
    lean = jnp.sum(cotangent * normal, axis=1, keepdims=True) * part
    pooled_grad = normal_ref[:, channels : channels + 1] * (cotangent - level - normal * lean)
    even = pooled_grad * (1.0 / CELLS)
    even_ref[...] = even
    pull = even * gain_ref[...]
    pull_ref[...] = pull
    tilt_ref[...] = pull - jnp.sum(pull, axis=1, keepdims=True) * part

    for step in range(STEPS):
        filtered_copies[step].wait()
        for image in range(images):
            spot = pl.ds(image * CELLS, CELLS)
            average = mean_ref[spot, :]

            def lean_chunk(chunk, total, spot=spot, average=average, image=image):
                at = pl.ds(pl.multiple_of(chunk * LANES, LANES), LANES)
                return total + (filtered_ref[spot, at] - average) * pull_ref[pl.ds(image, 1), at]

            total = jnp.zeros((CELLS, LANES), F32) if step == 0 else lean_ref[spot, :]
            lean_ref[spot, :] = lax.fori_loop(
                step * per_block, (step + 1) * per_block, lean_chunk, total, unroll=True
            )
    inverse = inverse_ref[...]
    mean_lean = jnp.sum(lean_ref[...], axis=1, keepdims=True) * part
    lean_ref[...] = inverse * (inverse * (inverse * mean_lean))
    kernel_copy.wait()

    def filter_chunk(chunk, carry):
        at = pl.ds(pl.multiple_of(chunk * LANES, LANES), LANES)
        for first in range(0, images, 2):
            fields = []
            sums = []
            for image in range(first, first + 2):
                tilt = jnp.broadcast_to(tilt_ref[pl.ds(image, 1), at], (SIDE, LANES))
                even = jnp.broadcast_to(even_ref[pl.ds(image, 1), at], (SIDE, LANES))
                rows = []
                for row in range(SIDE):
                    spot = pl.ds(image * CELLS + row * SIDE, SIDE)
                    rows.append(
                        inverse_ref[spot, :] * tilt
                        - lean_ref[spot, :] * (filtered_ref[spot, at] - mean_ref[spot, :])
                    )
                fields.append(rows)
                sums.append([even] * SIDE)
            filter_rows(fields, sums, kernel_ref, at, True)
            for offset, total in enumerate(sums):
                for half in range(SIDE // 2):
                    two = jnp.concatenate(total[2 * half : 2 * half + 2], axis=0)
                    spot = pl.ds((first + offset) * CELLS + half * 2 * SIDE, 2 * SIDE)
                    out_ref[spot, at] = two.astype(jnp.bfloat16)
        step = chunk // per_block

        @pl.when(chunk == step * per_block + per_block - 1)
        def _():
            out_copy(step).start()

        return carry

    lax.fori_loop(0, chunks, filter_chunk, 0)
    for step in range(STEPS):
        out_copy(step).wait()


def block_backward(blocks, normal, norm_gain, head_gain, filtered, mean, inverse, kernel, after):
    cells, channels = filtered.shape
    images = cells // CELLS
    dma = pltpu.SemaphoreType.DMA
    operands = [
        *blocks, normal, norm_gain.reshape(1, channels), head_gain.reshape(1, channels),
        filtered, mean, inverse, kernel, after,
    ]
    return call(
        backward_kernel,
        ((shape_of((cells, channels), BF16), HBM),),
        tuple((array, HBM) for array in operands),
        "block_backward",
        14,
        scratch=(
            pltpu.VMEM((len(blocks),) + blocks[0].shape, F32),
            pltpu.VMEM(normal.shape, F32),
            pltpu.VMEM((1, channels), F32),
            pltpu.VMEM((1, channels), F32),
            pltpu.VMEM((cells, channels), F32),
            pltpu.VMEM((cells, LANES), F32),
            pltpu.VMEM((cells, LANES), F32),
            pltpu.VMEM(kernel.shape, F32),
            pltpu.VMEM((cells, channels), BF16),
            pltpu.VMEM((images, channels), F32),
            pltpu.VMEM((cells, LANES), F32),
            pltpu.VMEM((images, channels), F32),
            pltpu.VMEM((images, channels), F32),
            dma((len(blocks),)),
            dma((6,)),
            dma((STEPS,)),
            dma((STEPS,)),
        ),
        grant=BIG,
    )


def dot(left, right, left_dim, right_dim):
    return lax.dot_general(
        left, right, (((left_dim,), (right_dim,)), ((), ())), preferred_element_type=F32
    )


def inverse_length(values):
    return lax.rsqrt(jnp.sum(values * values, axis=-1, keepdims=True) + EPSILON)


def length_back(unit, inverse, cotangent):
    return inverse * (cotangent - unit * jnp.sum(unit * cotangent, axis=-1, keepdims=True))


def hot_rows(ids_ref, rows):
    row = lax.broadcasted_iota(jnp.int32, (rows, IDS), 0)
    ids = jnp.zeros((rows, IDS), jnp.int32)
    for index in range(rows):
        ids = jnp.where(row == index, ids_ref[index], ids)
    lane = lax.broadcasted_iota(jnp.int32, (rows, IDS), 1)
    return jnp.where(ids == lane, 1.0, 0.0).astype(BF16)


def pack_kernel(text_hbm, ids_hbm, out_ref, text_ref, ids_ref, sems):
    copies = [
        pltpu.make_async_copy(text_hbm, text_ref, sems.at[0]),
        pltpu.make_async_copy(ids_hbm, ids_ref, sems.at[1]),
    ]
    for copy in copies:
        copy.start()
    for copy in copies:
        copy.wait()
    rows, width = text_ref.shape
    text = text_ref[...].astype(F32)
    unit = (text * inverse_length(text)).astype(BF16)
    hot = hot_rows(ids_ref, rows)
    for target in range(out_ref.shape[0]):
        out_ref[target, :, :width] = unit
        out_ref[target, :, width:] = hot


def line_kernel(line_ref, out_ref):
    line, rows, _ = line_ref.shape
    for first in range(0, line, 4):
        four = [line_ref[first + offset].astype(F32) for offset in range(4)]
        at = slice(first * rows, (first + 4) * rows)
        out_ref[at, :] = jnp.concatenate(four, axis=0).astype(BF16)


def join_texts_kernel(own_ref, next_ref, after_ref, out_ref):
    del after_ref
    texts = own_ref.shape[0]
    out_ref[:texts, :] = own_ref[...]
    out_ref[texts:, :] = next_ref[...]


def partial_kernel(received_ref, projection_ref, out_ref, columns_ref, hot_ref):
    group = received_ref.shape[0]
    share = projection_ref.shape[0]
    rows = jnp.concatenate([received_ref[owner].astype(F32) for owner in range(group)], axis=0)
    columns = rows[:, :share].astype(BF16)
    columns_ref[...] = columns
    hot_ref[...] = rows[:, share:].astype(BF16)
    partial = dot(columns, projection_ref[...], 1, 0).astype(BF16)
    for target in range(group):
        out_ref[target] = partial


def pair_kernel(
    partials_ref, hot_ref, projection_ref, t0, t1, t2, t3, t4, t5, t6, t7,
    scale_ref, shift_ref,
    stay_ref, send_ref, factors_ref,
    head_ref,
):
    group, images, width = partials_ref.shape
    blocks = (t0, t1, t2, t3, t4, t5, t6, t7)
    scale, shift = scale_ref[0], shift_ref[0]
    embedded = partials_ref[0].astype(F32)
    for owner in range(1, group):
        embedded += partials_ref[owner].astype(F32)
    inverse = inverse_length(embedded)
    unit = embedded * inverse
    low = unit.astype(BF16)
    factors_ref[:, width : 2 * width] = low
    hot = hot_ref[...]
    weights = []
    for block in blocks:
        logits = scale * dot(low, block[:, :width], 1, 1) + shift
        signs = 2.0 * dot(hot, block[:, width:], 1, 1) - 1.0
        weights.append((-signs * jax.nn.sigmoid(-signs * logits)).astype(BF16))
    image_grad = dot(weights[0], t0[:, :width], 1, 0)
    for weight, block in zip(weights[1:], blocks[1:]):
        image_grad += dot(weight, block[:, :width], 1, 0)
    embed = length_back(unit, inverse, scale * image_grad).astype(BF16)
    factors_ref[:, :width] = embed
    factors_ref[:, 2 * width : 2 * width + LANES] = weights[0]
    factors_ref[:, 2 * width + LANES :] = weights[4]
    head = dot(embed, projection_ref[...], 1, 1)
    rows = images // group
    for owner in range(group):
        head_ref[owner] = head[owner * rows : (owner + 1) * rows]
    x, y_hi = lax.axis_index("x"), lax.axis_index("y_hi")
    for step in range(4):
        stay_ref[step] = head_ref[group_peer(x, y_hi, step, 0)]
        send_ref[step] = head_ref[group_peer(x, y_hi, step, 1)]


def merge_kernel(stay_ref, got_ref, s0, s1, s2, s3):
    for step, out_ref in enumerate((s0, s1, s2, s3)):
        out_ref[0] = stay_ref[step]
        out_ref[1] = got_ref[step]


def strip_make_kernel(mine_ref, theirs_ref, columns_ref, far_columns_ref, out_ref, rows_ref, near_ref, far_ref):
    width = (mine_ref.shape[1] - 2 * LANES) // 2
    line, strip_rows, half = out_ref.shape
    strip = columns_ref.shape[1] // line
    rows = (strip_rows - strip) // 2
    texts = line * rows
    start = pl.multiple_of(lax.axis_index("core") * (width - half), LANES)

    def both(at):
        return jnp.concatenate([mine_ref[:, at], theirs_ref[:, at]], axis=0)

    columns = jnp.concatenate([columns_ref[...], far_columns_ref[...]], axis=0)
    rows_ref[...] = dot(columns, both(pl.ds(start, half)), 0, 0)
    low = both(pl.ds(pl.multiple_of(start + width, LANES), half))
    first = slice(2 * width, 2 * width + texts)
    second = slice(2 * width + LANES, 2 * width + LANES + texts)
    own = jnp.concatenate([mine_ref[:, first], theirs_ref[:, second]], axis=0)
    other = jnp.concatenate([mine_ref[:, second], theirs_ref[:, first]], axis=0)
    near_ref[...] = dot(own, low, 0, 0)
    far_ref[...] = dot(other, low, 0, 0)
    for target in range(line):
        at = slice(target * rows, (target + 1) * rows)
        stacked = jnp.concatenate(
            [rows_ref[target * strip : (target + 1) * strip], near_ref[at], far_ref[at]], axis=0
        )
        out_ref[target] = stacked.astype(BF16)


def strip_kernel(strips_ref, out_ref, mine_ref, theirs_ref):
    line, rows, half = strips_ref.shape
    texts = mine_ref.shape[0]
    strip = rows - 2 * texts
    total = strips_ref[0].astype(F32)
    for source in range(1, line):
        total += strips_ref[source].astype(F32)
    low = total[:strip].astype(BF16)
    for target in range(line):
        out_ref[target] = low
    mine_ref[...] = total[strip : strip + texts]
    theirs_ref[...] = total[strip + texts :]


def text_kernel(text_ref, mine_ref, got_ref, scale_ref, out_ref):
    width = text_ref.shape[1]
    text = text_ref[...].astype(F32)
    inverse = inverse_length(text)
    first = lax.axis_index("core") == 0
    mine, got = mine_ref[...], got_ref[...]
    left = jnp.where(first, mine, got)
    right = jnp.where(first, got, mine)
    grad = jnp.concatenate([left, right[:, 2 * HALF - width :]], axis=1)
    out_ref[...] = length_back(text * inverse, inverse, scale_ref[0] * grad)


def join_kernel(near_ref, far_ref, out_ref):
    core = lax.axis_index("core")
    width = out_ref.shape[1]

    def put(left, right):
        out_ref[:, :HALF] = left[...].astype(F32)
        out_ref[:, HALF:] = right[:, 2 * HALF - width :].astype(F32)

    pl.when(core == 0)(lambda: put(near_ref, far_ref))
    pl.when(core != 0)(lambda: put(far_ref, near_ref))


def exchange(blocks, axes):
    return lax.all_to_all(blocks, axes, 0, 0, tiled=True)


def swap_core(block):
    return lax.ppermute(block, "core", ((0, 1), (1, 0)))


def along_x(block, step):
    return lax.ppermute(block, "x", tuple((i, (i + step) % 4) for i in range(4)))


def local(
    features,
    text_embed,
    img_ids,
    txt_ids,
    kernel,
    norm_gain,
    head_gain,
    projection,
    logit_scale,
    logit_bias,
):
    rows, width = text_embed.shape
    share = projection.shape[0]
    group = lax.axis_size(GROUP)
    line = lax.axis_size(LINE)
    images = group * rows
    texts = line * rows
    strip = share // line
    dma = pltpu.SemaphoreType.DMA

    packed = call(
        pack_kernel,
        ((shape_of((line, rows, width + IDS), BF16), VMEM),),
        ((text_embed, HBM), (txt_ids, HBM)),
        "text_pack", 1,
        scratch=(
            pltpu.VMEM((rows, width), BF16), pltpu.SMEM((rows,), jnp.int32), dma((2,)),
        ),
        grant=BIG,
    )
    gathered = exchange(packed, LINE)
    filtered, mean, inverse, normal, send = block_forward(
        features, kernel, norm_gain, head_gain, img_ids, group
    )
    gathered, send = lax.optimization_barrier((gathered, send))
    received = exchange(send, GROUP)
    partials, columns, hot = call(
        partial_kernel,
        (
            (shape_of((group, images, width), BF16), VMEM),
            (shape_of((images, share), BF16), VMEM),
            (shape_of((images, IDS), BF16), VMEM),
        ),
        ((received, VMEM), (projection, VMEM)),
        "partial_embed", 2,
    )
    own_line = call(
        line_kernel, ((shape_of((texts, width + IDS), BF16), VMEM),), ((gathered, VMEM),),
        "line_rows", 1,
    )
    next_line = lax.ppermute(own_line, "y_hi", ((0, 1), (1, 0)))
    near = [
        call(
            join_texts_kernel,
            ((shape_of((2 * texts, width + IDS), BF16), VMEM),),
            ((own_line, VMEM), (next_line, VMEM), (columns, VMEM)),
            "join_texts", 1,
        )
    ]
    near += [along_x(near[0], step) for step in (1, 3, 2)]
    far = [swap_core(block) for block in near]
    far_columns = swap_core(columns)
    partials = exchange(partials, GROUP)
    stay, away, factors = call(
        pair_kernel,
        (
            (shape_of((4, rows, share), F32), VMEM),
            (shape_of((4, rows, share), F32), VMEM),
            (shape_of((images, 2 * width + 2 * LANES), BF16), VMEM),
        ),
        tuple((array, VMEM) for array in (partials, hot, projection, *near, *far))
        + ((logit_scale, SMEM), (logit_bias, SMEM)),
        "pairs", 4,
        scratch=(pltpu.VMEM((group, rows, share), F32),),
    )
    far_factors = swap_core(factors)
    got = lax.ppermute(away, "y_hi", ((0, 1), (1, 0)))
    strips = call(
        strip_make_kernel,
        ((shape_of((line, strip + 2 * rows, HALF), BF16), VMEM),),
        tuple((array, VMEM) for array in (factors, far_factors, columns, far_columns)),
        "strip_make", 2,
        scratch=(
            pltpu.VMEM((share, HALF), F32),
            pltpu.VMEM((texts, HALF), F32),
            pltpu.VMEM((texts, HALF), F32),
        ),
    )
    strips = exchange(strips, LINE)
    merged = call(
        merge_kernel,
        ((shape_of((2, rows, share), F32), VMEM),) * 4,
        ((stay, VMEM), (got, VMEM)),
        "head_merge", 1,
    )
    blocks = [merged[0]] + [along_x(merged[step], step) for step in (1, 2, 3)]
    shared = (normal, norm_gain, head_gain, filtered, mean, inverse, kernel)
    strips, *blocks = lax.optimization_barrier((strips, *blocks))
    sums, mine, theirs = call(
        strip_kernel,
        (
            (shape_of((line, strip, HALF), BF16), VMEM),
            (shape_of((rows, HALF), F32), VMEM),
            (shape_of((rows, HALF), F32), VMEM),
        ),
        ((strips, VMEM),),
        "strip_sum", 1,
    )
    near_half = exchange(sums, LINE).reshape(share, HALF)
    grad_text = call(
        text_kernel,
        ((shape_of((rows, width), F32), VMEM),),
        ((text_embed, VMEM), (mine, VMEM), (swap_core(theirs), VMEM), (logit_scale, SMEM)),
        "text_grad", 1,
    )
    grad_features = block_backward(blocks, *shared, mine)
    near_half, grad_features, grad_text = lax.optimization_barrier(
        (near_half, grad_features, grad_text)
    )
    grad_proj = call(
        join_kernel,
        ((shape_of((share, width), F32), VMEM),),
        ((near_half, VMEM), (swap_core(near_half), VMEM)),
        "proj_join", 2,
    )
    grad_features = grad_features.reshape(features.shape)
    return (grad_features, grad_text, grad_proj)


def solution(mesh):
    fine = Mesh(mesh.devices.reshape(SIZES), AXES)
    placed = (
        P(ALL, None, None, None),
        P(ALL, None),
        P(ALL),
        P(ALL),
        P(),
        P(),
        P(),
        P(GROUP, None),
        P(),
        P(),
    )
    return jax.shard_map(
        local,
        mesh=fine,
        in_specs=placed,
        out_specs=(P(ALL, None, None, None), P(ALL, None), P(GROUP, None)),
        check_vma=False,
    )
```

```python
import jax
import jax.numpy as jnp
from jax import lax
from jax.experimental import pallas as pl
from jax.experimental.pallas import tpu as pltpu
from jax.sharding import Mesh, PartitionSpec as P

EPSILON = 1e-06
AXES = ("y_lo", "z", "core", "x", "y_hi")
SIZES = (2, 8, 2, 4, 2)
ALL = AXES
GROUP = ("x", "y_hi")
LINE = ("y_lo", "z")
PLANE = ("y_lo", "x", "y_hi")
OWN = 16
MIB = 1024 * 1024
BIG = 60
IDS = 128
HALF = 640
LANES = 128
SIDE = 8
CELLS = 64
TAPS = 7
VMEM = pl.BlockSpec(memory_space=pltpu.VMEM)
SMEM = pl.BlockSpec(memory_space=pltpu.SMEM)
HBM = pl.BlockSpec(memory_space=pltpu.HBM)
STEPS = 4
PEERS = tuple((step_x, step_y) for step_x in range(4) for step_y in range(2))
BF16 = jnp.bfloat16
F32 = jnp.float32


def shape_of(dims, dtype):
    return jax.ShapeDtypeStruct(dims, dtype)


def call(body, outs, operands, name, micros, scratch=(), grant=40):
    specs = tuple(spec for _, spec in outs)
    shapes = tuple(shape for shape, _ in outs)
    single = len(outs) == 1
    return pl.pallas_call(
        body,
        out_shape=shapes[0] if single else shapes,
        in_specs=[spec for _, spec in operands],
        out_specs=specs[0] if single else specs,
        scratch_shapes=list(scratch),
        compiler_params=pltpu.CompilerParams(vmem_limit_bytes=grant * MIB),
        cost_estimate=pl.CostEstimate(
            flops=0, bytes_accessed=int(micros * 3e6), transcendentals=0
        ),
        name=name,
    )(*[operand for operand, _ in operands])


def group_peer(x, y_hi, step_x, step_y):
    return lax.rem(x + step_x, 4) * 2 + lax.rem(y_hi + step_y, 2)


def tap_weights(kernel_ref, at, column, flip):
    place = lax.broadcasted_iota(jnp.int32, (SIDE, LANES), 0) + (column - TAPS // 2)
    valid = (place >= 0) & (place < SIDE)
    weights = []
    for row in range(TAPS):
        if flip:
            line = kernel_ref[TAPS - 1 - row, pl.ds(TAPS - 1 - column, 1), at]
        else:
            line = kernel_ref[row, pl.ds(column, 1), at]
        weights.append(jnp.where(valid, jnp.broadcast_to(line, (SIDE, LANES)), 0.0))
    return weights


def filter_rows(fields, sums, kernel_ref, at, flip):
    for column in range(TAPS):
        weights = tap_weights(kernel_ref, at, column, flip)
        shift = (TAPS // 2 - column) % SIDE
        for field, total in zip(fields, sums):
            for source in range(SIDE):
                moved = field[source] if shift == 0 else pltpu.roll(field[source], shift, 0)
                for row in range(TAPS):
                    target = source - row + TAPS // 2
                    if 0 <= target < SIDE:
                        term = moved * weights[row]
                        total[target] = term if total[target] is None else total[target] + term
    return sums


def forward_kernel(
    pair, field_hbm, kernel_hbm, gain_hbm,
    filtered_hbm, mean_ref, inverse_ref,
    field_ref, kernel_ref, gain_ref, filtered_ref, pooled_ref, total_ref,
    field_sems, kernel_sems, small_sems, out_sems,
):
    images = field_ref.shape[0] // CELLS
    channels = field_ref.shape[1]
    chunks = channels // LANES
    part = 1.0 / channels
    block = channels // STEPS
    per_block = chunks // STEPS

    def block_at(step):
        return pl.ds(pl.multiple_of(step * block, LANES), block)

    def field_copy(step):
        at = block_at(step)
        return pltpu.make_async_copy(field_hbm.at[pair * images * CELLS : (pair + 1) * images * CELLS, at], field_ref.at[:, at], field_sems.at[step])

    def kernel_copy(step):
        at = block_at(step)
        return pltpu.make_async_copy(
            kernel_hbm.at[:, :, at], kernel_ref.at[:, :, at], kernel_sems.at[step]
        )

    def filtered_copy(step):
        at = block_at(step)
        return pltpu.make_async_copy(filtered_ref.at[:, at], filtered_hbm.at[:, at], out_sems.at[step])

    small_copies = [pltpu.make_async_copy(gain_hbm, gain_ref, small_sems.at[0])]
    for step in range(STEPS):
        field_copy(step).start()
        kernel_copy(step).start()
    for copy in small_copies:
        copy.start()

    total_ref[...] = jnp.zeros_like(total_ref)

    def filter_chunk(chunk, carry):
        step = chunk // per_block

        @pl.when(chunk == step * per_block)
        def _():
            field_copy(step).wait()
            kernel_copy(step).wait()

        at = pl.ds(pl.multiple_of(chunk * LANES, LANES), LANES)
        for first in range(0, images, 2):
            fields = []
            for image in range(first, first + 2):
                rows = []
                for pair in range(SIDE // 2):
                    both = field_ref[pl.ds(image * CELLS + pair * 2 * SIDE, 2 * SIDE), at]
                    both = both.astype(jnp.float32)
                    rows += [both[:SIDE], both[SIDE:]]
                fields.append(rows)
            sums = [[None] * SIDE for _ in fields]
            filter_rows(fields, sums, kernel_ref, at, False)
            for offset, total in enumerate(sums):
                for row in range(SIDE):
                    cells = pl.ds((first + offset) * CELLS + row * SIDE, SIDE)
                    filtered_ref[cells, at] = total[row]
                    total_ref[cells, :] += total[row]
        return carry

    lax.fori_loop(0, chunks, filter_chunk, 0)
    for step in range(STEPS):
        filtered_copy(step).start()
    for copy in small_copies:
        copy.wait()
    mean_ref[...] = jnp.broadcast_to(
        jnp.sum(total_ref[...], axis=1, keepdims=True) * part, mean_ref.shape
    )

    for image in range(images):
        cells = pl.ds(image * CELLS, CELLS)
        average = mean_ref[cells, :]

        def spread_chunk(chunk, squares):
            at = pl.ds(pl.multiple_of(chunk * LANES, LANES), LANES)
            centred = filtered_ref[cells, at] - average
            return squares + centred * centred

        squares = lax.fori_loop(
            0, chunks, spread_chunk, jnp.zeros((CELLS, LANES), jnp.float32), unroll=4
        )
        spread = jnp.sum(squares, axis=1, keepdims=True) * part
        inverse_ref[cells, :] = jnp.broadcast_to(lax.rsqrt(spread + EPSILON), (CELLS, LANES))

    for image in range(images):
        cells = pl.ds(image * CELLS, CELLS)
        average = mean_ref[cells, :]
        inverse = inverse_ref[cells, :]

        def pool_chunk(chunk, carry):
            at = pl.ds(pl.multiple_of(chunk * LANES, LANES), LANES)
            normal = (filtered_ref[cells, at] - average) * inverse
            mixed = field_ref[cells, at].astype(jnp.float32) + normal * gain_ref[:, at]
            pooled_ref[pl.ds(image, 1), at] = jnp.sum(mixed, axis=0, keepdims=True) * (1.0 / CELLS)
            return carry

        lax.fori_loop(0, chunks, pool_chunk, 0, unroll=2)

    for step in range(STEPS):
        filtered_copy(step).wait()


def first_forward(
    field_hbm, kernel_hbm, gain_hbm, filtered_hbm, mean_ref, inverse_ref, pooled_ref, *scratch
):
    forward_kernel(
        0, field_hbm, kernel_hbm, gain_hbm, filtered_hbm, mean_ref, inverse_ref,
        *scratch[:4], pooled_ref, *scratch[4:],
    )


def second_forward(
    field_hbm, kernel_hbm, gain_hbm, pooled_hbm, head_gain_hbm, ids_hbm, after_hbm,
    filtered_hbm, mean_ref, inverse_ref, normal_ref, send_ref,
    field_ref, kernel_ref, gain_ref, filtered_ref, total_ref, *rest,
):
    del after_hbm
    sems, (late_ref, both_ref, head_gain_ref, ids_ref, late_sems) = rest[:4], rest[4:]
    half, channels = late_ref.shape
    images = 2 * half
    part = 1.0 / channels
    copies = [
        pltpu.make_async_copy(pooled_hbm, both_ref, late_sems.at[0]),
        pltpu.make_async_copy(head_gain_hbm, head_gain_ref, late_sems.at[1]),
        pltpu.make_async_copy(ids_hbm, ids_ref, late_sems.at[2]),
    ]
    for copy in copies:
        copy.start()
    forward_kernel(
        1, field_hbm, kernel_hbm, gain_hbm, filtered_hbm, mean_ref, inverse_ref,
        field_ref, kernel_ref, gain_ref, filtered_ref, late_ref, total_ref, *sems,
    )
    for copy in copies:
        copy.wait()
    pooled = jnp.concatenate([both_ref[...], late_ref[...]], axis=0)
    centred = pooled - jnp.sum(pooled, axis=1, keepdims=True) * part
    spread = jnp.sum(centred * centred, axis=1, keepdims=True) * part
    head_inverse = lax.rsqrt(spread + EPSILON)
    normal = centred * head_inverse
    normal_ref[:, :channels] = normal
    normal_ref[:, channels:] = jnp.broadcast_to(head_inverse, (images, LANES))
    head_input = (normal * head_gain_ref[...]).astype(jnp.bfloat16)
    hot = hot_rows(ids_ref, images)
    group = send_ref.shape[0]
    share = channels // group
    for owner in range(group):
        send_ref[owner, :, :share] = head_input[:, owner * share : (owner + 1) * share]
        send_ref[owner, :, share:] = hot


def forward_scratch(features, kernel):
    cells, channels = features.shape[0] * CELLS // 2, features.shape[3]
    return (
        pltpu.VMEM((cells, channels), BF16),
        pltpu.VMEM(kernel.shape, F32),
        pltpu.VMEM((1, channels), F32),
        pltpu.VMEM((cells, channels), F32),
        pltpu.VMEM((cells, LANES), F32),
        pltpu.SemaphoreType.DMA((STEPS,)),
        pltpu.SemaphoreType.DMA((STEPS,)),
        pltpu.SemaphoreType.DMA((1,)),
        pltpu.SemaphoreType.DMA((STEPS,)),
    )


def forward_outs(features):
    cells, channels = features.shape[0] * CELLS // 2, features.shape[3]
    return (
        (shape_of((cells, channels), F32), HBM),
        (shape_of((cells, LANES), F32), VMEM),
        (shape_of((cells, LANES), F32), VMEM),
    )


def forward_operands(features, kernel, norm_gain):
    images, channels = features.shape[0], features.shape[3]
    return (
        (features.reshape(images * CELLS, channels), HBM),
        (kernel, HBM),
        (norm_gain.reshape(1, channels), HBM),
    )


def block_forward_first(features, kernel, norm_gain):
    images, channels = features.shape[0], features.shape[3]
    return call(
        first_forward,
        forward_outs(features) + ((shape_of((images // 2, channels), F32), VMEM),),
        forward_operands(features, kernel, norm_gain),
        "block_forward_first", 8,
        scratch=forward_scratch(features, kernel),
        grant=BIG,
    )


def block_forward_second(features, kernel, norm_gain, pooled, head_gain, img_ids, after, group):
    images, channels = features.shape[0], features.shape[3]
    return call(
        second_forward,
        forward_outs(features)
        + (
            (shape_of((images, channels + LANES), F32), VMEM),
            (shape_of((group, images, channels // group + IDS), BF16), VMEM),
        ),
        forward_operands(features, kernel, norm_gain)
        + ((pooled, HBM), (head_gain.reshape(1, channels), HBM), (img_ids, HBM), (after, HBM)),
        "block_forward_second", 8,
        scratch=forward_scratch(features, kernel)
        + (
            pltpu.VMEM((images // 2, channels), F32),
            pltpu.VMEM((images // 2, channels), F32),
            pltpu.VMEM((1, channels), F32),
            pltpu.SMEM(img_ids.shape, jnp.int32),
            pltpu.SemaphoreType.DMA((3,)),
        ),
        grant=BIG,
    )


def backward_kernel(
    s0, s1, s2, s3, normal_hbm, gain_hbm, head_gain_hbm,
    f0, f1, m0, m1, i0, i1, kernel_hbm, after_hbm,
    out_hbm,
    blocks_ref, normal_ref, gain_ref, head_gain_ref, filtered_ref, mean_ref, inverse_ref, kernel_ref,
    out_ref, even_ref, lean_ref, pull_ref, tilt_ref,
    block_sems, small_sems, filtered_sems, out_sems,
):
    del after_hbm
    images, channels = even_ref.shape
    blocks = (s0, s1, s2, s3)
    share = channels // len(PEERS)
    wide = channels // STEPS
    some = images * CELLS // 2

    def block_at(step):
        return pl.ds(pl.multiple_of(step * wide, LANES), wide)

    def out_copy(step):
        at = block_at(step)
        return pltpu.make_async_copy(out_ref.at[:, at], out_hbm.at[:, at], out_sems.at[step])

    head_copies = [
        pltpu.make_async_copy(block, blocks_ref.at[index], block_sems.at[index])
        for index, block in enumerate(blocks)
    ]
    small_copies = [
        pltpu.make_async_copy(source, target, small_sems.at[index])
        for index, (source, target) in enumerate((
            (head_gain_hbm, head_gain_ref), (gain_hbm, gain_ref), (normal_hbm, normal_ref),
            (m0, mean_ref.at[:some, :]), (m1, mean_ref.at[some:, :]),
            (i0, inverse_ref.at[:some, :]), (i1, inverse_ref.at[some:, :]),
        ))
    ]
    filtered_copies = [
        pltpu.make_async_copy(
            source.at[:, block_at(step)],
            filtered_ref.at[half * some : (half + 1) * some, block_at(step)],
            filtered_sems.at[2 * step + half],
        )
        for step in range(STEPS)
        for half, source in enumerate((f0, f1))
    ]
    kernel_copy = pltpu.make_async_copy(kernel_hbm, kernel_ref, small_sems.at[7])
    for copy in (*head_copies, *small_copies, *filtered_copies, kernel_copy):
        copy.start()
    chunks = channels // LANES
    per_block = chunks // STEPS
    part = 1.0 / channels

    for copy in (*head_copies, *small_copies):
        copy.wait()
    x, y_hi = lax.axis_index("x"), lax.axis_index("y_hi")
    for step_x, step_y in PEERS:
        owner = group_peer(x, y_hi, 4 - step_x, step_y)
        at = pl.ds(pl.multiple_of(owner * share, LANES), share)
        tilt_ref[:, at] = blocks_ref[step_x, step_y] * head_gain_ref[:, at]
    cotangent = tilt_ref[...]
    normal = normal_ref[:, :channels]
    level = jnp.sum(cotangent, axis=1, keepdims=True) * part
    lean = jnp.sum(cotangent * normal, axis=1, keepdims=True) * part
    pooled_grad = normal_ref[:, channels : channels + 1] * (cotangent - level - normal * lean)
    even = pooled_grad * (1.0 / CELLS)
    even_ref[...] = even
    pull = even * gain_ref[...]
    pull_ref[...] = pull
    tilt_ref[...] = pull - jnp.sum(pull, axis=1, keepdims=True) * part

    for step in range(STEPS):
        filtered_copies[2 * step].wait()
        filtered_copies[2 * step + 1].wait()
        for image in range(images):
            spot = pl.ds(image * CELLS, CELLS)
            average = mean_ref[spot, :]

            def lean_chunk(chunk, total, spot=spot, average=average, image=image):
                at = pl.ds(pl.multiple_of(chunk * LANES, LANES), LANES)
                return total + (filtered_ref[spot, at] - average) * pull_ref[pl.ds(image, 1), at]

            total = jnp.zeros((CELLS, LANES), F32) if step == 0 else lean_ref[spot, :]
            lean_ref[spot, :] = lax.fori_loop(
                step * per_block, (step + 1) * per_block, lean_chunk, total, unroll=True
            )
    inverse = inverse_ref[...]
    mean_lean = jnp.sum(lean_ref[...], axis=1, keepdims=True) * part
    lean_ref[...] = inverse * (inverse * (inverse * mean_lean))
    kernel_copy.wait()

    def filter_chunk(chunk, carry):
        at = pl.ds(pl.multiple_of(chunk * LANES, LANES), LANES)
        for first in range(0, images, 2):
            fields = []
            sums = []
            for image in range(first, first + 2):
                tilt = jnp.broadcast_to(tilt_ref[pl.ds(image, 1), at], (SIDE, LANES))
                even = jnp.broadcast_to(even_ref[pl.ds(image, 1), at], (SIDE, LANES))
                rows = []
                for row in range(SIDE):
                    spot = pl.ds(image * CELLS + row * SIDE, SIDE)
                    rows.append(
                        inverse_ref[spot, :] * tilt
                        - lean_ref[spot, :] * (filtered_ref[spot, at] - mean_ref[spot, :])
                    )
                fields.append(rows)
                sums.append([even] * SIDE)
            filter_rows(fields, sums, kernel_ref, at, True)
            for offset, total in enumerate(sums):
                for half in range(SIDE // 2):
                    two = jnp.concatenate(total[2 * half : 2 * half + 2], axis=0)
                    spot = pl.ds((first + offset) * CELLS + half * 2 * SIDE, 2 * SIDE)
                    out_ref[spot, at] = two.astype(jnp.bfloat16)
        step = chunk // per_block

        @pl.when(chunk == step * per_block + per_block - 1)
        def _():
            out_copy(step).start()

        return carry

    lax.fori_loop(0, chunks, filter_chunk, 0)
    for step in range(STEPS):
        out_copy(step).wait()


def block_backward(blocks, normal, norm_gain, head_gain, filtered, mean, inverse, kernel, after):
    cells, channels = 2 * filtered[0].shape[0], filtered[0].shape[1]
    images = cells // CELLS
    dma = pltpu.SemaphoreType.DMA
    operands = [
        *blocks, normal, norm_gain.reshape(1, channels), head_gain.reshape(1, channels),
        *filtered, *mean, *inverse, kernel, after,
    ]
    return call(
        backward_kernel,
        ((shape_of((cells, channels), BF16), HBM),),
        tuple((array, HBM) for array in operands),
        "block_backward",
        14,
        scratch=(
            pltpu.VMEM((len(blocks),) + blocks[0].shape, F32),
            pltpu.VMEM(normal.shape, F32),
            pltpu.VMEM((1, channels), F32),
            pltpu.VMEM((1, channels), F32),
            pltpu.VMEM((cells, channels), F32),
            pltpu.VMEM((cells, LANES), F32),
            pltpu.VMEM((cells, LANES), F32),
            pltpu.VMEM(kernel.shape, F32),
            pltpu.VMEM((cells, channels), BF16),
            pltpu.VMEM((images, channels), F32),
            pltpu.VMEM((cells, LANES), F32),
            pltpu.VMEM((images, channels), F32),
            pltpu.VMEM((images, channels), F32),
            dma((len(blocks),)),
            dma((8,)),
            dma((2 * STEPS,)),
            dma((STEPS,)),
        ),
        grant=BIG,
    )


def dot(left, right, left_dim, right_dim):
    return lax.dot_general(
        left, right, (((left_dim,), (right_dim,)), ((), ())), preferred_element_type=F32
    )


def inverse_length(values):
    return lax.rsqrt(jnp.sum(values * values, axis=-1, keepdims=True) + EPSILON)


def length_back(unit, inverse, cotangent):
    return inverse * (cotangent - unit * jnp.sum(unit * cotangent, axis=-1, keepdims=True))


def hot_rows(ids_ref, rows):
    row = lax.broadcasted_iota(jnp.int32, (rows, IDS), 0)
    ids = jnp.zeros((rows, IDS), jnp.int32)
    for index in range(rows):
        ids = jnp.where(row == index, ids_ref[index], ids)
    lane = lax.broadcasted_iota(jnp.int32, (rows, IDS), 1)
    return jnp.where(ids == lane, 1.0, 0.0).astype(BF16)


def pack_kernel(text_hbm, ids_hbm, out_ref, text_ref, ids_ref, sems):
    copies = [
        pltpu.make_async_copy(text_hbm, text_ref, sems.at[0]),
        pltpu.make_async_copy(ids_hbm, ids_ref, sems.at[1]),
    ]
    for copy in copies:
        copy.start()
    for copy in copies:
        copy.wait()
    rows, width = text_ref.shape
    text = text_ref[...].astype(F32)
    unit = (text * inverse_length(text)).astype(BF16)
    hot = hot_rows(ids_ref, rows)
    for target in range(out_ref.shape[0]):
        out_ref[target, :, :width] = unit
        out_ref[target, :, width:] = hot


def line_kernel(plane_ref, after_ref, out_ref):
    del after_ref
    blocks, rows, _ = plane_ref.shape
    group = blocks // 2
    mine = lax.axis_index("x") * 2 + lax.axis_index("y_hi")
    for first in range(0, group, 2):
        four = [
            plane_ref[side * group + lax.rem(mine + first + offset, group)].astype(F32)
            for offset in range(2)
            for side in range(2)
        ]
        at = slice(2 * first * rows, 2 * (first + 2) * rows)
        out_ref[at, :] = jnp.concatenate(four, axis=0).astype(BF16)


def partial_kernel(received_ref, projection_ref, out_ref, columns_ref, hot_ref):
    group = received_ref.shape[0]
    share = projection_ref.shape[0]
    rows = jnp.concatenate([received_ref[owner].astype(F32) for owner in range(group)], axis=0)
    columns = rows[:, :share].astype(BF16)
    columns_ref[...] = columns
    hot_ref[...] = rows[:, share:].astype(BF16)
    partial = dot(columns, projection_ref[...], 1, 0).astype(BF16)
    for target in range(group):
        out_ref[target] = partial


def pair_kernel(
    partials_ref, hot_ref, projection_ref, near_ref, far_ref,
    scale_ref, shift_ref,
    stay_ref, send_ref, factors_ref,
    head_ref,
):
    group, images, width = partials_ref.shape
    scale, shift = scale_ref[0], shift_ref[0]
    embedded = partials_ref[0].astype(F32)
    for owner in range(1, group):
        embedded += partials_ref[owner].astype(F32)
    inverse = inverse_length(embedded)
    unit = embedded * inverse
    low = unit.astype(BF16)
    factors_ref[:, width : 2 * width] = low
    hot = hot_ref[...]

    def weigh(block):
        logits = scale * dot(low, block[:, :width], 1, 1) + shift
        signs = 2.0 * dot(hot, block[:, width:], 1, 1) - 1.0
        return (-signs * jax.nn.sigmoid(-signs * logits)).astype(BF16)

    image_grad = jnp.zeros((images, width), F32)
    for side, texts_ref in enumerate((near_ref, far_ref)):
        ring, rows, wide = texts_ref.shape
        for first in range(0, ring, 2):
            block = texts_ref[first : first + 2].reshape(2 * rows, wide)
            image_grad += dot(weigh(block), block[:, :width], 1, 0)
        own = jnp.concatenate([texts_ref[at, :OWN, :] for at in range(ring)], axis=0)
        factors_ref[:, 2 * width + side * LANES : 2 * width + (side + 1) * LANES] = weigh(own)
    embed = length_back(unit, inverse, scale * image_grad).astype(BF16)
    factors_ref[:, :width] = embed
    head = dot(embed, projection_ref[...], 1, 1)
    rows = images // group
    for owner in range(group):
        head_ref[owner] = head[owner * rows : (owner + 1) * rows]
    x, y_hi = lax.axis_index("x"), lax.axis_index("y_hi")
    for step in range(4):
        stay_ref[step] = head_ref[group_peer(x, y_hi, step, 0)]
        send_ref[step] = head_ref[group_peer(x, y_hi, step, 1)]


def merge_kernel(stay_ref, got_ref, s0, s1, s2, s3):
    for step, out_ref in enumerate((s0, s1, s2, s3)):
        out_ref[0] = stay_ref[step]
        out_ref[1] = got_ref[step]


def strip_make_kernel(mine_ref, theirs_ref, columns_ref, far_columns_ref, out_ref, rows_ref, near_ref, far_ref):
    width = (mine_ref.shape[1] - 2 * LANES) // 2
    line, strip_rows, half = out_ref.shape
    strip = columns_ref.shape[1] // line
    rows = (strip_rows - strip) // 2
    start = pl.multiple_of(lax.axis_index("core") * (width - half), LANES)

    def both(at):
        return jnp.concatenate([mine_ref[:, at], theirs_ref[:, at]], axis=0)

    columns = jnp.concatenate([columns_ref[...], far_columns_ref[...]], axis=0)
    rows_ref[...] = dot(columns, both(pl.ds(start, half)), 0, 0)
    low = both(pl.ds(pl.multiple_of(start + width, LANES), half))
    first, second = slice(2 * width, 2 * width + LANES), slice(2 * width + LANES, None)
    own = jnp.concatenate([mine_ref[:, first], theirs_ref[:, second]], axis=0)
    other = jnp.concatenate([mine_ref[:, second], theirs_ref[:, first]], axis=0)
    near_ref[...] = dot(own, low, 0, 0)
    far_ref[...] = dot(other, low, 0, 0)
    for target in range(line):
        place = target % (line // 2) * OWN + target // (line // 2) * rows
        at = slice(place, place + rows)
        stacked = jnp.concatenate(
            [rows_ref[target * strip : (target + 1) * strip], near_ref[at], far_ref[at]], axis=0
        )
        out_ref[target] = stacked.astype(BF16)


def strip_kernel(strips_ref, out_ref, mine_ref, theirs_ref):
    line, rows, half = strips_ref.shape
    texts = mine_ref.shape[0]
    strip = rows - 2 * texts
    total = strips_ref[0].astype(F32)
    for source in range(1, line):
        total += strips_ref[source].astype(F32)
    low = total[:strip].astype(BF16)
    for target in range(line):
        out_ref[target] = low
    mine_ref[...] = total[strip : strip + texts]
    theirs_ref[...] = total[strip + texts :]


def text_kernel(text_ref, mine_ref, got_ref, scale_ref, out_ref):
    width = text_ref.shape[1]
    text = text_ref[...].astype(F32)
    inverse = inverse_length(text)
    first = lax.axis_index("core") == 0
    mine, got = mine_ref[...], got_ref[...]
    left = jnp.where(first, mine, got)
    right = jnp.where(first, got, mine)
    grad = jnp.concatenate([left, right[:, 2 * HALF - width :]], axis=1)
    out_ref[...] = length_back(text * inverse, inverse, scale_ref[0] * grad)


def join_kernel(near_ref, far_ref, out_ref):
    core = lax.axis_index("core")
    width = out_ref.shape[1]

    def put(left, right):
        out_ref[:, :HALF] = left[...].astype(F32)
        out_ref[:, HALF:] = right[:, 2 * HALF - width :].astype(F32)

    pl.when(core == 0)(lambda: put(near_ref, far_ref))
    pl.when(core != 0)(lambda: put(far_ref, near_ref))


def exchange(blocks, axes):
    return lax.all_to_all(blocks, axes, 0, 0, tiled=True)


def swap_core(block):
    return lax.ppermute(block, "core", ((0, 1), (1, 0)))


def along_x(block, step):
    return lax.ppermute(block, "x", tuple((i, (i + step) % 4) for i in range(4)))


def local(
    features,
    text_embed,
    img_ids,
    txt_ids,
    kernel,
    norm_gain,
    head_gain,
    projection,
    logit_scale,
    logit_bias,
):
    rows, width = text_embed.shape
    share = projection.shape[0]
    group = lax.axis_size(GROUP)
    line = lax.axis_size(LINE)
    images = group * rows
    texts = line * rows
    strip = share // line
    dma = pltpu.SemaphoreType.DMA

    packed = call(
        pack_kernel,
        ((shape_of((line, rows, width + IDS), BF16), VMEM),),
        ((text_embed, HBM), (txt_ids, HBM)),
        "text_pack", 1,
        scratch=(
            pltpu.VMEM((rows, width), BF16), pltpu.SMEM((rows,), jnp.int32), dma((2,)),
        ),
        grant=BIG,
    )
    gathered = exchange(packed, PLANE)
    early_filtered, early_mean, early_inverse, pooled = block_forward_first(
        features, kernel, norm_gain
    )
    own_texts = call(
        line_kernel,
        ((shape_of((texts, width + IDS), BF16), VMEM),),
        ((gathered, VMEM), (early_mean, HBM)),
        "line_rows", 1,
    )
    near = lax.all_gather(own_texts, "z", axis=0, tiled=False)
    late_filtered, late_mean, late_inverse, normal, send = block_forward_second(
        features, kernel, norm_gain, pooled, head_gain, img_ids, own_texts, group
    )
    filtered = (early_filtered, late_filtered)
    mean = (early_mean, late_mean)
    inverse = (early_inverse, late_inverse)
    received = exchange(send, GROUP)
    partials, columns, hot = call(
        partial_kernel,
        (
            (shape_of((group, images, width), BF16), VMEM),
            (shape_of((images, share), BF16), VMEM),
            (shape_of((images, IDS), BF16), VMEM),
        ),
        ((received, VMEM), (projection, VMEM)),
        "partial_embed", 2,
    )
    far_columns = swap_core(columns)
    partials = exchange(partials, GROUP)
    near, partials = lax.optimization_barrier((near, partials))
    far = swap_core(near)
    stay, away, factors = call(
        pair_kernel,
        (
            (shape_of((4, rows, share), F32), VMEM),
            (shape_of((4, rows, share), F32), VMEM),
            (shape_of((images, 2 * width + 2 * LANES), BF16), VMEM),
        ),
        tuple((array, VMEM) for array in (partials, hot, projection, near, far))
        + ((logit_scale, SMEM), (logit_bias, SMEM)),
        "pairs", 4,
        scratch=(pltpu.VMEM((group, rows, share), F32),),
    )
    far_factors = swap_core(factors)
    got = lax.ppermute(away, "y_hi", ((0, 1), (1, 0)))
    strips = call(
        strip_make_kernel,
        ((shape_of((line, strip + 2 * rows, HALF), BF16), VMEM),),
        tuple((array, VMEM) for array in (factors, far_factors, columns, far_columns)),
        "strip_make", 2,
        scratch=(
            pltpu.VMEM((share, HALF), F32),
            pltpu.VMEM((LANES, HALF), F32),
            pltpu.VMEM((LANES, HALF), F32),
        ),
    )
    strips = exchange(strips, LINE)
    merged = call(
        merge_kernel,
        ((shape_of((2, rows, share), F32), VMEM),) * 4,
        ((stay, VMEM), (got, VMEM)),
        "head_merge", 1,
    )
    blocks = [merged[0]] + [along_x(merged[step], step) for step in (1, 2, 3)]
    shared = (normal, norm_gain, head_gain, filtered, mean, inverse, kernel)
    strips, *blocks = lax.optimization_barrier((strips, *blocks))
    sums, mine, theirs = call(
        strip_kernel,
        (
            (shape_of((line, strip, HALF), BF16), VMEM),
            (shape_of((rows, HALF), F32), VMEM),
            (shape_of((rows, HALF), F32), VMEM),
        ),
        ((strips, VMEM),),
        "strip_sum", 1,
    )
    near_half = exchange(sums, LINE).reshape(share, HALF)
    grad_text = call(
        text_kernel,
        ((shape_of((rows, width), F32), VMEM),),
        ((text_embed, VMEM), (mine, VMEM), (swap_core(theirs), VMEM), (logit_scale, SMEM)),
        "text_grad", 1,
    )
    grad_features = block_backward(blocks, *shared, mine)
    near_half, grad_features, grad_text = lax.optimization_barrier(
        (near_half, grad_features, grad_text)
    )
    grad_proj = call(
        join_kernel,
        ((shape_of((share, width), F32), VMEM),),
        ((near_half, VMEM), (swap_core(near_half), VMEM)),
        "proj_join", 2,
    )
    grad_features = grad_features.reshape(features.shape)
    return (grad_features, grad_text, grad_proj)


def solution(mesh):
    fine = Mesh(mesh.devices.reshape(SIZES), AXES)
    placed = (
        P(ALL, None, None, None),
        P(ALL, None),
        P(ALL),
        P(ALL),
        P(),
        P(),
        P(),
        P(GROUP, None),
        P(),
        P(),
    )
    return jax.shard_map(
        local,
        mesh=fine,
        in_specs=placed,
        out_specs=(P(ALL, None, None, None), P(ALL, None), P(GROUP, None)),
        check_vma=False,
    )
```

```python
import jax
import jax.numpy as jnp
from jax import lax
from jax.experimental import pallas as pl
from jax.experimental.pallas import tpu as pltpu
from jax.sharding import Mesh, PartitionSpec as P

EPSILON = 1e-06
AXES = ("y_lo", "z", "core", "x", "y_hi")
SIZES = (2, 8, 2, 4, 2)
ALL = AXES
GROUP = ("x", "y_hi")
LINE = ("y_lo", "z")
MIB = 1024 * 1024
BIG = 60
IDS = 128
HALF = 640
LANES = 128
SIDE = 8
CELLS = 64
TAPS = 7
VMEM = pl.BlockSpec(memory_space=pltpu.VMEM)
SMEM = pl.BlockSpec(memory_space=pltpu.SMEM)
HBM = pl.BlockSpec(memory_space=pltpu.HBM)
STEPS = 4
PEERS = tuple((step_x, step_y) for step_x in range(4) for step_y in range(2))
BF16 = jnp.bfloat16
F32 = jnp.float32


def shape_of(dims, dtype):
    return jax.ShapeDtypeStruct(dims, dtype)


def call(body, outs, operands, name, micros, scratch=(), grant=40):
    specs = tuple(spec for _, spec in outs)
    shapes = tuple(shape for shape, _ in outs)
    single = len(outs) == 1
    return pl.pallas_call(
        body,
        out_shape=shapes[0] if single else shapes,
        in_specs=[spec for _, spec in operands],
        out_specs=specs[0] if single else specs,
        scratch_shapes=list(scratch),
        compiler_params=pltpu.CompilerParams(vmem_limit_bytes=grant * MIB),
        cost_estimate=pl.CostEstimate(
            flops=0, bytes_accessed=int(micros * 3e6), transcendentals=0
        ),
        name=name,
    )(*[operand for operand, _ in operands])


def group_peer(x, y_hi, step_x, step_y):
    return lax.rem(x + step_x, 4) * 2 + lax.rem(y_hi + step_y, 2)


def tap_weights(kernel_ref, at, column, flip):
    place = lax.broadcasted_iota(jnp.int32, (SIDE, LANES), 0) + (column - TAPS // 2)
    valid = (place >= 0) & (place < SIDE)
    weights = []
    for row in range(TAPS):
        if flip:
            line = kernel_ref[TAPS - 1 - row, pl.ds(TAPS - 1 - column, 1), at]
        else:
            line = kernel_ref[row, pl.ds(column, 1), at]
        weights.append(jnp.where(valid, jnp.broadcast_to(line, (SIDE, LANES)), 0.0))
    return weights


def filter_rows(fields, sums, kernel_ref, at, flip):
    for column in range(TAPS):
        weights = tap_weights(kernel_ref, at, column, flip)
        shift = (TAPS // 2 - column) % SIDE
        for field, total in zip(fields, sums):
            for source in range(SIDE):
                moved = field[source] if shift == 0 else pltpu.roll(field[source], shift, 0)
                for row in range(TAPS):
                    target = source - row + TAPS // 2
                    if 0 <= target < SIDE:
                        term = moved * weights[row]
                        total[target] = term if total[target] is None else total[target] + term
    return sums


def forward_kernel(
    field_hbm, kernel_hbm, gain_hbm, head_gain_hbm, ids_hbm,
    filtered_hbm, mean_ref, inverse_ref, normal_ref, send_ref,
    field_ref, kernel_ref, gain_ref, head_gain_ref, ids_ref, filtered_ref, pooled_ref, total_ref, mixed_ref,
    field_sems, kernel_sems, small_sems, out_sems,
):
    images = field_ref.shape[0] // CELLS
    channels = field_ref.shape[1]
    chunks = channels // LANES
    part = 1.0 / channels
    block = channels // STEPS
    per_block = chunks // STEPS

    def block_at(step):
        return pl.ds(pl.multiple_of(step * block, LANES), block)

    def field_copy(step):
        at = block_at(step)
        return pltpu.make_async_copy(field_hbm.at[:, at], field_ref.at[:, at], field_sems.at[step])

    def kernel_copy(step):
        at = block_at(step)
        return pltpu.make_async_copy(
            kernel_hbm.at[:, :, at], kernel_ref.at[:, :, at], kernel_sems.at[step]
        )

    def filtered_copy(step):
        at = block_at(step)
        return pltpu.make_async_copy(filtered_ref.at[:, at], filtered_hbm.at[:, at], out_sems.at[step])

    small_copies = [
        pltpu.make_async_copy(gain_hbm, gain_ref, small_sems.at[0]),
        pltpu.make_async_copy(head_gain_hbm, head_gain_ref, small_sems.at[1]),
        pltpu.make_async_copy(ids_hbm, ids_ref, small_sems.at[2]),
    ]
    for step in range(STEPS):
        field_copy(step).start()
        kernel_copy(step).start()
    for copy in small_copies:
        copy.start()

    total_ref[...] = jnp.zeros_like(total_ref)

    def filter_chunk(chunk, carry):
        step = chunk // per_block

        @pl.when(chunk == step * per_block)
        def _():
            field_copy(step).wait()
            kernel_copy(step).wait()

        at = pl.ds(pl.multiple_of(chunk * LANES, LANES), LANES)
        for first in range(0, images, 4):
            fields = []
            for image in range(first, first + 4):
                rows = []
                for pair in range(SIDE // 2):
                    both = field_ref[pl.ds(image * CELLS + pair * 2 * SIDE, 2 * SIDE), at]
                    both = both.astype(jnp.float32)
                    rows += [both[:SIDE], both[SIDE:]]
                fields.append(rows)
                level = rows[0]
                for row in rows[1:]:
                    level = level + row
                mixed_ref[pl.ds(image * SIDE, SIDE), at] = level
            sums = [[None] * SIDE for _ in fields]
            filter_rows(fields, sums, kernel_ref, at, False)
            for offset, total in enumerate(sums):
                for row in range(SIDE):
                    cells = pl.ds((first + offset) * CELLS + row * SIDE, SIDE)
                    filtered_ref[cells, at] = total[row]
                    total_ref[cells, :] += total[row]
        return carry

    lax.fori_loop(0, chunks, filter_chunk, 0)
    for step in range(STEPS):
        filtered_copy(step).start()
    for copy in small_copies:
        copy.wait()
    mean_ref[...] = jnp.broadcast_to(
        jnp.sum(total_ref[...], axis=1, keepdims=True) * part, mean_ref.shape
    )

    for image in range(images):
        cells = pl.ds(image * CELLS, CELLS)
        average = mean_ref[cells, :]

        def spread_chunk(chunk, squares):
            at = pl.ds(pl.multiple_of(chunk * LANES, LANES), LANES)
            centred = filtered_ref[cells, at] - average
            return squares + centred * centred

        squares = lax.fori_loop(
            0, chunks, spread_chunk, jnp.zeros((CELLS, LANES), jnp.float32), unroll=8
        )
        spread = jnp.sum(squares, axis=1, keepdims=True) * part
        inverse_ref[cells, :] = jnp.broadcast_to(lax.rsqrt(spread + EPSILON), (CELLS, LANES))

    for image in range(images):
        cells = pl.ds(image * CELLS, CELLS)
        average = mean_ref[cells, :]
        inverse = inverse_ref[cells, :]

        def pool_chunk(chunk, carry):
            at = pl.ds(pl.multiple_of(chunk * LANES, LANES), LANES)
            normal = (filtered_ref[cells, at] - average) * inverse
            level = jnp.sum(normal.reshape(SIDE, SIDE, LANES), axis=0)
            spot = pl.ds(image * SIDE, SIDE)
            mixed_ref[spot, at] = mixed_ref[spot, at] + level * gain_ref[:, at]
            return carry

        lax.fori_loop(0, chunks, pool_chunk, 0, unroll=8)
        pooled_ref[pl.ds(image, 1), :] = jnp.sum(
            mixed_ref[pl.ds(image * SIDE, SIDE), :], axis=0, keepdims=True
        ) * (1.0 / CELLS)

    pooled = pooled_ref[...]
    centred = pooled - jnp.sum(pooled, axis=1, keepdims=True) * part
    spread = jnp.sum(centred * centred, axis=1, keepdims=True) * part
    head_inverse = lax.rsqrt(spread + EPSILON)
    normal = centred * head_inverse
    normal_ref[:, :channels] = normal
    normal_ref[:, channels:] = jnp.broadcast_to(head_inverse, (images, LANES))
    head_input = (normal * head_gain_ref[...]).astype(jnp.bfloat16)
    hot = hot_rows(ids_ref, images)
    group = send_ref.shape[0]
    share = channels // group
    for owner in range(group):
        send_ref[owner, :, :share] = head_input[:, owner * share : (owner + 1) * share]
        send_ref[owner, :, share:] = hot
    for step in range(STEPS):
        filtered_copy(step).wait()


def block_forward(features, kernel, norm_gain, head_gain, img_ids, group):
    images, channels = features.shape[0], features.shape[3]
    cells = images * CELLS
    dma = pltpu.SemaphoreType.DMA
    return call(
        forward_kernel,
        (
            (shape_of((cells, channels), F32), HBM),
            (shape_of((cells, LANES), F32), VMEM),
            (shape_of((cells, LANES), F32), VMEM),
            (shape_of((images, channels + LANES), F32), VMEM),
            (shape_of((group, images, channels // group + IDS), BF16), VMEM),
        ),
        (
            (features.reshape(cells, channels), HBM),
            (kernel, HBM),
            (norm_gain.reshape(1, channels), HBM),
            (head_gain.reshape(1, channels), HBM),
            (img_ids, HBM),
        ),
        "block_forward",
        14,
        scratch=(
            pltpu.VMEM((cells, channels), BF16),
            pltpu.VMEM(kernel.shape, F32),
            pltpu.VMEM((1, channels), F32),
            pltpu.VMEM((1, channels), F32),
            pltpu.SMEM(img_ids.shape, jnp.int32),
            pltpu.VMEM((cells, channels), F32),
            pltpu.VMEM((images, channels), F32),
            pltpu.VMEM((cells, LANES), F32),
            pltpu.VMEM((images * SIDE, channels), F32),
            dma((STEPS,)),
            dma((STEPS,)),
            dma((3,)),
            dma((STEPS,)),
        ),
        grant=BIG,
    )


def lean_kernel(
    s0, s1, s2, s3, normal_ref, gain_ref, head_gain_ref, filtered_hbm, mean_ref, inverse_ref,
    slopes_ref, lean_ref,
    filtered_ref, pull_ref, tilt_ref, filtered_sems,
):
    images, channels = pull_ref.shape
    blocks = (s0, s1, s2, s3)
    share = channels // len(PEERS)
    wide = channels // STEPS

    def block_at(step):
        return pl.ds(pl.multiple_of(step * wide, LANES), wide)

    filtered_copies = [
        pltpu.make_async_copy(
            filtered_hbm.at[:, block_at(step)], filtered_ref.at[:, block_at(step)],
            filtered_sems.at[step],
        )
        for step in range(STEPS)
    ]
    for copy in filtered_copies:
        copy.start()
    chunks = channels // LANES
    per_block = chunks // STEPS
    part = 1.0 / channels

    x, y_hi = lax.axis_index("x"), lax.axis_index("y_hi")
    for step_x, step_y in PEERS:
        owner = group_peer(x, y_hi, 4 - step_x, step_y)
        at = pl.ds(pl.multiple_of(owner * share, LANES), share)
        tilt_ref[:, at] = blocks[step_x][step_y] * head_gain_ref[:, at]
    cotangent = tilt_ref[...]
    normal = normal_ref[:, :channels]
    level = jnp.sum(cotangent, axis=1, keepdims=True) * part
    lean = jnp.sum(cotangent * normal, axis=1, keepdims=True) * part
    pooled_grad = normal_ref[:, channels : channels + 1] * (cotangent - level - normal * lean)
    even = pooled_grad * (1.0 / CELLS)
    slopes_ref[0] = even
    pull = even * gain_ref[...]
    pull_ref[...] = pull
    slopes_ref[1] = pull - jnp.sum(pull, axis=1, keepdims=True) * part

    for step in range(STEPS):
        filtered_copies[step].wait()
        for image in range(images):
            spot = pl.ds(image * CELLS, CELLS)
            average = mean_ref[spot, :]

            def lean_chunk(chunk, total, spot=spot, average=average, image=image):
                at = pl.ds(pl.multiple_of(chunk * LANES, LANES), LANES)
                return total + (filtered_ref[spot, at] - average) * pull_ref[pl.ds(image, 1), at]

            total = jnp.zeros((CELLS, LANES), F32) if step == 0 else lean_ref[spot, :]
            lean_ref[spot, :] = lax.fori_loop(
                step * per_block, (step + 1) * per_block, lean_chunk, total, unroll=True
            )
    inverse = inverse_ref[...]
    mean_lean = jnp.sum(lean_ref[...], axis=1, keepdims=True) * part
    lean_ref[...] = inverse * (inverse * (inverse * mean_lean))


def backward_kernel(
    slopes_hbm, lean_hbm, filtered_hbm, mean_hbm, inverse_hbm, kernel_hbm, after_hbm,
    out_hbm,
    slopes_ref, lean_ref, filtered_ref, mean_ref, inverse_ref, kernel_ref, out_ref,
    small_sems, filtered_sems, kernel_sems, out_sems,
):
    del after_hbm
    images, channels = slopes_ref.shape[1:]
    even_ref, tilt_ref = slopes_ref.at[0], slopes_ref.at[1]
    wide = channels // STEPS
    chunks = channels // LANES
    per_block = chunks // STEPS

    def block_at(step):
        return pl.ds(pl.multiple_of(step * wide, LANES), wide)

    def out_copy(step):
        at = block_at(step)
        return pltpu.make_async_copy(out_ref.at[:, at], out_hbm.at[:, at], out_sems.at[step])

    def filtered_copy(step):
        at = block_at(step)
        return pltpu.make_async_copy(
            filtered_hbm.at[:, at], filtered_ref.at[:, at], filtered_sems.at[step]
        )

    def kernel_copy(step):
        at = block_at(step)
        return pltpu.make_async_copy(
            kernel_hbm.at[:, :, at], kernel_ref.at[:, :, at], kernel_sems.at[step]
        )

    small_copies = [
        pltpu.make_async_copy(source, target, small_sems.at[index])
        for index, (source, target) in enumerate((
            (slopes_hbm, slopes_ref), (lean_hbm, lean_ref), (mean_hbm, mean_ref),
            (inverse_hbm, inverse_ref),
        ))
    ]
    for copy in small_copies:
        copy.start()
    for step in range(STEPS):
        filtered_copy(step).start()
        kernel_copy(step).start()
    for copy in small_copies:
        copy.wait()

    def filter_chunk(chunk, carry):
        step = chunk // per_block

        @pl.when(chunk == step * per_block)
        def _():
            filtered_copy(step).wait()
            kernel_copy(step).wait()

        at = pl.ds(pl.multiple_of(chunk * LANES, LANES), LANES)
        for first in range(0, images, 2):
            fields = []
            sums = []
            for image in range(first, first + 2):
                tilt = jnp.broadcast_to(tilt_ref[pl.ds(image, 1), at], (SIDE, LANES))
                even = jnp.broadcast_to(even_ref[pl.ds(image, 1), at], (SIDE, LANES))
                rows = []
                for row in range(SIDE):
                    spot = pl.ds(image * CELLS + row * SIDE, SIDE)
                    rows.append(
                        inverse_ref[spot, :] * tilt
                        - lean_ref[spot, :] * (filtered_ref[spot, at] - mean_ref[spot, :])
                    )
                fields.append(rows)
                sums.append([even] * SIDE)
            filter_rows(fields, sums, kernel_ref, at, True)
            for offset, total in enumerate(sums):
                for half in range(SIDE // 2):
                    two = jnp.concatenate(total[2 * half : 2 * half + 2], axis=0)
                    spot = pl.ds((first + offset) * CELLS + half * 2 * SIDE, 2 * SIDE)
                    out_ref[spot, at] = two.astype(jnp.bfloat16)
        @pl.when(chunk == step * per_block + per_block - 1)
        def _():
            out_copy(step).start()

        return carry

    lax.fori_loop(0, chunks, filter_chunk, 0)
    for step in range(STEPS):
        out_copy(step).wait()


def block_lean(blocks, normal, norm_gain, head_gain, filtered, mean, inverse):
    cells, channels = filtered.shape
    images = cells // CELLS
    return call(
        lean_kernel,
        (
            (shape_of((2, images, channels), F32), VMEM),
            (shape_of((cells, LANES), F32), VMEM),
        ),
        tuple(
            (array, VMEM)
            for array in (
                *blocks, normal, norm_gain.reshape(1, channels), head_gain.reshape(1, channels)
            )
        )
        + ((filtered, HBM), (mean, VMEM), (inverse, VMEM)),
        "block_lean", 3,
        scratch=(
            pltpu.VMEM((cells, channels), F32),
            pltpu.VMEM((images, channels), F32),
            pltpu.VMEM((images, channels), F32),
            pltpu.SemaphoreType.DMA((STEPS,)),
        ),
        grant=BIG,
    )


def block_backward(slopes, lean, filtered, mean, inverse, kernel, after):
    cells, channels = filtered.shape
    dma = pltpu.SemaphoreType.DMA
    return call(
        backward_kernel,
        ((shape_of((cells, channels), BF16), HBM),),
        tuple((array, HBM) for array in (slopes, lean, filtered, mean, inverse, kernel, after)),
        "block_backward", 13,
        scratch=(
            pltpu.VMEM(slopes.shape, F32),
            pltpu.VMEM((cells, LANES), F32),
            pltpu.VMEM((cells, channels), F32),
            pltpu.VMEM((cells, LANES), F32),
            pltpu.VMEM((cells, LANES), F32),
            pltpu.VMEM(kernel.shape, F32),
            pltpu.VMEM((cells, channels), BF16),
            dma((4,)),
            dma((STEPS,)),
            dma((STEPS,)),
            dma((STEPS,)),
        ),
        grant=BIG,
    )


def dot(left, right, left_dim, right_dim):
    return lax.dot_general(
        left, right, (((left_dim,), (right_dim,)), ((), ())), preferred_element_type=F32
    )


def inverse_length(values):
    return lax.rsqrt(jnp.sum(values * values, axis=-1, keepdims=True) + EPSILON)


def length_back(unit, inverse, cotangent):
    return inverse * (cotangent - unit * jnp.sum(unit * cotangent, axis=-1, keepdims=True))


def hot_rows(ids_ref, rows):
    row = lax.broadcasted_iota(jnp.int32, (rows, IDS), 0)
    ids = jnp.zeros((rows, IDS), jnp.int32)
    for index in range(rows):
        ids = jnp.where(row == index, ids_ref[index], ids)
    lane = lax.broadcasted_iota(jnp.int32, (rows, IDS), 1)
    return jnp.where(ids == lane, 1.0, 0.0).astype(BF16)


def pack_kernel(text_hbm, ids_hbm, out_ref, text_ref, ids_ref, sems):
    copies = [
        pltpu.make_async_copy(text_hbm, text_ref, sems.at[0]),
        pltpu.make_async_copy(ids_hbm, ids_ref, sems.at[1]),
    ]
    for copy in copies:
        copy.start()
    for copy in copies:
        copy.wait()
    rows, width = text_ref.shape
    text = text_ref[...].astype(F32)
    unit = (text * inverse_length(text)).astype(BF16)
    hot = hot_rows(ids_ref, rows)
    for target in range(out_ref.shape[0]):
        out_ref[target, :, :width] = unit
        out_ref[target, :, width:] = hot


def line_kernel(line_ref, out_ref):
    line, rows, _ = line_ref.shape
    for first in range(0, line, 4):
        four = [line_ref[first + offset].astype(F32) for offset in range(4)]
        at = slice(first * rows, (first + 4) * rows)
        out_ref[at, :] = jnp.concatenate(four, axis=0).astype(BF16)


def join_texts_kernel(own_ref, next_ref, after_ref, out_ref):
    del after_ref
    texts = own_ref.shape[0]
    out_ref[:texts, :] = own_ref[...]
    out_ref[texts:, :] = next_ref[...]


def partial_kernel(received_ref, projection_ref, out_ref, columns_ref, hot_ref):
    group = received_ref.shape[0]
    share = projection_ref.shape[0]
    rows = jnp.concatenate([received_ref[owner].astype(F32) for owner in range(group)], axis=0)
    columns = rows[:, :share].astype(BF16)
    columns_ref[...] = columns
    hot_ref[...] = rows[:, share:].astype(BF16)
    partial = dot(columns, projection_ref[...], 1, 0).astype(BF16)
    for target in range(group):
        out_ref[target] = partial


def pair_kernel(
    partials_ref, hot_ref, projection_ref, t0, t1, t2, t3, t4, t5, t6, t7,
    scale_ref, shift_ref,
    stay_ref, send_ref, factors_ref,
    head_ref,
):
    group, images, width = partials_ref.shape
    blocks = (t0, t1, t2, t3, t4, t5, t6, t7)
    scale, shift = scale_ref[0], shift_ref[0]
    embedded = partials_ref[0].astype(F32)
    for owner in range(1, group):
        embedded += partials_ref[owner].astype(F32)
    inverse = inverse_length(embedded)
    unit = embedded * inverse
    low = unit.astype(BF16)
    factors_ref[:, width : 2 * width] = low
    hot = hot_ref[...]
    weights = []
    for block in blocks:
        logits = scale * dot(low, block[:, :width], 1, 1) + shift
        signs = 2.0 * dot(hot, block[:, width:], 1, 1) - 1.0
        weights.append((-signs * jax.nn.sigmoid(-signs * logits)).astype(BF16))
    image_grad = dot(weights[0], t0[:, :width], 1, 0)
    for weight, block in zip(weights[1:], blocks[1:]):
        image_grad += dot(weight, block[:, :width], 1, 0)
    embed = length_back(unit, inverse, scale * image_grad).astype(BF16)
    factors_ref[:, :width] = embed
    factors_ref[:, 2 * width : 2 * width + LANES] = weights[0]
    factors_ref[:, 2 * width + LANES :] = weights[4]
    head = dot(embed, projection_ref[...], 1, 1)
    rows = images // group
    for owner in range(group):
        head_ref[owner] = head[owner * rows : (owner + 1) * rows]
    x, y_hi = lax.axis_index("x"), lax.axis_index("y_hi")
    for step in range(4):
        stay_ref[step] = head_ref[group_peer(x, y_hi, step, 0)]
        send_ref[step] = head_ref[group_peer(x, y_hi, step, 1)]


def merge_kernel(stay_ref, got_ref, s0, s1, s2, s3):
    for step, out_ref in enumerate((s0, s1, s2, s3)):
        out_ref[0] = stay_ref[step]
        out_ref[1] = got_ref[step]


def strip_make_kernel(mine_ref, theirs_ref, columns_ref, far_columns_ref, out_ref, rows_ref, near_ref, far_ref):
    width = (mine_ref.shape[1] - 2 * LANES) // 2
    line, strip_rows, half = out_ref.shape
    strip = columns_ref.shape[1] // line
    rows = (strip_rows - strip) // 2
    texts = line * rows
    start = pl.multiple_of(lax.axis_index("core") * (width - half), LANES)

    def both(at):
        return jnp.concatenate([mine_ref[:, at], theirs_ref[:, at]], axis=0)

    columns = jnp.concatenate([columns_ref[...], far_columns_ref[...]], axis=0)
    rows_ref[...] = dot(columns, both(pl.ds(start, half)), 0, 0)
    low = both(pl.ds(pl.multiple_of(start + width, LANES), half))
    first = slice(2 * width, 2 * width + texts)
    second = slice(2 * width + LANES, 2 * width + LANES + texts)
    own = jnp.concatenate([mine_ref[:, first], theirs_ref[:, second]], axis=0)
    other = jnp.concatenate([mine_ref[:, second], theirs_ref[:, first]], axis=0)
    near_ref[...] = dot(own, low, 0, 0)
    far_ref[...] = dot(other, low, 0, 0)
    for target in range(line):
        at = slice(target * rows, (target + 1) * rows)
        stacked = jnp.concatenate(
            [rows_ref[target * strip : (target + 1) * strip], near_ref[at], far_ref[at]], axis=0
        )
        out_ref[target] = stacked.astype(BF16)


def strip_kernel(strips_ref, out_ref, mine_hbm, theirs_hbm, texts_ref, sems):
    line, rows, half = strips_ref.shape
    texts = texts_ref.shape[1]
    strip = rows - 2 * texts
    total = strips_ref[0].astype(F32)
    for source in range(1, line):
        total += strips_ref[source].astype(F32)
    texts_ref[0] = total[strip : strip + texts]
    texts_ref[1] = total[strip + texts :]
    copies = [
        pltpu.make_async_copy(texts_ref.at[side], target, sems.at[side])
        for side, target in enumerate((mine_hbm, theirs_hbm))
    ]
    for copy in copies:
        copy.start()
    low = total[:strip].astype(BF16)
    for target in range(line):
        out_ref[target] = low
    for copy in copies:
        copy.wait()


def text_kernel(text_ref, mine_ref, got_ref, scale_ref, out_ref):
    width = text_ref.shape[1]
    text = text_ref[...].astype(F32)
    inverse = inverse_length(text)
    first = lax.axis_index("core") == 0
    mine, got = mine_ref[...], got_ref[...]
    left = jnp.where(first, mine, got)
    right = jnp.where(first, got, mine)
    grad = jnp.concatenate([left, right[:, 2 * HALF - width :]], axis=1)
    out_ref[...] = length_back(text * inverse, inverse, scale_ref[0] * grad)


def join_kernel(near_ref, far_ref, out_ref):
    core = lax.axis_index("core")
    width = out_ref.shape[1]

    def put(left, right):
        out_ref[:, :HALF] = left[...].astype(F32)
        out_ref[:, HALF:] = right[:, 2 * HALF - width :].astype(F32)

    pl.when(core == 0)(lambda: put(near_ref, far_ref))
    pl.when(core != 0)(lambda: put(far_ref, near_ref))


def exchange(blocks, axes):
    return lax.all_to_all(blocks, axes, 0, 0, tiled=True)


def swap_core(block):
    return lax.ppermute(block, "core", ((0, 1), (1, 0)))


def along_x(block, step):
    return lax.ppermute(block, "x", tuple((i, (i + step) % 4) for i in range(4)))


def local(
    features,
    text_embed,
    img_ids,
    txt_ids,
    kernel,
    norm_gain,
    head_gain,
    projection,
    logit_scale,
    logit_bias,
):
    rows, width = text_embed.shape
    share = projection.shape[0]
    group = lax.axis_size(GROUP)
    line = lax.axis_size(LINE)
    images = group * rows
    texts = line * rows
    strip = share // line
    dma = pltpu.SemaphoreType.DMA

    packed = call(
        pack_kernel,
        ((shape_of((line, rows, width + IDS), BF16), VMEM),),
        ((text_embed, HBM), (txt_ids, HBM)),
        "text_pack", 1,
        scratch=(
            pltpu.VMEM((rows, width), BF16), pltpu.SMEM((rows,), jnp.int32), dma((2,)),
        ),
        grant=BIG,
    )
    gathered = exchange(packed, LINE)
    filtered, mean, inverse, normal, send = block_forward(
        features, kernel, norm_gain, head_gain, img_ids, group
    )
    gathered, send = lax.optimization_barrier((gathered, send))
    received = exchange(send, GROUP)
    partials, columns, hot = call(
        partial_kernel,
        (
            (shape_of((group, images, width), BF16), VMEM),
            (shape_of((images, share), BF16), VMEM),
            (shape_of((images, IDS), BF16), VMEM),
        ),
        ((received, VMEM), (projection, VMEM)),
        "partial_embed", 2,
    )
    own_line = call(
        line_kernel, ((shape_of((texts, width + IDS), BF16), VMEM),), ((gathered, VMEM),),
        "line_rows", 1,
    )
    next_line = lax.ppermute(own_line, "y_hi", ((0, 1), (1, 0)))
    near = [
        call(
            join_texts_kernel,
            ((shape_of((2 * texts, width + IDS), BF16), VMEM),),
            ((own_line, VMEM), (next_line, VMEM), (columns, VMEM)),
            "join_texts", 1,
        )
    ]
    near += [along_x(near[0], step) for step in (1, 3, 2)]
    far = [swap_core(block) for block in near]
    far_columns = swap_core(columns)
    partials = exchange(partials, GROUP)
    stay, away, factors = call(
        pair_kernel,
        (
            (shape_of((4, rows, share), F32), VMEM),
            (shape_of((4, rows, share), F32), VMEM),
            (shape_of((images, 2 * width + 2 * LANES), BF16), VMEM),
        ),
        tuple((array, VMEM) for array in (partials, hot, projection, *near, *far))
        + ((logit_scale, SMEM), (logit_bias, SMEM)),
        "pairs", 4,
        scratch=(pltpu.VMEM((group, rows, share), F32),),
    )
    far_factors = swap_core(factors)
    got = lax.ppermute(away, "y_hi", ((0, 1), (1, 0)))
    strips = call(
        strip_make_kernel,
        ((shape_of((line, strip + 2 * rows, HALF), BF16), VMEM),),
        tuple((array, VMEM) for array in (factors, far_factors, columns, far_columns)),
        "strip_make", 2,
        scratch=(
            pltpu.VMEM((share, HALF), F32),
            pltpu.VMEM((texts, HALF), F32),
            pltpu.VMEM((texts, HALF), F32),
        ),
    )
    strips = exchange(strips, LINE)
    merged = call(
        merge_kernel,
        ((shape_of((2, rows, share), F32), VMEM),) * 4,
        ((stay, VMEM), (got, VMEM)),
        "head_merge", 1,
    )
    blocks = [merged[0]] + [along_x(merged[step], step) for step in (1, 2, 3)]
    slopes, lean = block_lean(blocks, normal, norm_gain, head_gain, filtered, mean, inverse)
    strips, slopes, lean = lax.optimization_barrier((strips, slopes, lean))
    sums, mine, theirs = call(
        strip_kernel,
        (
            (shape_of((line, strip, HALF), BF16), VMEM),
            (shape_of((rows, HALF), F32), HBM),
            (shape_of((rows, HALF), F32), HBM),
        ),
        ((strips, VMEM),),
        "strip_sum", 1,
        scratch=(pltpu.VMEM((2, rows, HALF), F32), dma((2,))),
    )
    near_half = exchange(sums, LINE).reshape(share, HALF)
    grad_text = call(
        text_kernel,
        ((shape_of((rows, width), F32), VMEM),),
        ((text_embed, VMEM), (mine, VMEM), (swap_core(theirs), VMEM), (logit_scale, SMEM)),
        "text_grad", 1,
    )
    grad_features = block_backward(slopes, lean, filtered, mean, inverse, kernel, mine)
    near_half, grad_features, grad_text = lax.optimization_barrier(
        (near_half, grad_features, grad_text)
    )
    grad_proj = call(
        join_kernel,
        ((shape_of((share, width), F32), VMEM),),
        ((near_half, VMEM), (swap_core(near_half), VMEM)),
        "proj_join", 2,
    )
    grad_features = grad_features.reshape(features.shape)
    return (grad_features, grad_text, grad_proj)


def solution(mesh):
    fine = Mesh(mesh.devices.reshape(SIZES), AXES)
    placed = (
        P(ALL, None, None, None),
        P(ALL, None),
        P(ALL),
        P(ALL),
        P(),
        P(),
        P(),
        P(GROUP, None),
        P(),
        P(),
    )
    return jax.shard_map(
        local,
        mesh=fine,
        in_specs=placed,
        out_specs=(P(ALL, None, None, None), P(ALL, None), P(GROUP, None)),
        check_vma=False,
    )
```

```python
import jax
import jax.numpy as jnp
from jax import lax
from jax.experimental import pallas as pl
from jax.experimental.pallas import tpu as pltpu
from jax.sharding import Mesh, PartitionSpec as P

EPSILON = 1e-06
AXES = ("y_lo", "z", "core", "x", "y_hi")
SIZES = (2, 8, 2, 4, 2)
ALL = AXES
GROUP = ("x", "y_hi")
LINE = ("y_lo", "z")
MIB = 1024 * 1024
BIG = 60
IDS = 128
HALF = 640
LANES = 128
SIDE = 8
CELLS = 64
TAPS = 7
VMEM = pl.BlockSpec(memory_space=pltpu.VMEM)
SMEM = pl.BlockSpec(memory_space=pltpu.SMEM)
HBM = pl.BlockSpec(memory_space=pltpu.HBM)
STEPS = 4
PEERS = tuple((step_x, step_y) for step_x in range(4) for step_y in range(2))
BF16 = jnp.bfloat16
F32 = jnp.float32


def shape_of(dims, dtype):
    return jax.ShapeDtypeStruct(dims, dtype)


def call(body, outs, operands, name, micros, scratch=(), grant=40):
    specs = tuple(spec for _, spec in outs)
    shapes = tuple(shape for shape, _ in outs)
    single = len(outs) == 1
    return pl.pallas_call(
        body,
        out_shape=shapes[0] if single else shapes,
        in_specs=[spec for _, spec in operands],
        out_specs=specs[0] if single else specs,
        scratch_shapes=list(scratch),
        compiler_params=pltpu.CompilerParams(vmem_limit_bytes=grant * MIB),
        cost_estimate=pl.CostEstimate(
            flops=0, bytes_accessed=int(micros * 3e6), transcendentals=0
        ),
        name=name,
    )(*[operand for operand, _ in operands])


def group_peer(x, y_hi, step_x, step_y):
    return lax.rem(x + step_x, 4) * 2 + lax.rem(y_hi + step_y, 2)


def tap_weights(kernel_ref, at, column, flip):
    place = lax.broadcasted_iota(jnp.int32, (SIDE, LANES), 0) + (column - TAPS // 2)
    valid = (place >= 0) & (place < SIDE)
    weights = []
    for row in range(TAPS):
        if flip:
            line = kernel_ref[TAPS - 1 - row, pl.ds(TAPS - 1 - column, 1), at]
        else:
            line = kernel_ref[row, pl.ds(column, 1), at]
        weights.append(jnp.where(valid, jnp.broadcast_to(line, (SIDE, LANES)), 0.0))
    return weights


def filter_rows(fields, sums, kernel_ref, at, flip):
    for column in range(TAPS):
        weights = tap_weights(kernel_ref, at, column, flip)
        shift = (TAPS // 2 - column) % SIDE
        for field, total in zip(fields, sums):
            for source in range(SIDE):
                moved = field[source] if shift == 0 else pltpu.roll(field[source], shift, 0)
                for row in range(TAPS):
                    target = source - row + TAPS // 2
                    if 0 <= target < SIDE:
                        term = moved * weights[row]
                        total[target] = term if total[target] is None else total[target] + term
    return sums


def forward_kernel(
    field_hbm, kernel_hbm, gain_hbm, head_gain_hbm, ids_hbm,
    filtered_hbm, mean_ref, inverse_ref, normal_ref, send_ref,
    field_ref, kernel_ref, gain_ref, head_gain_ref, ids_ref, filtered_ref, pooled_ref, total_ref, mixed_ref,
    field_sems, kernel_sems, small_sems, out_sems,
):
    images = field_ref.shape[0] // CELLS
    channels = field_ref.shape[1]
    chunks = channels // LANES
    part = 1.0 / channels
    block = channels // STEPS
    per_block = chunks // STEPS

    def block_at(step):
        return pl.ds(pl.multiple_of(step * block, LANES), block)

    def field_copy(step):
        at = block_at(step)
        return pltpu.make_async_copy(field_hbm.at[:, at], field_ref.at[:, at], field_sems.at[step])

    def kernel_copy(step):
        at = block_at(step)
        return pltpu.make_async_copy(
            kernel_hbm.at[:, :, at], kernel_ref.at[:, :, at], kernel_sems.at[step]
        )

    def filtered_copy(step):
        at = block_at(step)
        return pltpu.make_async_copy(filtered_ref.at[:, at], filtered_hbm.at[:, at], out_sems.at[step])

    small_copies = [
        pltpu.make_async_copy(gain_hbm, gain_ref, small_sems.at[0]),
        pltpu.make_async_copy(head_gain_hbm, head_gain_ref, small_sems.at[1]),
        pltpu.make_async_copy(ids_hbm, ids_ref, small_sems.at[2]),
    ]
    for step in range(STEPS):
        field_copy(step).start()
        kernel_copy(step).start()
    for copy in small_copies:
        copy.start()

    total_ref[...] = jnp.zeros_like(total_ref)

    def filter_chunk(chunk, carry):
        at = pl.ds(pl.multiple_of(chunk * LANES, LANES), LANES)
        for first in range(0, images, 4):
            fields = []
            for image in range(first, first + 4):
                rows = []
                for pair in range(SIDE // 2):
                    both = field_ref[pl.ds(image * CELLS + pair * 2 * SIDE, 2 * SIDE), at]
                    both = both.astype(jnp.float32)
                    rows += [both[:SIDE], both[SIDE:]]
                fields.append(rows)
                level = rows[0]
                for row in rows[1:]:
                    level = level + row
                mixed_ref[pl.ds(image * SIDE, SIDE), at] = level
            sums = [[None] * SIDE for _ in fields]
            filter_rows(fields, sums, kernel_ref, at, False)
            for offset, total in enumerate(sums):
                for row in range(SIDE):
                    cells = pl.ds((first + offset) * CELLS + row * SIDE, SIDE)
                    filtered_ref[cells, at] = total[row]
                    total_ref[cells, :] += total[row]
        return carry

    def filter_block(step, carry):
        field_copy(step).wait()
        kernel_copy(step).wait()
        first = step * per_block
        return lax.fori_loop(
            0, per_block, lambda chunk, held: filter_chunk(first + chunk, held), carry, unroll=2
        )

    lax.fori_loop(0, STEPS, filter_block, 0)
    for step in range(STEPS):
        filtered_copy(step).start()
    for copy in small_copies:
        copy.wait()
    mean_ref[...] = jnp.broadcast_to(
        jnp.sum(total_ref[...], axis=1, keepdims=True) * part, mean_ref.shape
    )

    for image in range(images):
        cells = pl.ds(image * CELLS, CELLS)
        average = mean_ref[cells, :]

        def spread_chunk(chunk, squares):
            at = pl.ds(pl.multiple_of(chunk * LANES, LANES), LANES)
            centred = filtered_ref[cells, at] - average
            return squares + centred * centred

        squares = lax.fori_loop(
            0, chunks, spread_chunk, jnp.zeros((CELLS, LANES), jnp.float32), unroll=8
        )
        spread = jnp.sum(squares, axis=1, keepdims=True) * part
        inverse_ref[cells, :] = jnp.broadcast_to(lax.rsqrt(spread + EPSILON), (CELLS, LANES))

    for image in range(images):
        cells = pl.ds(image * CELLS, CELLS)
        average = mean_ref[cells, :]
        inverse = inverse_ref[cells, :]

        def pool_chunk(chunk, carry):
            at = pl.ds(pl.multiple_of(chunk * LANES, LANES), LANES)
            normal = (filtered_ref[cells, at] - average) * inverse
            level = jnp.sum(normal.reshape(SIDE, SIDE, LANES), axis=0)
            spot = pl.ds(image * SIDE, SIDE)
            mixed_ref[spot, at] = mixed_ref[spot, at] + level * gain_ref[:, at]
            return carry

        lax.fori_loop(0, chunks, pool_chunk, 0, unroll=8)
        pooled_ref[pl.ds(image, 1), :] = jnp.sum(
            mixed_ref[pl.ds(image * SIDE, SIDE), :], axis=0, keepdims=True
        ) * (1.0 / CELLS)

    pooled = pooled_ref[...]
    centred = pooled - jnp.sum(pooled, axis=1, keepdims=True) * part
    spread = jnp.sum(centred * centred, axis=1, keepdims=True) * part
    head_inverse = lax.rsqrt(spread + EPSILON)
    normal = centred * head_inverse
    normal_ref[:, :channels] = normal
    normal_ref[:, channels:] = jnp.broadcast_to(head_inverse, (images, LANES))
    head_input = (normal * head_gain_ref[...]).astype(jnp.bfloat16)
    hot = hot_rows(ids_ref, images)
    group = send_ref.shape[0]
    share = channels // group
    for owner in range(group):
        send_ref[owner, :, :share] = head_input[:, owner * share : (owner + 1) * share]
        send_ref[owner, :, share:] = hot
    for step in range(STEPS):
        filtered_copy(step).wait()


def block_forward(features, kernel, norm_gain, head_gain, img_ids, group):
    images, channels = features.shape[0], features.shape[3]
    cells = images * CELLS
    dma = pltpu.SemaphoreType.DMA
    return call(
        forward_kernel,
        (
            (shape_of((cells, channels), F32), HBM),
            (shape_of((cells, LANES), F32), VMEM),
            (shape_of((cells, LANES), F32), VMEM),
            (shape_of((images, channels + LANES), F32), VMEM),
            (shape_of((group, images, channels // group + IDS), BF16), VMEM),
        ),
        (
            (features.reshape(cells, channels), HBM),
            (kernel, HBM),
            (norm_gain.reshape(1, channels), HBM),
            (head_gain.reshape(1, channels), HBM),
            (img_ids, HBM),
        ),
        "block_forward",
        14,
        scratch=(
            pltpu.VMEM((cells, channels), BF16),
            pltpu.VMEM(kernel.shape, F32),
            pltpu.VMEM((1, channels), F32),
            pltpu.VMEM((1, channels), F32),
            pltpu.SMEM(img_ids.shape, jnp.int32),
            pltpu.VMEM((cells, channels), F32),
            pltpu.VMEM((images, channels), F32),
            pltpu.VMEM((cells, LANES), F32),
            pltpu.VMEM((images * SIDE, channels), F32),
            dma((STEPS,)),
            dma((STEPS,)),
            dma((3,)),
            dma((STEPS,)),
        ),
        grant=BIG,
    )


def backward_kernel(
    s0, s1, s2, s3, normal_hbm, gain_hbm, head_gain_hbm,
    filtered_hbm, mean_hbm, inverse_hbm, kernel_hbm, after_hbm,
    out_hbm,
    blocks_ref, normal_ref, gain_ref, head_gain_ref, filtered_ref, mean_ref, inverse_ref, kernel_ref,
    out_ref, even_ref, lean_ref, pull_ref, tilt_ref,
    block_sems, small_sems, filtered_sems, out_sems,
):
    del after_hbm
    images, channels = even_ref.shape
    blocks = (s0, s1, s2, s3)
    share = channels // len(PEERS)
    wide = channels // STEPS

    def block_at(step):
        return pl.ds(pl.multiple_of(step * wide, LANES), wide)

    def out_copy(step):
        at = block_at(step)
        return pltpu.make_async_copy(out_ref.at[:, at], out_hbm.at[:, at], out_sems.at[step])

    head_copies = [
        pltpu.make_async_copy(block, blocks_ref.at[index], block_sems.at[index])
        for index, block in enumerate(blocks)
    ]
    small_copies = [
        pltpu.make_async_copy(source, target, small_sems.at[index])
        for index, (source, target) in enumerate((
            (head_gain_hbm, head_gain_ref), (gain_hbm, gain_ref), (normal_hbm, normal_ref),
            (mean_hbm, mean_ref), (inverse_hbm, inverse_ref),
        ))
    ]
    filtered_copies = [
        pltpu.make_async_copy(
            filtered_hbm.at[:, block_at(step)], filtered_ref.at[:, block_at(step)],
            filtered_sems.at[step],
        )
        for step in range(STEPS)
    ]
    kernel_copy = pltpu.make_async_copy(kernel_hbm, kernel_ref, small_sems.at[5])
    for copy in (*head_copies, *small_copies, *filtered_copies, kernel_copy):
        copy.start()
    chunks = channels // LANES
    per_block = chunks // STEPS
    part = 1.0 / channels

    for copy in (*head_copies, *small_copies):
        copy.wait()
    x, y_hi = lax.axis_index("x"), lax.axis_index("y_hi")
    for step_x, step_y in PEERS:
        owner = group_peer(x, y_hi, 4 - step_x, step_y)
        at = pl.ds(pl.multiple_of(owner * share, LANES), share)
        tilt_ref[:, at] = blocks_ref[step_x, step_y] * head_gain_ref[:, at]
    cotangent = tilt_ref[...]
    normal = normal_ref[:, :channels]
    level = jnp.sum(cotangent, axis=1, keepdims=True) * part
    lean = jnp.sum(cotangent * normal, axis=1, keepdims=True) * part
    pooled_grad = normal_ref[:, channels : channels + 1] * (cotangent - level - normal * lean)
    even = pooled_grad * (1.0 / CELLS)
    even_ref[...] = even
    pull = even * gain_ref[...]
    pull_ref[...] = pull
    tilt_ref[...] = pull - jnp.sum(pull, axis=1, keepdims=True) * part

    for step in range(STEPS):
        filtered_copies[step].wait()
        for image in range(images):
            spot = pl.ds(image * CELLS, CELLS)
            average = mean_ref[spot, :]

            def lean_chunk(chunk, total, spot=spot, average=average, image=image):
                at = pl.ds(pl.multiple_of(chunk * LANES, LANES), LANES)
                return total + (filtered_ref[spot, at] - average) * pull_ref[pl.ds(image, 1), at]

            total = jnp.zeros((CELLS, LANES), F32) if step == 0 else lean_ref[spot, :]
            lean_ref[spot, :] = lax.fori_loop(
                step * per_block, (step + 1) * per_block, lean_chunk, total, unroll=True
            )
    inverse = inverse_ref[...]
    mean_lean = jnp.sum(lean_ref[...], axis=1, keepdims=True) * part
    lean_ref[...] = inverse * (inverse * (inverse * mean_lean))
    kernel_copy.wait()

    def filter_chunk(chunk, carry):
        at = pl.ds(pl.multiple_of(chunk * LANES, LANES), LANES)
        for first in range(0, images, 2):
            fields = []
            sums = []
            for image in range(first, first + 2):
                tilt = jnp.broadcast_to(tilt_ref[pl.ds(image, 1), at], (SIDE, LANES))
                even = jnp.broadcast_to(even_ref[pl.ds(image, 1), at], (SIDE, LANES))
                rows = []
                for row in range(SIDE):
                    spot = pl.ds(image * CELLS + row * SIDE, SIDE)
                    rows.append(
                        inverse_ref[spot, :] * tilt
                        - lean_ref[spot, :] * (filtered_ref[spot, at] - mean_ref[spot, :])
                    )
                fields.append(rows)
                sums.append([even] * SIDE)
            filter_rows(fields, sums, kernel_ref, at, True)
            for offset, total in enumerate(sums):
                for half in range(SIDE // 2):
                    two = jnp.concatenate(total[2 * half : 2 * half + 2], axis=0)
                    spot = pl.ds((first + offset) * CELLS + half * 2 * SIDE, 2 * SIDE)
                    out_ref[spot, at] = two.astype(jnp.bfloat16)
        return carry

    def filter_block(step, carry):
        first = step * per_block
        lax.fori_loop(
            0, per_block, lambda chunk, held: filter_chunk(first + chunk, held), 0, unroll=2
        )
        out_copy(step).start()
        return carry

    lax.fori_loop(0, STEPS, filter_block, 0)
    for step in range(STEPS):
        out_copy(step).wait()


def block_backward(blocks, normal, norm_gain, head_gain, filtered, mean, inverse, kernel, after):
    cells, channels = filtered.shape
    images = cells // CELLS
    dma = pltpu.SemaphoreType.DMA
    operands = [
        *blocks, normal, norm_gain.reshape(1, channels), head_gain.reshape(1, channels),
        filtered, mean, inverse, kernel, after,
    ]
    return call(
        backward_kernel,
        ((shape_of((cells, channels), BF16), HBM),),
        tuple((array, HBM) for array in operands),
        "block_backward",
        14,
        scratch=(
            pltpu.VMEM((len(blocks),) + blocks[0].shape, F32),
            pltpu.VMEM(normal.shape, F32),
            pltpu.VMEM((1, channels), F32),
            pltpu.VMEM((1, channels), F32),
            pltpu.VMEM((cells, channels), F32),
            pltpu.VMEM((cells, LANES), F32),
            pltpu.VMEM((cells, LANES), F32),
            pltpu.VMEM(kernel.shape, F32),
            pltpu.VMEM((cells, channels), BF16),
            pltpu.VMEM((images, channels), F32),
            pltpu.VMEM((cells, LANES), F32),
            pltpu.VMEM((images, channels), F32),
            pltpu.VMEM((images, channels), F32),
            dma((len(blocks),)),
            dma((6,)),
            dma((STEPS,)),
            dma((STEPS,)),
        ),
        grant=BIG,
    )


def dot(left, right, left_dim, right_dim):
    return lax.dot_general(
        left, right, (((left_dim,), (right_dim,)), ((), ())), preferred_element_type=F32
    )


def inverse_length(values):
    return lax.rsqrt(jnp.sum(values * values, axis=-1, keepdims=True) + EPSILON)


def length_back(unit, inverse, cotangent):
    return inverse * (cotangent - unit * jnp.sum(unit * cotangent, axis=-1, keepdims=True))


def hot_rows(ids_ref, rows):
    row = lax.broadcasted_iota(jnp.int32, (rows, IDS), 0)
    ids = jnp.zeros((rows, IDS), jnp.int32)
    for index in range(rows):
        ids = jnp.where(row == index, ids_ref[index], ids)
    lane = lax.broadcasted_iota(jnp.int32, (rows, IDS), 1)
    return jnp.where(ids == lane, 1.0, 0.0).astype(BF16)


def pack_kernel(text_hbm, ids_hbm, out_ref, text_ref, ids_ref, sems):
    copies = [
        pltpu.make_async_copy(text_hbm, text_ref, sems.at[0]),
        pltpu.make_async_copy(ids_hbm, ids_ref, sems.at[1]),
    ]
    for copy in copies:
        copy.start()
    for copy in copies:
        copy.wait()
    rows, width = text_ref.shape
    text = text_ref[...].astype(F32)
    unit = (text * inverse_length(text)).astype(BF16)
    hot = hot_rows(ids_ref, rows)
    for target in range(out_ref.shape[0]):
        out_ref[target, :, :width] = unit
        out_ref[target, :, width:] = hot


def line_kernel(line_ref, out_ref):
    line, rows, _ = line_ref.shape
    for first in range(0, line, 4):
        four = [line_ref[first + offset].astype(F32) for offset in range(4)]
        at = slice(first * rows, (first + 4) * rows)
        out_ref[at, :] = jnp.concatenate(four, axis=0).astype(BF16)


def join_texts_kernel(own_ref, next_ref, after_ref, out_ref):
    del after_ref
    texts = own_ref.shape[0]
    out_ref[:texts, :] = own_ref[...]
    out_ref[texts:, :] = next_ref[...]


def partial_kernel(received_ref, projection_ref, out_ref, columns_ref, hot_ref):
    group = received_ref.shape[0]
    share = projection_ref.shape[0]
    rows = jnp.concatenate([received_ref[owner].astype(F32) for owner in range(group)], axis=0)
    columns = rows[:, :share].astype(BF16)
    columns_ref[...] = columns
    hot_ref[...] = rows[:, share:].astype(BF16)
    partial = dot(columns, projection_ref[...], 1, 0).astype(BF16)
    for target in range(group):
        out_ref[target] = partial


def pair_kernel(
    partials_ref, hot_ref, projection_ref, t0, t1, t2, t3, t4, t5, t6, t7,
    scale_ref, shift_ref,
    stay_ref, send_ref, factors_ref,
    head_ref,
):
    group, images, width = partials_ref.shape
    blocks = (t0, t1, t2, t3, t4, t5, t6, t7)
    scale, shift = scale_ref[0], shift_ref[0]
    embedded = partials_ref[0].astype(F32)
    for owner in range(1, group):
        embedded += partials_ref[owner].astype(F32)
    inverse = inverse_length(embedded)
    unit = embedded * inverse
    low = unit.astype(BF16)
    factors_ref[:, width : 2 * width] = low
    hot = hot_ref[...]
    weights = []
    for block in blocks:
        logits = scale * dot(low, block[:, :width], 1, 1) + shift
        signs = 2.0 * dot(hot, block[:, width:], 1, 1) - 1.0
        weights.append((-signs * jax.nn.sigmoid(-signs * logits)).astype(BF16))
    image_grad = dot(weights[0], t0[:, :width], 1, 0)
    for weight, block in zip(weights[1:], blocks[1:]):
        image_grad += dot(weight, block[:, :width], 1, 0)
    embed = length_back(unit, inverse, scale * image_grad).astype(BF16)
    factors_ref[:, :width] = embed
    factors_ref[:, 2 * width : 2 * width + LANES] = weights[0]
    factors_ref[:, 2 * width + LANES :] = weights[4]
    head = dot(embed, projection_ref[...], 1, 1)
    rows = images // group
    for owner in range(group):
        head_ref[owner] = head[owner * rows : (owner + 1) * rows]
    x, y_hi = lax.axis_index("x"), lax.axis_index("y_hi")
    for step in range(4):
        stay_ref[step] = head_ref[group_peer(x, y_hi, step, 0)]
        send_ref[step] = head_ref[group_peer(x, y_hi, step, 1)]


def merge_kernel(stay_ref, got_ref, s0, s1, s2, s3):
    for step, out_ref in enumerate((s0, s1, s2, s3)):
        out_ref[0] = stay_ref[step]
        out_ref[1] = got_ref[step]


def strip_make_kernel(mine_ref, theirs_ref, columns_ref, far_columns_ref, out_ref, rows_ref, near_ref, far_ref):
    width = (mine_ref.shape[1] - 2 * LANES) // 2
    line, strip_rows, half = out_ref.shape
    strip = columns_ref.shape[1] // line
    rows = (strip_rows - strip) // 2
    texts = line * rows
    start = pl.multiple_of(lax.axis_index("core") * (width - half), LANES)

    def both(at):
        return jnp.concatenate([mine_ref[:, at], theirs_ref[:, at]], axis=0)

    columns = jnp.concatenate([columns_ref[...], far_columns_ref[...]], axis=0)
    rows_ref[...] = dot(columns, both(pl.ds(start, half)), 0, 0)
    low = both(pl.ds(pl.multiple_of(start + width, LANES), half))
    first = slice(2 * width, 2 * width + texts)
    second = slice(2 * width + LANES, 2 * width + LANES + texts)
    own = jnp.concatenate([mine_ref[:, first], theirs_ref[:, second]], axis=0)
    other = jnp.concatenate([mine_ref[:, second], theirs_ref[:, first]], axis=0)
    near_ref[...] = dot(own, low, 0, 0)
    far_ref[...] = dot(other, low, 0, 0)
    for target in range(line):
        at = slice(target * rows, (target + 1) * rows)
        stacked = jnp.concatenate(
            [rows_ref[target * strip : (target + 1) * strip], near_ref[at], far_ref[at]], axis=0
        )
        out_ref[target] = stacked.astype(BF16)


def strip_kernel(strips_ref, out_ref, mine_ref, theirs_ref):
    line, rows, half = strips_ref.shape
    texts = mine_ref.shape[0]
    strip = rows - 2 * texts
    total = strips_ref[0].astype(F32)
    for source in range(1, line):
        total += strips_ref[source].astype(F32)
    low = total[:strip].astype(BF16)
    for target in range(line):
        out_ref[target] = low
    mine_ref[...] = total[strip : strip + texts]
    theirs_ref[...] = total[strip + texts :]


def text_kernel(text_ref, mine_ref, got_ref, scale_ref, out_ref):
    width = text_ref.shape[1]
    text = text_ref[...].astype(F32)
    inverse = inverse_length(text)
    first = lax.axis_index("core") == 0
    mine, got = mine_ref[...], got_ref[...]
    left = jnp.where(first, mine, got)
    right = jnp.where(first, got, mine)
    grad = jnp.concatenate([left, right[:, 2 * HALF - width :]], axis=1)
    out_ref[...] = length_back(text * inverse, inverse, scale_ref[0] * grad)


def join_kernel(near_ref, far_ref, out_ref):
    core = lax.axis_index("core")
    width = out_ref.shape[1]

    def put(left, right):
        out_ref[:, :HALF] = left[...].astype(F32)
        out_ref[:, HALF:] = right[:, 2 * HALF - width :].astype(F32)

    pl.when(core == 0)(lambda: put(near_ref, far_ref))
    pl.when(core != 0)(lambda: put(far_ref, near_ref))


def exchange(blocks, axes):
    return lax.all_to_all(blocks, axes, 0, 0, tiled=True)


def swap_core(block):
    return lax.ppermute(block, "core", ((0, 1), (1, 0)))


def along_x(block, step):
    return lax.ppermute(block, "x", tuple((i, (i + step) % 4) for i in range(4)))


def local(
    features,
    text_embed,
    img_ids,
    txt_ids,
    kernel,
    norm_gain,
    head_gain,
    projection,
    logit_scale,
    logit_bias,
):
    rows, width = text_embed.shape
    share = projection.shape[0]
    group = lax.axis_size(GROUP)
    line = lax.axis_size(LINE)
    images = group * rows
    texts = line * rows
    strip = share // line
    dma = pltpu.SemaphoreType.DMA

    packed = call(
        pack_kernel,
        ((shape_of((line, rows, width + IDS), BF16), VMEM),),
        ((text_embed, HBM), (txt_ids, HBM)),
        "text_pack", 1,
        scratch=(
            pltpu.VMEM((rows, width), BF16), pltpu.SMEM((rows,), jnp.int32), dma((2,)),
        ),
        grant=BIG,
    )
    gathered = exchange(packed, LINE)
    filtered, mean, inverse, normal, send = block_forward(
        features, kernel, norm_gain, head_gain, img_ids, group
    )
    gathered, send = lax.optimization_barrier((gathered, send))
    received = exchange(send, GROUP)
    partials, columns, hot = call(
        partial_kernel,
        (
            (shape_of((group, images, width), BF16), VMEM),
            (shape_of((images, share), BF16), VMEM),
            (shape_of((images, IDS), BF16), VMEM),
        ),
        ((received, VMEM), (projection, VMEM)),
        "partial_embed", 2,
    )
    own_line = call(
        line_kernel, ((shape_of((texts, width + IDS), BF16), VMEM),), ((gathered, VMEM),),
        "line_rows", 1,
    )
    next_line = lax.ppermute(own_line, "y_hi", ((0, 1), (1, 0)))
    near = [
        call(
            join_texts_kernel,
            ((shape_of((2 * texts, width + IDS), BF16), VMEM),),
            ((own_line, VMEM), (next_line, VMEM), (columns, VMEM)),
            "join_texts", 1,
        )
    ]
    near += [along_x(near[0], step) for step in (1, 3, 2)]
    far = [swap_core(block) for block in near]
    far_columns = swap_core(columns)
    partials = exchange(partials, GROUP)
    stay, away, factors = call(
        pair_kernel,
        (
            (shape_of((4, rows, share), F32), VMEM),
            (shape_of((4, rows, share), F32), VMEM),
            (shape_of((images, 2 * width + 2 * LANES), BF16), VMEM),
        ),
        tuple((array, VMEM) for array in (partials, hot, projection, *near, *far))
        + ((logit_scale, SMEM), (logit_bias, SMEM)),
        "pairs", 4,
        scratch=(pltpu.VMEM((group, rows, share), F32),),
    )
    far_factors = swap_core(factors)
    got = lax.ppermute(away, "y_hi", ((0, 1), (1, 0)))
    strips = call(
        strip_make_kernel,
        ((shape_of((line, strip + 2 * rows, HALF), BF16), VMEM),),
        tuple((array, VMEM) for array in (factors, far_factors, columns, far_columns)),
        "strip_make", 2,
        scratch=(
            pltpu.VMEM((share, HALF), F32),
            pltpu.VMEM((texts, HALF), F32),
            pltpu.VMEM((texts, HALF), F32),
        ),
    )
    strips = exchange(strips, LINE)
    merged = call(
        merge_kernel,
        ((shape_of((2, rows, share), F32), VMEM),) * 4,
        ((stay, VMEM), (got, VMEM)),
        "head_merge", 1,
    )
    blocks = [merged[0]] + [along_x(merged[step], step) for step in (1, 2, 3)]
    shared = (normal, norm_gain, head_gain, filtered, mean, inverse, kernel)
    strips, *blocks = lax.optimization_barrier((strips, *blocks))
    sums, mine, theirs = call(
        strip_kernel,
        (
            (shape_of((line, strip, HALF), BF16), VMEM),
            (shape_of((rows, HALF), F32), VMEM),
            (shape_of((rows, HALF), F32), VMEM),
        ),
        ((strips, VMEM),),
        "strip_sum", 1,
    )
    near_half = exchange(sums, LINE).reshape(share, HALF)
    grad_text = call(
        text_kernel,
        ((shape_of((rows, width), F32), VMEM),),
        ((text_embed, VMEM), (mine, VMEM), (swap_core(theirs), VMEM), (logit_scale, SMEM)),
        "text_grad", 1,
    )
    grad_features = block_backward(blocks, *shared, mine)
    near_half, grad_features, grad_text = lax.optimization_barrier(
        (near_half, grad_features, grad_text)
    )
    grad_proj = call(
        join_kernel,
        ((shape_of((share, width), F32), VMEM),),
        ((near_half, VMEM), (swap_core(near_half), VMEM)),
        "proj_join", 2,
    )
    grad_features = grad_features.reshape(features.shape)
    return (grad_features, grad_text, grad_proj)


def solution(mesh):
    fine = Mesh(mesh.devices.reshape(SIZES), AXES)
    placed = (
        P(ALL, None, None, None),
        P(ALL, None),
        P(ALL),
        P(ALL),
        P(),
        P(),
        P(),
        P(GROUP, None),
        P(),
        P(),
    )
    return jax.shard_map(
        local,
        mesh=fine,
        in_specs=placed,
        out_specs=(P(ALL, None, None, None), P(ALL, None), P(GROUP, None)),
        check_vma=False,
    )
```

```python
import jax
import jax.numpy as jnp
from jax import lax
from jax.experimental import pallas as pl
from jax.experimental.pallas import tpu as pltpu
from jax.sharding import Mesh, PartitionSpec as P

EPSILON = 1e-06
AXES = ("y_lo", "z", "core", "x", "y_hi")
SIZES = (2, 8, 2, 4, 2)
ALL = AXES
GROUP = ("x", "y_hi")
LINE = ("y_lo", "z")
MIB = 1024 * 1024
BIG = 60
IDS = 128
HALF = 640
LANES = 128
SIDE = 8
CELLS = 64
TAPS = 7
VMEM = pl.BlockSpec(memory_space=pltpu.VMEM)
SMEM = pl.BlockSpec(memory_space=pltpu.SMEM)
HBM = pl.BlockSpec(memory_space=pltpu.HBM)
STEPS = 4
PEERS = tuple((step_x, step_y) for step_x in range(4) for step_y in range(2))
BF16 = jnp.bfloat16
F32 = jnp.float32


def shape_of(dims, dtype):
    return jax.ShapeDtypeStruct(dims, dtype)


def call(body, outs, operands, name, micros, scratch=(), grant=40):
    specs = tuple(spec for _, spec in outs)
    shapes = tuple(shape for shape, _ in outs)
    single = len(outs) == 1
    return pl.pallas_call(
        body,
        out_shape=shapes[0] if single else shapes,
        in_specs=[spec for _, spec in operands],
        out_specs=specs[0] if single else specs,
        scratch_shapes=list(scratch),
        compiler_params=pltpu.CompilerParams(vmem_limit_bytes=grant * MIB),
        cost_estimate=pl.CostEstimate(
            flops=0, bytes_accessed=int(micros * 3e6), transcendentals=0
        ),
        name=name,
    )(*[operand for operand, _ in operands])


def group_peer(x, y_hi, step_x, step_y):
    return lax.rem(x + step_x, 4) * 2 + lax.rem(y_hi + step_y, 2)


def tap_weights(kernel_ref, at, column, flip):
    place = lax.broadcasted_iota(jnp.int32, (SIDE, LANES), 0) + (column - TAPS // 2)
    valid = (place >= 0) & (place < SIDE)
    weights = []
    for row in range(TAPS):
        if flip:
            line = kernel_ref[TAPS - 1 - row, pl.ds(TAPS - 1 - column, 1), at]
        else:
            line = kernel_ref[row, pl.ds(column, 1), at]
        weights.append(jnp.where(valid, jnp.broadcast_to(line, (SIDE, LANES)), 0.0))
    return weights


def filter_rows(fields, sums, kernel_ref, at, flip):
    for column in range(TAPS):
        weights = tap_weights(kernel_ref, at, column, flip)
        shift = (TAPS // 2 - column) % SIDE
        for field, total in zip(fields, sums):
            for source in range(SIDE):
                moved = field[source] if shift == 0 else pltpu.roll(field[source], shift, 0)
                for row in range(TAPS):
                    target = source - row + TAPS // 2
                    if 0 <= target < SIDE:
                        term = moved * weights[row]
                        total[target] = term if total[target] is None else total[target] + term
    return sums


def forward_kernel(
    field_hbm, kernel_hbm, gain_hbm, head_gain_hbm, ids_hbm,
    filtered_hbm, mean_ref, inverse_ref, normal_ref, send_ref,
    field_ref, kernel_ref, gain_ref, head_gain_ref, ids_ref, filtered_ref, pooled_ref, total_ref, mixed_ref,
    field_sems, kernel_sems, small_sems, out_sems,
):
    images = field_ref.shape[0] // CELLS
    channels = field_ref.shape[1]
    chunks = channels // LANES
    part = 1.0 / channels
    block = channels // STEPS
    per_block = chunks // STEPS

    def block_at(step):
        return pl.ds(pl.multiple_of(step * block, LANES), block)

    def field_copy(step):
        at = block_at(step)
        return pltpu.make_async_copy(field_hbm.at[:, at], field_ref.at[:, at], field_sems.at[step])

    def kernel_copy(step):
        at = block_at(step)
        return pltpu.make_async_copy(
            kernel_hbm.at[:, :, at], kernel_ref.at[:, :, at], kernel_sems.at[step]
        )

    def filtered_copy(step):
        at = block_at(step)
        return pltpu.make_async_copy(filtered_ref.at[:, at], filtered_hbm.at[:, at], out_sems.at[step])

    small_copies = [
        pltpu.make_async_copy(gain_hbm, gain_ref, small_sems.at[0]),
        pltpu.make_async_copy(head_gain_hbm, head_gain_ref, small_sems.at[1]),
        pltpu.make_async_copy(ids_hbm, ids_ref, small_sems.at[2]),
    ]
    for step in range(STEPS):
        field_copy(step).start()
        kernel_copy(step).start()
    for copy in small_copies:
        copy.start()

    total_ref[...] = jnp.zeros_like(total_ref)

    def filter_chunk(chunk, carry):
        at = pl.ds(pl.multiple_of(chunk * LANES, LANES), LANES)
        for first in range(0, images, 4):
            fields = []
            for image in range(first, first + 4):
                rows = []
                for pair in range(SIDE // 2):
                    both = field_ref[pl.ds(image * CELLS + pair * 2 * SIDE, 2 * SIDE), at]
                    both = both.astype(jnp.float32)
                    rows += [both[:SIDE], both[SIDE:]]
                fields.append(rows)
                level = rows[0]
                for row in rows[1:]:
                    level = level + row
                mixed_ref[pl.ds(image * SIDE, SIDE), at] = level
            sums = [[None] * SIDE for _ in fields]
            filter_rows(fields, sums, kernel_ref, at, False)
            for offset, total in enumerate(sums):
                for row in range(SIDE):
                    cells = pl.ds((first + offset) * CELLS + row * SIDE, SIDE)
                    filtered_ref[cells, at] = total[row]
                    total_ref[cells, :] += total[row]
        return carry

    def filter_block(step, carry):
        field_copy(step).wait()
        kernel_copy(step).wait()
        first = step * per_block
        return lax.fori_loop(
            0, per_block, lambda chunk, held: filter_chunk(first + chunk, held), carry, unroll=3
        )

    lax.fori_loop(0, STEPS, filter_block, 0)
    for step in range(STEPS):
        filtered_copy(step).start()
    for copy in small_copies:
        copy.wait()
    mean_ref[...] = jnp.broadcast_to(
        jnp.sum(total_ref[...], axis=1, keepdims=True) * part, mean_ref.shape
    )

    for image in range(images):
        cells = pl.ds(image * CELLS, CELLS)
        average = mean_ref[cells, :]

        def spread_chunk(chunk, squares):
            at = pl.ds(pl.multiple_of(chunk * LANES, LANES), LANES)
            centred = filtered_ref[cells, at] - average
            return squares + centred * centred

        squares = lax.fori_loop(
            0, chunks, spread_chunk, jnp.zeros((CELLS, LANES), jnp.float32), unroll=8
        )
        spread = jnp.sum(squares, axis=1, keepdims=True) * part
        inverse_ref[cells, :] = jnp.broadcast_to(lax.rsqrt(spread + EPSILON), (CELLS, LANES))

    for image in range(images):
        cells = pl.ds(image * CELLS, CELLS)
        average = mean_ref[cells, :]
        inverse = inverse_ref[cells, :]

        def pool_chunk(chunk, carry):
            at = pl.ds(pl.multiple_of(chunk * LANES, LANES), LANES)
            normal = (filtered_ref[cells, at] - average) * inverse
            level = jnp.sum(normal.reshape(SIDE, SIDE, LANES), axis=0)
            spot = pl.ds(image * SIDE, SIDE)
            mixed_ref[spot, at] = mixed_ref[spot, at] + level * gain_ref[:, at]
            return carry

        lax.fori_loop(0, chunks, pool_chunk, 0, unroll=8)
        pooled_ref[pl.ds(image, 1), :] = jnp.sum(
            mixed_ref[pl.ds(image * SIDE, SIDE), :], axis=0, keepdims=True
        ) * (1.0 / CELLS)

    pooled = pooled_ref[...]
    centred = pooled - jnp.sum(pooled, axis=1, keepdims=True) * part
    spread = jnp.sum(centred * centred, axis=1, keepdims=True) * part
    head_inverse = lax.rsqrt(spread + EPSILON)
    normal = centred * head_inverse
    normal_ref[:, :channels] = normal
    normal_ref[:, channels:] = jnp.broadcast_to(head_inverse, (images, LANES))
    head_input = (normal * head_gain_ref[...]).astype(jnp.bfloat16)
    hot = hot_rows(ids_ref, images)
    group = send_ref.shape[0]
    share = channels // group
    for owner in range(group):
        send_ref[owner, :, :share] = head_input[:, owner * share : (owner + 1) * share]
        send_ref[owner, :, share:] = hot
    for step in range(STEPS):
        filtered_copy(step).wait()


def block_forward(features, kernel, norm_gain, head_gain, img_ids, group):
    images, channels = features.shape[0], features.shape[3]
    cells = images * CELLS
    dma = pltpu.SemaphoreType.DMA
    return call(
        forward_kernel,
        (
            (shape_of((cells, channels), F32), HBM),
            (shape_of((cells, LANES), F32), VMEM),
            (shape_of((cells, LANES), F32), VMEM),
            (shape_of((images, channels + LANES), F32), VMEM),
            (shape_of((group, images, channels // group + IDS), BF16), VMEM),
        ),
        (
            (features.reshape(cells, channels), HBM),
            (kernel, HBM),
            (norm_gain.reshape(1, channels), HBM),
            (head_gain.reshape(1, channels), HBM),
            (img_ids, HBM),
        ),
        "block_forward",
        14,
        scratch=(
            pltpu.VMEM((cells, channels), BF16),
            pltpu.VMEM(kernel.shape, F32),
            pltpu.VMEM((1, channels), F32),
            pltpu.VMEM((1, channels), F32),
            pltpu.SMEM(img_ids.shape, jnp.int32),
            pltpu.VMEM((cells, channels), F32),
            pltpu.VMEM((images, channels), F32),
            pltpu.VMEM((cells, LANES), F32),
            pltpu.VMEM((images * SIDE, channels), F32),
            dma((STEPS,)),
            dma((STEPS,)),
            dma((3,)),
            dma((STEPS,)),
        ),
        grant=BIG,
    )


def backward_kernel(
    s0, s1, s2, s3, normal_hbm, gain_hbm, head_gain_hbm,
    filtered_hbm, mean_hbm, inverse_hbm, kernel_hbm, after_hbm,
    out_hbm,
    blocks_ref, normal_ref, gain_ref, head_gain_ref, filtered_ref, mean_ref, inverse_ref, kernel_ref,
    out_ref, even_ref, lean_ref, pull_ref, tilt_ref,
    block_sems, small_sems, filtered_sems, out_sems,
):
    del after_hbm
    images, channels = even_ref.shape
    blocks = (s0, s1, s2, s3)
    share = channels // len(PEERS)
    wide = channels // STEPS

    def block_at(step):
        return pl.ds(pl.multiple_of(step * wide, LANES), wide)

    def out_copy(step):
        at = block_at(step)
        return pltpu.make_async_copy(out_ref.at[:, at], out_hbm.at[:, at], out_sems.at[step])

    head_copies = [
        pltpu.make_async_copy(block, blocks_ref.at[index], block_sems.at[index])
        for index, block in enumerate(blocks)
    ]
    small_copies = [
        pltpu.make_async_copy(source, target, small_sems.at[index])
        for index, (source, target) in enumerate((
            (head_gain_hbm, head_gain_ref), (gain_hbm, gain_ref), (normal_hbm, normal_ref),
            (mean_hbm, mean_ref), (inverse_hbm, inverse_ref),
        ))
    ]
    filtered_copies = [
        pltpu.make_async_copy(
            filtered_hbm.at[:, block_at(step)], filtered_ref.at[:, block_at(step)],
            filtered_sems.at[step],
        )
        for step in range(STEPS)
    ]
    kernel_copy = pltpu.make_async_copy(kernel_hbm, kernel_ref, small_sems.at[5])
    for copy in (*head_copies, *small_copies, *filtered_copies, kernel_copy):
        copy.start()
    chunks = channels // LANES
    per_block = chunks // STEPS
    part = 1.0 / channels

    for copy in (*head_copies, *small_copies):
        copy.wait()
    x, y_hi = lax.axis_index("x"), lax.axis_index("y_hi")
    for step_x, step_y in PEERS:
        owner = group_peer(x, y_hi, 4 - step_x, step_y)
        at = pl.ds(pl.multiple_of(owner * share, LANES), share)
        tilt_ref[:, at] = blocks_ref[step_x, step_y] * head_gain_ref[:, at]
    cotangent = tilt_ref[...]
    normal = normal_ref[:, :channels]
    level = jnp.sum(cotangent, axis=1, keepdims=True) * part
    lean = jnp.sum(cotangent * normal, axis=1, keepdims=True) * part
    pooled_grad = normal_ref[:, channels : channels + 1] * (cotangent - level - normal * lean)
    even = pooled_grad * (1.0 / CELLS)
    even_ref[...] = even
    pull = even * gain_ref[...]
    pull_ref[...] = pull
    tilt_ref[...] = pull - jnp.sum(pull, axis=1, keepdims=True) * part

    for step in range(STEPS):
        filtered_copies[step].wait()
        for image in range(images):
            spot = pl.ds(image * CELLS, CELLS)
            average = mean_ref[spot, :]

            def lean_chunk(chunk, total, spot=spot, average=average, image=image):
                at = pl.ds(pl.multiple_of(chunk * LANES, LANES), LANES)
                return total + (filtered_ref[spot, at] - average) * pull_ref[pl.ds(image, 1), at]

            total = jnp.zeros((CELLS, LANES), F32) if step == 0 else lean_ref[spot, :]
            lean_ref[spot, :] = lax.fori_loop(
                step * per_block, (step + 1) * per_block, lean_chunk, total, unroll=True
            )
    inverse = inverse_ref[...]
    mean_lean = jnp.sum(lean_ref[...], axis=1, keepdims=True) * part
    lean_ref[...] = inverse * (inverse * (inverse * mean_lean))
    kernel_copy.wait()

    def filter_chunk(chunk, carry):
        at = pl.ds(pl.multiple_of(chunk * LANES, LANES), LANES)
        for first in range(0, images, 2):
            fields = []
            sums = []
            for image in range(first, first + 2):
                tilt = jnp.broadcast_to(tilt_ref[pl.ds(image, 1), at], (SIDE, LANES))
                even = jnp.broadcast_to(even_ref[pl.ds(image, 1), at], (SIDE, LANES))
                rows = []
                for row in range(SIDE):
                    spot = pl.ds(image * CELLS + row * SIDE, SIDE)
                    rows.append(
                        inverse_ref[spot, :] * tilt
                        - lean_ref[spot, :] * (filtered_ref[spot, at] - mean_ref[spot, :])
                    )
                fields.append(rows)
                sums.append([even] * SIDE)
            filter_rows(fields, sums, kernel_ref, at, True)
            for offset, total in enumerate(sums):
                for half in range(SIDE // 2):
                    two = jnp.concatenate(total[2 * half : 2 * half + 2], axis=0)
                    spot = pl.ds((first + offset) * CELLS + half * 2 * SIDE, 2 * SIDE)
                    out_ref[spot, at] = two.astype(jnp.bfloat16)
        return carry

    def filter_block(step, carry):
        first = step * per_block
        lax.fori_loop(
            0, per_block, lambda chunk, held: filter_chunk(first + chunk, held), 0, unroll=2
        )
        out_copy(step).start()
        return carry

    lax.fori_loop(0, STEPS, filter_block, 0)
    for step in range(STEPS):
        out_copy(step).wait()


def block_backward(blocks, normal, norm_gain, head_gain, filtered, mean, inverse, kernel, after):
    cells, channels = filtered.shape
    images = cells // CELLS
    dma = pltpu.SemaphoreType.DMA
    operands = [
        *blocks, normal, norm_gain.reshape(1, channels), head_gain.reshape(1, channels),
        filtered, mean, inverse, kernel, after,
    ]
    return call(
        backward_kernel,
        ((shape_of((cells, channels), BF16), HBM),),
        tuple((array, HBM) for array in operands),
        "block_backward",
        14,
        scratch=(
            pltpu.VMEM((len(blocks),) + blocks[0].shape, F32),
            pltpu.VMEM(normal.shape, F32),
            pltpu.VMEM((1, channels), F32),
            pltpu.VMEM((1, channels), F32),
            pltpu.VMEM((cells, channels), F32),
            pltpu.VMEM((cells, LANES), F32),
            pltpu.VMEM((cells, LANES), F32),
            pltpu.VMEM(kernel.shape, F32),
            pltpu.VMEM((cells, channels), BF16),
            pltpu.VMEM((images, channels), F32),
            pltpu.VMEM((cells, LANES), F32),
            pltpu.VMEM((images, channels), F32),
            pltpu.VMEM((images, channels), F32),
            dma((len(blocks),)),
            dma((6,)),
            dma((STEPS,)),
            dma((STEPS,)),
        ),
        grant=BIG,
    )


def dot(left, right, left_dim, right_dim):
    return lax.dot_general(
        left, right, (((left_dim,), (right_dim,)), ((), ())), preferred_element_type=F32
    )


def inverse_length(values):
    return lax.rsqrt(jnp.sum(values * values, axis=-1, keepdims=True) + EPSILON)


def length_back(unit, inverse, cotangent):
    return inverse * (cotangent - unit * jnp.sum(unit * cotangent, axis=-1, keepdims=True))


def hot_rows(ids_ref, rows):
    row = lax.broadcasted_iota(jnp.int32, (rows, IDS), 0)
    ids = jnp.zeros((rows, IDS), jnp.int32)
    for index in range(rows):
        ids = jnp.where(row == index, ids_ref[index], ids)
    lane = lax.broadcasted_iota(jnp.int32, (rows, IDS), 1)
    return jnp.where(ids == lane, 1.0, 0.0).astype(BF16)


def pack_kernel(text_hbm, ids_hbm, out_ref, text_ref, ids_ref, sems):
    copies = [
        pltpu.make_async_copy(text_hbm, text_ref, sems.at[0]),
        pltpu.make_async_copy(ids_hbm, ids_ref, sems.at[1]),
    ]
    for copy in copies:
        copy.start()
    for copy in copies:
        copy.wait()
    rows, width = text_ref.shape
    text = text_ref[...].astype(F32)
    unit = (text * inverse_length(text)).astype(BF16)
    hot = hot_rows(ids_ref, rows)
    for target in range(out_ref.shape[0]):
        out_ref[target, :, :width] = unit
        out_ref[target, :, width:] = hot


def line_kernel(line_ref, out_ref):
    line, rows, _ = line_ref.shape
    for first in range(0, line, 4):
        four = [line_ref[first + offset].astype(F32) for offset in range(4)]
        at = slice(first * rows, (first + 4) * rows)
        out_ref[at, :] = jnp.concatenate(four, axis=0).astype(BF16)


def join_texts_kernel(own_ref, next_ref, after_ref, out_ref):
    del after_ref
    texts = own_ref.shape[0]
    out_ref[:texts, :] = own_ref[...]
    out_ref[texts:, :] = next_ref[...]


def partial_kernel(received_ref, projection_ref, out_ref, columns_ref, hot_ref):
    group = received_ref.shape[0]
    share = projection_ref.shape[0]
    rows = jnp.concatenate([received_ref[owner].astype(F32) for owner in range(group)], axis=0)
    columns = rows[:, :share].astype(BF16)
    columns_ref[...] = columns
    hot_ref[...] = rows[:, share:].astype(BF16)
    partial = dot(columns, projection_ref[...], 1, 0).astype(BF16)
    for target in range(group):
        out_ref[target] = partial


def pair_kernel(
    partials_ref, hot_ref, projection_ref, t0, t1, t2, t3, t4, t5, t6, t7,
    scale_ref, shift_ref,
    stay_ref, send_ref, factors_ref,
    head_ref,
):
    group, images, width = partials_ref.shape
    blocks = (t0, t1, t2, t3, t4, t5, t6, t7)
    scale, shift = scale_ref[0], shift_ref[0]
    embedded = partials_ref[0].astype(F32)
    for owner in range(1, group):
        embedded += partials_ref[owner].astype(F32)
    inverse = inverse_length(embedded)
    unit = embedded * inverse
    low = unit.astype(BF16)
    factors_ref[:, width : 2 * width] = low
    hot = hot_ref[...]
    weights = []
    for block in blocks:
        logits = scale * dot(low, block[:, :width], 1, 1) + shift
        signs = 2.0 * dot(hot, block[:, width:], 1, 1) - 1.0
        weights.append((-signs * jax.nn.sigmoid(-signs * logits)).astype(BF16))
    image_grad = dot(weights[0], t0[:, :width], 1, 0)
    for weight, block in zip(weights[1:], blocks[1:]):
        image_grad += dot(weight, block[:, :width], 1, 0)
    embed = length_back(unit, inverse, scale * image_grad).astype(BF16)
    factors_ref[:, :width] = embed
    factors_ref[:, 2 * width : 2 * width + LANES] = weights[0]
    factors_ref[:, 2 * width + LANES :] = weights[4]
    head = dot(embed, projection_ref[...], 1, 1)
    rows = images // group
    for owner in range(group):
        head_ref[owner] = head[owner * rows : (owner + 1) * rows]
    x, y_hi = lax.axis_index("x"), lax.axis_index("y_hi")
    for step in range(4):
        stay_ref[step] = head_ref[group_peer(x, y_hi, step, 0)]
        send_ref[step] = head_ref[group_peer(x, y_hi, step, 1)]


def merge_kernel(stay_ref, got_ref, s0, s1, s2, s3):
    for step, out_ref in enumerate((s0, s1, s2, s3)):
        out_ref[0] = stay_ref[step]
        out_ref[1] = got_ref[step]


def strip_make_kernel(mine_ref, theirs_ref, columns_ref, far_columns_ref, out_ref, rows_ref, near_ref, far_ref):
    width = (mine_ref.shape[1] - 2 * LANES) // 2
    line, strip_rows, half = out_ref.shape
    strip = columns_ref.shape[1] // line
    rows = (strip_rows - strip) // 2
    texts = line * rows
    start = pl.multiple_of(lax.axis_index("core") * (width - half), LANES)

    def both(at):
        return jnp.concatenate([mine_ref[:, at], theirs_ref[:, at]], axis=0)

    columns = jnp.concatenate([columns_ref[...], far_columns_ref[...]], axis=0)
    rows_ref[...] = dot(columns, both(pl.ds(start, half)), 0, 0)
    low = both(pl.ds(pl.multiple_of(start + width, LANES), half))
    first = slice(2 * width, 2 * width + texts)
    second = slice(2 * width + LANES, 2 * width + LANES + texts)
    own = jnp.concatenate([mine_ref[:, first], theirs_ref[:, second]], axis=0)
    other = jnp.concatenate([mine_ref[:, second], theirs_ref[:, first]], axis=0)
    near_ref[...] = dot(own, low, 0, 0)
    far_ref[...] = dot(other, low, 0, 0)
    for target in range(line):
        at = slice(target * rows, (target + 1) * rows)
        stacked = jnp.concatenate(
            [rows_ref[target * strip : (target + 1) * strip], near_ref[at], far_ref[at]], axis=0
        )
        out_ref[target] = stacked.astype(BF16)


def strip_kernel(strips_ref, out_ref, mine_ref, theirs_ref):
    line, rows, half = strips_ref.shape
    texts = mine_ref.shape[0]
    strip = rows - 2 * texts
    total = strips_ref[0].astype(F32)
    for source in range(1, line):
        total += strips_ref[source].astype(F32)
    low = total[:strip].astype(BF16)
    for target in range(line):
        out_ref[target] = low
    mine_ref[...] = total[strip : strip + texts]
    theirs_ref[...] = total[strip + texts :]


def text_kernel(text_ref, mine_ref, got_ref, scale_ref, out_ref):
    width = text_ref.shape[1]
    text = text_ref[...].astype(F32)
    inverse = inverse_length(text)
    first = lax.axis_index("core") == 0
    mine, got = mine_ref[...], got_ref[...]
    left = jnp.where(first, mine, got)
    right = jnp.where(first, got, mine)
    grad = jnp.concatenate([left, right[:, 2 * HALF - width :]], axis=1)
    out_ref[...] = length_back(text * inverse, inverse, scale_ref[0] * grad)


def join_kernel(near_ref, far_ref, out_ref):
    core = lax.axis_index("core")
    width = out_ref.shape[1]

    def put(left, right):
        out_ref[:, :HALF] = left[...].astype(F32)
        out_ref[:, HALF:] = right[:, 2 * HALF - width :].astype(F32)

    pl.when(core == 0)(lambda: put(near_ref, far_ref))
    pl.when(core != 0)(lambda: put(far_ref, near_ref))


def exchange(blocks, axes):
    return lax.all_to_all(blocks, axes, 0, 0, tiled=True)


def swap_core(block):
    return lax.ppermute(block, "core", ((0, 1), (1, 0)))


def along_x(block, step):
    return lax.ppermute(block, "x", tuple((i, (i + step) % 4) for i in range(4)))


def local(
    features,
    text_embed,
    img_ids,
    txt_ids,
    kernel,
    norm_gain,
    head_gain,
    projection,
    logit_scale,
    logit_bias,
):
    rows, width = text_embed.shape
    share = projection.shape[0]
    group = lax.axis_size(GROUP)
    line = lax.axis_size(LINE)
    images = group * rows
    texts = line * rows
    strip = share // line
    dma = pltpu.SemaphoreType.DMA

    packed = call(
        pack_kernel,
        ((shape_of((line, rows, width + IDS), BF16), VMEM),),
        ((text_embed, HBM), (txt_ids, HBM)),
        "text_pack", 1,
        scratch=(
            pltpu.VMEM((rows, width), BF16), pltpu.SMEM((rows,), jnp.int32), dma((2,)),
        ),
        grant=BIG,
    )
    gathered = exchange(packed, LINE)
    filtered, mean, inverse, normal, send = block_forward(
        features, kernel, norm_gain, head_gain, img_ids, group
    )
    gathered, send = lax.optimization_barrier((gathered, send))
    received = exchange(send, GROUP)
    partials, columns, hot = call(
        partial_kernel,
        (
            (shape_of((group, images, width), BF16), VMEM),
            (shape_of((images, share), BF16), VMEM),
            (shape_of((images, IDS), BF16), VMEM),
        ),
        ((received, VMEM), (projection, VMEM)),
        "partial_embed", 2,
    )
    own_line = call(
        line_kernel, ((shape_of((texts, width + IDS), BF16), VMEM),), ((gathered, VMEM),),
        "line_rows", 1,
    )
    next_line = lax.ppermute(own_line, "y_hi", ((0, 1), (1, 0)))
    near = [
        call(
            join_texts_kernel,
            ((shape_of((2 * texts, width + IDS), BF16), VMEM),),
            ((own_line, VMEM), (next_line, VMEM), (columns, VMEM)),
            "join_texts", 1,
        )
    ]
    near += [along_x(near[0], step) for step in (1, 3, 2)]
    far = [swap_core(block) for block in near]
    far_columns = swap_core(columns)
    partials = exchange(partials, GROUP)
    stay, away, factors = call(
        pair_kernel,
        (
            (shape_of((4, rows, share), F32), VMEM),
            (shape_of((4, rows, share), F32), VMEM),
            (shape_of((images, 2 * width + 2 * LANES), BF16), VMEM),
        ),
        tuple((array, VMEM) for array in (partials, hot, projection, *near, *far))
        + ((logit_scale, SMEM), (logit_bias, SMEM)),
        "pairs", 4,
        scratch=(pltpu.VMEM((group, rows, share), F32),),
    )
    far_factors = swap_core(factors)
    got = lax.ppermute(away, "y_hi", ((0, 1), (1, 0)))
    strips = call(
        strip_make_kernel,
        ((shape_of((line, strip + 2 * rows, HALF), BF16), VMEM),),
        tuple((array, VMEM) for array in (factors, far_factors, columns, far_columns)),
        "strip_make", 2,
        scratch=(
            pltpu.VMEM((share, HALF), F32),
            pltpu.VMEM((texts, HALF), F32),
            pltpu.VMEM((texts, HALF), F32),
        ),
    )
    strips = exchange(strips, LINE)
    merged = call(
        merge_kernel,
        ((shape_of((2, rows, share), F32), VMEM),) * 4,
        ((stay, VMEM), (got, VMEM)),
        "head_merge", 1,
    )
    blocks = [merged[0]] + [along_x(merged[step], step) for step in (1, 2, 3)]
    shared = (normal, norm_gain, head_gain, filtered, mean, inverse, kernel)
    strips, *blocks = lax.optimization_barrier((strips, *blocks))
    sums, mine, theirs = call(
        strip_kernel,
        (
            (shape_of((line, strip, HALF), BF16), VMEM),
            (shape_of((rows, HALF), F32), VMEM),
            (shape_of((rows, HALF), F32), VMEM),
        ),
        ((strips, VMEM),),
        "strip_sum", 1,
    )
    near_half = exchange(sums, LINE).reshape(share, HALF)
    grad_text = call(
        text_kernel,
        ((shape_of((rows, width), F32), VMEM),),
        ((text_embed, VMEM), (mine, VMEM), (swap_core(theirs), VMEM), (logit_scale, SMEM)),
        "text_grad", 1,
    )
    grad_features = block_backward(blocks, *shared, mine)
    near_half, grad_features, grad_text = lax.optimization_barrier(
        (near_half, grad_features, grad_text)
    )
    grad_proj = call(
        join_kernel,
        ((shape_of((share, width), F32), VMEM),),
        ((near_half, VMEM), (swap_core(near_half), VMEM)),
        "proj_join", 2,
    )
    grad_features = grad_features.reshape(features.shape)
    return (grad_features, grad_text, grad_proj)


def solution(mesh):
    fine = Mesh(mesh.devices.reshape(SIZES), AXES)
    placed = (
        P(ALL, None, None, None),
        P(ALL, None),
        P(ALL),
        P(ALL),
        P(),
        P(),
        P(),
        P(GROUP, None),
        P(),
        P(),
    )
    return jax.shard_map(
        local,
        mesh=fine,
        in_specs=placed,
        out_specs=(P(ALL, None, None, None), P(ALL, None), P(GROUP, None)),
        check_vma=False,
    )
```

```python
import jax
import jax.numpy as jnp
from jax import lax
from jax.experimental import pallas as pl
from jax.experimental.pallas import tpu as pltpu
from jax.sharding import Mesh, PartitionSpec as P

EPSILON = 1e-06
AXES = ("y_lo", "z", "core", "x", "y_hi")
SIZES = (2, 8, 2, 4, 2)
ALL = AXES
GROUP = ("x", "y_hi")
LINE = ("y_lo", "z")
MIB = 1024 * 1024
BIG = 60
IDS = 128
HALF = 640
LANES = 128
SIDE = 8
CELLS = 64
TAPS = 7
VMEM = pl.BlockSpec(memory_space=pltpu.VMEM)
SMEM = pl.BlockSpec(memory_space=pltpu.SMEM)
HBM = pl.BlockSpec(memory_space=pltpu.HBM)
STEPS = 4
PEERS = tuple((step_x, step_y) for step_x in range(4) for step_y in range(2))
BF16 = jnp.bfloat16
F32 = jnp.float32


def shape_of(dims, dtype):
    return jax.ShapeDtypeStruct(dims, dtype)


def call(body, outs, operands, name, micros, scratch=(), grant=40):
    specs = tuple(spec for _, spec in outs)
    shapes = tuple(shape for shape, _ in outs)
    single = len(outs) == 1
    return pl.pallas_call(
        body,
        out_shape=shapes[0] if single else shapes,
        in_specs=[spec for _, spec in operands],
        out_specs=specs[0] if single else specs,
        scratch_shapes=list(scratch),
        compiler_params=pltpu.CompilerParams(vmem_limit_bytes=grant * MIB),
        cost_estimate=pl.CostEstimate(
            flops=0, bytes_accessed=int(micros * 3e6), transcendentals=0
        ),
        name=name,
    )(*[operand for operand, _ in operands])


def group_peer(x, y_hi, step_x, step_y):
    return lax.rem(x + step_x, 4) * 2 + lax.rem(y_hi + step_y, 2)


def tap_weights(kernel_ref, at, column, flip):
    place = lax.broadcasted_iota(jnp.int32, (SIDE, LANES), 0) + (column - TAPS // 2)
    valid = (place >= 0) & (place < SIDE)
    weights = []
    for row in range(TAPS):
        if flip:
            line = kernel_ref[TAPS - 1 - row, pl.ds(TAPS - 1 - column, 1), at]
        else:
            line = kernel_ref[row, pl.ds(column, 1), at]
        weights.append(jnp.where(valid, jnp.broadcast_to(line, (SIDE, LANES)), 0.0))
    return weights


def filter_rows(fields, sums, kernel_ref, at, flip):
    for column in range(TAPS):
        weights = tap_weights(kernel_ref, at, column, flip)
        shift = (TAPS // 2 - column) % SIDE
        for field, total in zip(fields, sums):
            for source in range(SIDE):
                moved = field[source] if shift == 0 else pltpu.roll(field[source], shift, 0)
                for row in range(TAPS):
                    target = source - row + TAPS // 2
                    if 0 <= target < SIDE:
                        term = moved * weights[row]
                        total[target] = term if total[target] is None else total[target] + term
    return sums


def forward_kernel(
    field_hbm, kernel_hbm, gain_hbm, head_gain_hbm, ids_hbm,
    filtered_hbm, mean_ref, inverse_ref, normal_ref, send_ref,
    field_ref, kernel_ref, gain_ref, head_gain_ref, ids_ref, filtered_ref, pooled_ref, total_ref, mixed_ref,
    field_sems, kernel_sems, small_sems, out_sems,
):
    images = field_ref.shape[0] // CELLS
    channels = field_ref.shape[1]
    chunks = channels // LANES
    part = 1.0 / channels
    block = channels // STEPS
    per_block = chunks // STEPS

    def block_at(step):
        return pl.ds(pl.multiple_of(step * block, LANES), block)

    def field_copy(step):
        at = block_at(step)
        return pltpu.make_async_copy(field_hbm.at[:, at], field_ref.at[:, at], field_sems.at[step])

    def kernel_copy(step):
        at = block_at(step)
        return pltpu.make_async_copy(
            kernel_hbm.at[:, :, at], kernel_ref.at[:, :, at], kernel_sems.at[step]
        )

    def filtered_copy(step):
        at = block_at(step)
        return pltpu.make_async_copy(filtered_ref.at[:, at], filtered_hbm.at[:, at], out_sems.at[step])

    small_copies = [
        pltpu.make_async_copy(gain_hbm, gain_ref, small_sems.at[0]),
        pltpu.make_async_copy(head_gain_hbm, head_gain_ref, small_sems.at[1]),
        pltpu.make_async_copy(ids_hbm, ids_ref, small_sems.at[2]),
    ]
    for step in range(STEPS):
        field_copy(step).start()
        kernel_copy(step).start()
    for copy in small_copies:
        copy.start()

    total_ref[...] = jnp.zeros_like(total_ref)

    def filter_chunk(chunk, carry):
        at = pl.ds(pl.multiple_of(chunk * LANES, LANES), LANES)
        for first in range(0, images, 4):
            fields = []
            for image in range(first, first + 4):
                rows = []
                for pair in range(SIDE // 2):
                    both = field_ref[pl.ds(image * CELLS + pair * 2 * SIDE, 2 * SIDE), at]
                    both = both.astype(jnp.float32)
                    rows += [both[:SIDE], both[SIDE:]]
                fields.append(rows)
                level = rows[0]
                for row in rows[1:]:
                    level = level + row
                mixed_ref[pl.ds(image * SIDE, SIDE), at] = level
            sums = [[None] * SIDE for _ in fields]
            filter_rows(fields, sums, kernel_ref, at, False)
            for offset, total in enumerate(sums):
                for row in range(SIDE):
                    cells = pl.ds((first + offset) * CELLS + row * SIDE, SIDE)
                    filtered_ref[cells, at] = total[row]
                    total_ref[cells, :] += total[row]
        return carry

    def filter_block(step, carry):
        field_copy(step).wait()
        kernel_copy(step).wait()
        first = step * per_block
        return lax.fori_loop(
            0, per_block, lambda chunk, held: filter_chunk(first + chunk, held), carry, unroll=3
        )

    lax.fori_loop(0, STEPS, filter_block, 0)
    for step in range(STEPS):
        filtered_copy(step).start()
    for copy in small_copies:
        copy.wait()
    mean_ref[...] = jnp.broadcast_to(
        jnp.sum(total_ref[...], axis=1, keepdims=True) * part, mean_ref.shape
    )

    for image in range(images):
        cells = pl.ds(image * CELLS, CELLS)
        average = mean_ref[cells, :]

        def spread_chunk(chunk, squares):
            at = pl.ds(pl.multiple_of(chunk * LANES, LANES), LANES)
            centred = filtered_ref[cells, at] - average
            return squares + centred * centred

        squares = lax.fori_loop(
            0, chunks, spread_chunk, jnp.zeros((CELLS, LANES), jnp.float32), unroll=8
        )
        spread = jnp.sum(squares, axis=1, keepdims=True) * part
        inverse_ref[cells, :] = jnp.broadcast_to(lax.rsqrt(spread + EPSILON), (CELLS, LANES))

    for image in range(images):
        cells = pl.ds(image * CELLS, CELLS)
        average = mean_ref[cells, :]
        inverse = inverse_ref[cells, :]

        def pool_chunk(chunk, carry):
            at = pl.ds(pl.multiple_of(chunk * LANES, LANES), LANES)
            normal = (filtered_ref[cells, at] - average) * inverse
            level = jnp.sum(normal.reshape(SIDE, SIDE, LANES), axis=0)
            spot = pl.ds(image * SIDE, SIDE)
            mixed_ref[spot, at] = mixed_ref[spot, at] + level * gain_ref[:, at]
            return carry

        lax.fori_loop(0, chunks, pool_chunk, 0, unroll=8)
        pooled_ref[pl.ds(image, 1), :] = jnp.sum(
            mixed_ref[pl.ds(image * SIDE, SIDE), :], axis=0, keepdims=True
        ) * (1.0 / CELLS)

    pooled = pooled_ref[...]
    centred = pooled - jnp.sum(pooled, axis=1, keepdims=True) * part
    spread = jnp.sum(centred * centred, axis=1, keepdims=True) * part
    head_inverse = lax.rsqrt(spread + EPSILON)
    normal = centred * head_inverse
    normal_ref[:, :channels] = normal
    normal_ref[:, channels:] = jnp.broadcast_to(head_inverse, (images, LANES))
    head_input = (normal * head_gain_ref[...]).astype(jnp.bfloat16)
    hot = hot_rows(ids_ref, images)
    group = send_ref.shape[0]
    share = channels // group
    for owner in range(group):
        send_ref[owner, :, :share] = head_input[:, owner * share : (owner + 1) * share]
        send_ref[owner, :, share:] = hot
    for step in range(STEPS):
        filtered_copy(step).wait()


def block_forward(features, kernel, norm_gain, head_gain, img_ids, group):
    images, channels = features.shape[0], features.shape[3]
    cells = images * CELLS
    dma = pltpu.SemaphoreType.DMA
    return call(
        forward_kernel,
        (
            (shape_of((cells, channels), F32), HBM),
            (shape_of((cells, LANES), F32), VMEM),
            (shape_of((cells, LANES), F32), VMEM),
            (shape_of((images, channels + LANES), F32), VMEM),
            (shape_of((group, images, channels // group + IDS), BF16), VMEM),
        ),
        (
            (features.reshape(cells, channels), HBM),
            (kernel, HBM),
            (norm_gain.reshape(1, channels), HBM),
            (head_gain.reshape(1, channels), HBM),
            (img_ids, HBM),
        ),
        "block_forward",
        14,
        scratch=(
            pltpu.VMEM((cells, channels), BF16),
            pltpu.VMEM(kernel.shape, F32),
            pltpu.VMEM((1, channels), F32),
            pltpu.VMEM((1, channels), F32),
            pltpu.SMEM(img_ids.shape, jnp.int32),
            pltpu.VMEM((cells, channels), F32),
            pltpu.VMEM((images, channels), F32),
            pltpu.VMEM((cells, LANES), F32),
            pltpu.VMEM((images * SIDE, channels), F32),
            dma((STEPS,)),
            dma((STEPS,)),
            dma((3,)),
            dma((STEPS,)),
        ),
        grant=BIG,
    )


def backward_kernel(
    s0, s1, s2, s3, normal_hbm, gain_hbm, head_gain_hbm,
    filtered_hbm, mean_hbm, inverse_hbm, kernel_hbm, after_hbm,
    out_hbm,
    blocks_ref, normal_ref, gain_ref, head_gain_ref, filtered_ref, mean_ref, inverse_ref, kernel_ref,
    out_ref, even_ref, lean_ref, pull_ref, tilt_ref,
    block_sems, small_sems, filtered_sems, out_sems,
):
    del after_hbm
    images, channels = even_ref.shape
    blocks = (s0, s1, s2, s3)
    share = channels // len(PEERS)
    wide = channels // STEPS

    def block_at(step):
        return pl.ds(pl.multiple_of(step * wide, LANES), wide)

    def out_copy(step):
        at = block_at(step)
        return pltpu.make_async_copy(out_ref.at[:, at], out_hbm.at[:, at], out_sems.at[step])

    head_copies = [
        pltpu.make_async_copy(block, blocks_ref.at[index], block_sems.at[index])
        for index, block in enumerate(blocks)
    ]
    small_copies = [
        pltpu.make_async_copy(source, target, small_sems.at[index])
        for index, (source, target) in enumerate((
            (head_gain_hbm, head_gain_ref), (gain_hbm, gain_ref), (normal_hbm, normal_ref),
            (mean_hbm, mean_ref), (inverse_hbm, inverse_ref),
        ))
    ]
    filtered_copies = [
        pltpu.make_async_copy(
            filtered_hbm.at[:, block_at(step)], filtered_ref.at[:, block_at(step)],
            filtered_sems.at[step],
        )
        for step in range(STEPS)
    ]
    kernel_copy = pltpu.make_async_copy(kernel_hbm, kernel_ref, small_sems.at[5])
    for copy in (*head_copies, *small_copies, *filtered_copies, kernel_copy):
        copy.start()
    chunks = channels // LANES
    per_block = chunks // STEPS
    part = 1.0 / channels

    for copy in (*head_copies, *small_copies):
        copy.wait()
    x, y_hi = lax.axis_index("x"), lax.axis_index("y_hi")
    for step_x, step_y in PEERS:
        owner = group_peer(x, y_hi, 4 - step_x, step_y)
        at = pl.ds(pl.multiple_of(owner * share, LANES), share)
        tilt_ref[:, at] = blocks_ref[step_x, step_y] * head_gain_ref[:, at]
    cotangent = tilt_ref[...]
    normal = normal_ref[:, :channels]
    level = jnp.sum(cotangent, axis=1, keepdims=True) * part
    lean = jnp.sum(cotangent * normal, axis=1, keepdims=True) * part
    pooled_grad = normal_ref[:, channels : channels + 1] * (cotangent - level - normal * lean)
    even = pooled_grad * (1.0 / CELLS)
    even_ref[...] = even
    pull = even * gain_ref[...]
    pull_ref[...] = pull
    tilt_ref[...] = pull - jnp.sum(pull, axis=1, keepdims=True) * part

    for step in range(STEPS):
        filtered_copies[step].wait()
        for image in range(images):
            spot = pl.ds(image * CELLS, CELLS)
            average = mean_ref[spot, :]

            def lean_chunk(chunk, total, spot=spot, average=average, image=image):
                at = pl.ds(pl.multiple_of(chunk * LANES, LANES), LANES)
                return total + (filtered_ref[spot, at] - average) * pull_ref[pl.ds(image, 1), at]

            total = jnp.zeros((CELLS, LANES), F32) if step == 0 else lean_ref[spot, :]
            lean_ref[spot, :] = lax.fori_loop(
                step * per_block, (step + 1) * per_block, lean_chunk, total, unroll=True
            )
    inverse = inverse_ref[...]
    mean_lean = jnp.sum(lean_ref[...], axis=1, keepdims=True) * part
    lean_ref[...] = inverse * (inverse * (inverse * mean_lean))
    kernel_copy.wait()

    def filter_chunk(chunk, carry):
        at = pl.ds(pl.multiple_of(chunk * LANES, LANES), LANES)
        for first in range(0, images, 2):
            fields = []
            sums = []
            for image in range(first, first + 2):
                tilt = jnp.broadcast_to(tilt_ref[pl.ds(image, 1), at], (SIDE, LANES))
                even = jnp.broadcast_to(even_ref[pl.ds(image, 1), at], (SIDE, LANES))
                rows = []
                for row in range(SIDE):
                    spot = pl.ds(image * CELLS + row * SIDE, SIDE)
                    rows.append(
                        inverse_ref[spot, :] * tilt
                        - lean_ref[spot, :] * (filtered_ref[spot, at] - mean_ref[spot, :])
                    )
                fields.append(rows)
                sums.append([even] * SIDE)
            filter_rows(fields, sums, kernel_ref, at, True)
            for offset, total in enumerate(sums):
                for half in range(SIDE // 2):
                    two = jnp.concatenate(total[2 * half : 2 * half + 2], axis=0)
                    spot = pl.ds((first + offset) * CELLS + half * 2 * SIDE, 2 * SIDE)
                    out_ref[spot, at] = two.astype(jnp.bfloat16)
        return carry

    def filter_block(step, carry):
        first = step * per_block
        lax.fori_loop(
            0, per_block, lambda chunk, held: filter_chunk(first + chunk, held), 0, unroll=2
        )
        out_copy(step).start()
        return carry

    lax.fori_loop(0, STEPS, filter_block, 0)
    for step in range(STEPS):
        out_copy(step).wait()


def block_backward(blocks, normal, norm_gain, head_gain, filtered, mean, inverse, kernel, after):
    cells, channels = filtered.shape
    images = cells // CELLS
    dma = pltpu.SemaphoreType.DMA
    operands = [
        *blocks, normal, norm_gain.reshape(1, channels), head_gain.reshape(1, channels),
        filtered, mean, inverse, kernel, after,
    ]
    return call(
        backward_kernel,
        ((shape_of((cells, channels), BF16), HBM),),
        tuple((array, HBM) for array in operands),
        "block_backward",
        14,
        scratch=(
            pltpu.VMEM((len(blocks),) + blocks[0].shape, F32),
            pltpu.VMEM(normal.shape, F32),
            pltpu.VMEM((1, channels), F32),
            pltpu.VMEM((1, channels), F32),
            pltpu.VMEM((cells, channels), F32),
            pltpu.VMEM((cells, LANES), F32),
            pltpu.VMEM((cells, LANES), F32),
            pltpu.VMEM(kernel.shape, F32),
            pltpu.VMEM((cells, channels), BF16),
            pltpu.VMEM((images, channels), F32),
            pltpu.VMEM((cells, LANES), F32),
            pltpu.VMEM((images, channels), F32),
            pltpu.VMEM((images, channels), F32),
            dma((len(blocks),)),
            dma((6,)),
            dma((STEPS,)),
            dma((STEPS,)),
        ),
        grant=BIG,
    )


def dot(left, right, left_dim, right_dim):
    return lax.dot_general(
        left, right, (((left_dim,), (right_dim,)), ((), ())), preferred_element_type=F32
    )


def inverse_length(values):
    return lax.rsqrt(jnp.sum(values * values, axis=-1, keepdims=True) + EPSILON)


def length_back(unit, inverse, cotangent):
    return inverse * (cotangent - unit * jnp.sum(unit * cotangent, axis=-1, keepdims=True))


def hot_rows(ids_ref, rows):
    row = lax.broadcasted_iota(jnp.int32, (rows, IDS), 0)
    ids = jnp.zeros((rows, IDS), jnp.int32)
    for index in range(rows):
        ids = jnp.where(row == index, ids_ref[index], ids)
    lane = lax.broadcasted_iota(jnp.int32, (rows, IDS), 1)
    return jnp.where(ids == lane, 1.0, 0.0).astype(BF16)


def pack_kernel(text_hbm, ids_hbm, out_ref, text_ref, ids_ref, sems):
    copies = [
        pltpu.make_async_copy(text_hbm, text_ref, sems.at[0]),
        pltpu.make_async_copy(ids_hbm, ids_ref, sems.at[1]),
    ]
    for copy in copies:
        copy.start()
    for copy in copies:
        copy.wait()
    rows, width = text_ref.shape
    text = text_ref[...].astype(F32)
    unit = (text * inverse_length(text)).astype(BF16)
    hot = hot_rows(ids_ref, rows)
    for target in range(out_ref.shape[0]):
        out_ref[target, :, :width] = unit
        out_ref[target, :, width:] = hot


def line_kernel(line_ref, out_ref):
    line, rows, _ = line_ref.shape
    for first in range(0, line, 4):
        four = [line_ref[first + offset].astype(F32) for offset in range(4)]
        at = slice(first * rows, (first + 4) * rows)
        out_ref[at, :] = jnp.concatenate(four, axis=0).astype(BF16)


def join_texts_kernel(own_ref, next_ref, after_ref, out_ref):
    del after_ref
    texts = own_ref.shape[0]
    out_ref[:texts, :] = own_ref[...]
    out_ref[texts:, :] = next_ref[...]


def partial_kernel(received_ref, projection_ref, out_ref, columns_ref, hot_ref):
    group = received_ref.shape[0]
    share = projection_ref.shape[0]
    rows = jnp.concatenate([received_ref[owner].astype(F32) for owner in range(group)], axis=0)
    columns = rows[:, :share].astype(BF16)
    columns_ref[...] = columns
    hot_ref[...] = rows[:, share:].astype(BF16)
    partial = dot(columns, projection_ref[...], 1, 0).astype(BF16)
    for target in range(group):
        out_ref[target] = partial


def pair_kernel(
    partials_ref, hot_ref, projection_ref, t0, t1, t2, t3, t4, t5, t6, t7,
    scale_ref, shift_ref,
    stay_ref, send_ref, factors_ref,
    head_ref,
):
    group, images, width = partials_ref.shape
    blocks = (t0, t1, t2, t3, t4, t5, t6, t7)
    scale, shift = scale_ref[0], shift_ref[0]
    embedded = partials_ref[0].astype(F32)
    for owner in range(1, group):
        embedded += partials_ref[owner].astype(F32)
    inverse = inverse_length(embedded)
    unit = embedded * inverse
    low = unit.astype(BF16)
    factors_ref[:, width : 2 * width] = low
    hot = hot_ref[...]
    weights = []
    for block in blocks:
        logits = scale * dot(low, block[:, :width], 1, 1) + shift
        signs = 2.0 * dot(hot, block[:, width:], 1, 1) - 1.0
        weights.append((-signs * jax.nn.sigmoid(-signs * logits)).astype(BF16))
    image_grad = dot(weights[0], t0[:, :width], 1, 0)
    for weight, block in zip(weights[1:], blocks[1:]):
        image_grad += dot(weight, block[:, :width], 1, 0)
    embed = length_back(unit, inverse, scale * image_grad).astype(BF16)
    factors_ref[:, :width] = embed
    factors_ref[:, 2 * width : 2 * width + LANES] = weights[0]
    factors_ref[:, 2 * width + LANES :] = weights[4]
    head = dot(embed, projection_ref[...], 1, 1)
    rows = images // group
    for owner in range(group):
        head_ref[owner] = head[owner * rows : (owner + 1) * rows]
    x, y_hi = lax.axis_index("x"), lax.axis_index("y_hi")
    for step in range(4):
        stay_ref[step] = head_ref[group_peer(x, y_hi, step, 0)]
        send_ref[step] = head_ref[group_peer(x, y_hi, step, 1)]


def merge_kernel(stay_ref, got_ref, s0, s1, s2, s3):
    for step, out_ref in enumerate((s0, s1, s2, s3)):
        out_ref[0] = stay_ref[step]
        out_ref[1] = got_ref[step]


def strip_make_kernel(mine_ref, theirs_ref, columns_ref, far_columns_ref, out_ref, rows_ref, near_ref, far_ref):
    width = (mine_ref.shape[1] - 2 * LANES) // 2
    line, strip_rows, half = out_ref.shape
    strip = columns_ref.shape[1] // line
    rows = (strip_rows - strip) // 2
    texts = line * rows
    start = pl.multiple_of(lax.axis_index("core") * (width - half), LANES)

    def both(at):
        return jnp.concatenate([mine_ref[:, at], theirs_ref[:, at]], axis=0)

    columns = jnp.concatenate([columns_ref[...], far_columns_ref[...]], axis=0)
    rows_ref[...] = dot(columns, both(pl.ds(start, half)), 0, 0)
    low = both(pl.ds(pl.multiple_of(start + width, LANES), half))
    first = slice(2 * width, 2 * width + texts)
    second = slice(2 * width + LANES, 2 * width + LANES + texts)
    own = jnp.concatenate([mine_ref[:, first], theirs_ref[:, second]], axis=0)
    other = jnp.concatenate([mine_ref[:, second], theirs_ref[:, first]], axis=0)
    near_ref[...] = dot(own, low, 0, 0)
    far_ref[...] = dot(other, low, 0, 0)
    for target in range(line):
        at = slice(target * rows, (target + 1) * rows)
        stacked = jnp.concatenate(
            [rows_ref[target * strip : (target + 1) * strip], near_ref[at], far_ref[at]], axis=0
        )
        out_ref[target] = stacked.astype(BF16)


def strip_kernel(strips_ref, out_ref, mine_ref, theirs_ref):
    line, rows, half = strips_ref.shape
    texts = mine_ref.shape[0]
    strip = rows - 2 * texts
    total = strips_ref[0].astype(F32)
    for source in range(1, line):
        total += strips_ref[source].astype(F32)
    low = total[:strip].astype(BF16)
    for target in range(line):
        out_ref[target] = low
    mine_ref[...] = total[strip : strip + texts]
    theirs_ref[...] = total[strip + texts :]


def text_kernel(text_ref, mine_ref, got_ref, scale_ref, out_ref):
    width = text_ref.shape[1]
    text = text_ref[...].astype(F32)
    inverse = inverse_length(text)
    first = lax.axis_index("core") == 0
    mine, got = mine_ref[...], got_ref[...]
    left = jnp.where(first, mine, got)
    right = jnp.where(first, got, mine)
    grad = jnp.concatenate([left, right[:, 2 * HALF - width :]], axis=1)
    out_ref[...] = length_back(text * inverse, inverse, scale_ref[0] * grad)


def join_kernel(near_ref, far_ref, out_ref):
    core = lax.axis_index("core")
    width = out_ref.shape[1]

    def put(left, right):
        out_ref[:, :HALF] = left[...].astype(F32)
        out_ref[:, HALF:] = right[:, 2 * HALF - width :].astype(F32)

    pl.when(core == 0)(lambda: put(near_ref, far_ref))
    pl.when(core != 0)(lambda: put(far_ref, near_ref))


def exchange(blocks, axes):
    return lax.all_to_all(blocks, axes, 0, 0, tiled=True)


def swap_core(block):
    return lax.ppermute(block, "core", ((0, 1), (1, 0)))


def along_x(block, step):
    return lax.ppermute(block, "x", tuple((i, (i + step) % 4) for i in range(4)))


def local(
    features,
    text_embed,
    img_ids,
    txt_ids,
    kernel,
    norm_gain,
    head_gain,
    projection,
    logit_scale,
    logit_bias,
):
    rows, width = text_embed.shape
    share = projection.shape[0]
    group = lax.axis_size(GROUP)
    line = lax.axis_size(LINE)
    images = group * rows
    texts = line * rows
    strip = share // line
    dma = pltpu.SemaphoreType.DMA

    packed = call(
        pack_kernel,
        ((shape_of((line, rows, width + IDS), BF16), VMEM),),
        ((text_embed, HBM), (txt_ids, HBM)),
        "text_pack", 1,
        scratch=(
            pltpu.VMEM((rows, width), BF16), pltpu.SMEM((rows,), jnp.int32), dma((2,)),
        ),
        grant=BIG,
    )
    gathered = exchange(packed, LINE)
    filtered, mean, inverse, normal, send = block_forward(
        features, kernel, norm_gain, head_gain, img_ids, group
    )
    gathered, send = lax.optimization_barrier((gathered, send))
    received = exchange(send, GROUP)
    partials, columns, hot = call(
        partial_kernel,
        (
            (shape_of((group, images, width), BF16), VMEM),
            (shape_of((images, share), BF16), VMEM),
            (shape_of((images, IDS), BF16), VMEM),
        ),
        ((received, VMEM), (projection, VMEM)),
        "partial_embed", 2,
    )
    own_line = call(
        line_kernel, ((shape_of((texts, width + IDS), BF16), VMEM),), ((gathered, VMEM),),
        "line_rows", 1,
    )
    next_line = lax.ppermute(own_line, "y_hi", ((0, 1), (1, 0)))
    near = [
        call(
            join_texts_kernel,
            ((shape_of((2 * texts, width + IDS), BF16), VMEM),),
            ((own_line, VMEM), (next_line, VMEM), (columns, VMEM)),
            "join_texts", 1,
        )
    ]
    near += [along_x(near[0], step) for step in (2, 1, 3)]
    far = [swap_core(block) for block in near]
    far_columns = swap_core(columns)
    partials = exchange(partials, GROUP)
    stay, away, factors = call(
        pair_kernel,
        (
            (shape_of((4, rows, share), F32), VMEM),
            (shape_of((4, rows, share), F32), VMEM),
            (shape_of((images, 2 * width + 2 * LANES), BF16), VMEM),
        ),
        tuple((array, VMEM) for array in (partials, hot, projection, *near, *far))
        + ((logit_scale, SMEM), (logit_bias, SMEM)),
        "pairs", 4,
        scratch=(pltpu.VMEM((group, rows, share), F32),),
    )
    far_factors = swap_core(factors)
    got = lax.ppermute(away, "y_hi", ((0, 1), (1, 0)))
    strips = call(
        strip_make_kernel,
        ((shape_of((line, strip + 2 * rows, HALF), BF16), VMEM),),
        tuple((array, VMEM) for array in (factors, far_factors, columns, far_columns)),
        "strip_make", 2,
        scratch=(
            pltpu.VMEM((share, HALF), F32),
            pltpu.VMEM((texts, HALF), F32),
            pltpu.VMEM((texts, HALF), F32),
        ),
    )
    strips = exchange(strips, LINE)
    merged = call(
        merge_kernel,
        ((shape_of((2, rows, share), F32), VMEM),) * 4,
        ((stay, VMEM), (got, VMEM)),
        "head_merge", 1,
    )
    blocks = [merged[0]] + [along_x(merged[step], step) for step in (1, 2, 3)]
    shared = (normal, norm_gain, head_gain, filtered, mean, inverse, kernel)
    strips, *blocks = lax.optimization_barrier((strips, *blocks))
    sums, mine, theirs = call(
        strip_kernel,
        (
            (shape_of((line, strip, HALF), BF16), VMEM),
            (shape_of((rows, HALF), F32), VMEM),
            (shape_of((rows, HALF), F32), VMEM),
        ),
        ((strips, VMEM),),
        "strip_sum", 1,
    )
    near_half = exchange(sums, LINE).reshape(share, HALF)
    grad_text = call(
        text_kernel,
        ((shape_of((rows, width), F32), VMEM),),
        ((text_embed, VMEM), (mine, VMEM), (swap_core(theirs), VMEM), (logit_scale, SMEM)),
        "text_grad", 1,
    )
    grad_features = block_backward(blocks, *shared, mine)
    near_half, grad_features, grad_text = lax.optimization_barrier(
        (near_half, grad_features, grad_text)
    )
    grad_proj = call(
        join_kernel,
        ((shape_of((share, width), F32), VMEM),),
        ((near_half, VMEM), (swap_core(near_half), VMEM)),
        "proj_join", 2,
    )
    grad_features = grad_features.reshape(features.shape)
    return (grad_features, grad_text, grad_proj)


def solution(mesh):
    fine = Mesh(mesh.devices.reshape(SIZES), AXES)
    placed = (
        P(ALL, None, None, None),
        P(ALL, None),
        P(ALL),
        P(ALL),
        P(),
        P(),
        P(),
        P(GROUP, None),
        P(),
        P(),
    )
    return jax.shard_map(
        local,
        mesh=fine,
        in_specs=placed,
        out_specs=(P(ALL, None, None, None), P(ALL, None), P(GROUP, None)),
        check_vma=False,
    )
```
